32 devices in a mesh: groups: 2 (over y), epoch: 4 (over z), strip: 2 (over x), band: 2 (over core).
Axes of the slice: x: 2, y: 2, z: 4, core: 2. Of those that a mesh axis runs over, the one named last changes fastest.
Arguments:
- template: bfloat16 [16, 48, 512], P(('groups', 'epoch'), 'strip', 'band'), parts along dimension 0, may hold values from -6 to 6
- science: float32 [32, 48, 512], P(('groups', 'epoch'), 'strip', 'band'), parts along dimension 0, may hold values from -6 to 6
- variance: float32 [32, 48, 512], P(('groups', 'epoch'), 'strip', 'band'), parts along dimension 0, may hold values from 2 to 40
- bad_mask: int32 [32, 48, 512], P(('groups', 'epoch'), 'strip', 'band'), parts along dimension 0, may hold values 0 or 1
- intersection: int32 [32], P('groups'), parts along dimension 0, may hold values from 0 to 7, as said below
- offsets: int32 [32, 2], P(('groups', 'epoch')), parts along dimension 0, may hold values from -4 to 4
- basis_index: int32 [32, 16], P(('groups', 'epoch')), parts along dimension 0, may hold values from 0 to 48
- coefficients: float32 [32, 16, 6], P(('groups', 'epoch')), parts along dimension 0, may hold values from -2 to 2
- basis: float32 [49, 19, 19], replicated, may hold values from -0.3125 to 0.3125
Outputs:
- residual_image: float32 [32, 48, 512], P(('groups', 'epoch'), 'strip', 'band'), parts along dimension 0
- coadd: float32 [16, 48, 512], P(('groups', 'epoch'), 'strip', 'band'), parts along dimension 0
The draws below stay inside these ranges and needn't reach their ends.
There are 2 independent parts, one for each index of `groups`. The reference program is written for one: setup_inputs(seed, part) draws one part's arguments, and reference() takes and returns one part's arrays. A program takes and returns all parts, laid end to end along the dimension named above; an argument that names none is the same for every part. Nothing has to cross between parts.
Inputs may be any that keep to these rules, and one draw needn't show every extreme that they name: `intersection`: exposure d * 4 + k (k < 4) covers a tile with index from (k) * 2 to (k) * 2 + 1, chosen at random among these.
All inputs are finite; a program needn't handle non-finite values. No bound on the sum of `bad_mask` on one device may be relied on, other than what follows from the above.
Results may differ from the reference program's by a relative error of at most 0.0018.
Values may be sent and summed in bfloat16 or wider, within the bound.
No kernel may reach another device: no remote copies, remote signals or barrier semaphores. Data moves between devices by JAX's collectives and lax.ppermute only.
A program may use at most 64 MiB of HBM per device.

```python
import math
import jax
import jax.numpy as jnp
from jax import lax

KS = 19
HALF = 9
SHIFT = 4
NB = 49
NSEL = 16
NPOLY = 6
CAP = 1
TILE_DEV = 2
EXP_DEV = 4
EXPOSURES = 16
TILES = 8
HT = 48
WT = 512


def draw_intersection(key, part):
    position = jnp.arange(EXPOSURES, dtype=jnp.int32)
    owner = position % EXP_DEV // CAP
    choose = jax.random.randint(jax.random.fold_in(key, 17), (EXPOSURES,), 0, TILE_DEV)
    return (owner * TILE_DEV + choose).astype(jnp.int32)


def set_ends(drawn, rng, least, top_value):
    place = [jax.random.randint(jax.random.fold_in(rng, axis), (), 0, length) for axis, length in enumerate(drawn.shape)]
    widest = drawn.shape.index(max(drawn.shape))
    neighbour = place[:widest] + [(place[widest] + 1) % drawn.shape[widest]] + place[widest + 1:]
    return drawn.at[tuple(place)].set(least).at[tuple(neighbour)].set(top_value)


def block_scale(key, shape, shards, low, high):
    def one(dim, shards_of):
        heights = jax.random.uniform(jax.random.fold_in(jax.random.fold_in(key, 6), dim), (shards_of,), jnp.float32, low / len(shards), high / len(shards))
        return jnp.repeat(jnp.exp(heights), shape[dim] // shards_of).reshape((-1,) + (1,) * (len(shape) - dim - 1))

    loudness = one(*shards[0])
    for cut in shards[1:]:
        loudness = loudness * one(*cut)
    return loudness


def scatter_about(stream_key, shape, spread, reach, split=(), kind=jnp.bfloat16):
    drawn = jax.random.normal(stream_key, shape, jnp.float32) * spread
    if len(split) > 0:
        drawn = block_scale(stream_key, shape, split, -0.22, 0.18) * drawn
    return jnp.clip(drawn, min=-reach, max=reach).astype(kind)


def setup_inputs(seed: int = 0, part: int = 0) -> dict:
    streams_of = jax.random.split(jax.random.key(seed), 10)
    part_splits = jax.random.split(jax.random.fold_in(streams_of[9], part), 10)
    return {
        "template": scatter_about(part_splits[0], (TILES, HT, WT), 1.0, 6.0, ((0, 4), (1, 2), (2, 2))),
        "science": scatter_about(part_splits[1], (EXPOSURES, HT, WT), 1.0, 6.0, ((0, 4), (1, 2), (2, 2)), jnp.float32),
        "variance": jnp.clip(jnp.exp(math.log(40.0) - 2.9957323 * jax.random.uniform(part_splits[2], (EXPOSURES, HT, WT), jnp.float32) ** block_scale(part_splits[2], (EXPOSURES, HT, WT), ((0, 4), (1, 2), (2, 2)), -0.2, 0.2)), 2.0, 40.0),
        "bad_mask": set_ends((jax.random.randint(part_splits[3], (EXPOSURES, HT, WT), 0, 16) < 15).astype(jnp.int32), jax.random.fold_in(part_splits[3], 1), 0, 1),
        "intersection": draw_intersection(jax.random.fold_in(jax.random.fold_in(streams_of[9], part), 71), part),
        "offsets": set_ends(jax.random.randint(part_splits[5], (EXPOSURES, 2), 0 - SHIFT, SHIFT + 1), jax.random.fold_in(part_splits[5], 1), 0 - SHIFT, SHIFT).astype(jnp.int32),
        "basis_index": set_ends(jax.random.randint(part_splits[6], (EXPOSURES, NSEL), 0, NB), jax.random.fold_in(part_splits[6], 1), 0, NB - 1).astype(jnp.int32),
        "coefficients": scatter_about(part_splits[7], (EXPOSURES, NSEL, NPOLY), (0.5 / NSEL ** 0.5), 2.0, ((0, 4),), jnp.float32),
        "basis": scatter_about(streams_of[8], (NB, KS, KS), (KS * KS) ** -0.5, 0.3125, (), jnp.float32),
    }


highest = lax.Precision.HIGHEST


def poly_terms(rows_unit, cols_unit):
    ones = jnp.ones_like(rows_unit * cols_unit)
    return jnp.stack([ones, rows_unit * ones, cols_unit * ones, rows_unit * rows_unit * ones, rows_unit * cols_unit, cols_unit * cols_unit * ones])


def reference(template, science, variance, bad_mask, intersection, offsets, basis_index, coefficients, basis):
    height = template.shape[1]
    width = template.shape[2]
    rim = HALF + SHIFT
    padded = jnp.pad(template.astype(jnp.float32), ((0, 0), (rim, rim), (rim, rim)))
    picked = jnp.take(basis, basis_index, axis=0)
    kernels = jnp.einsum("ejp,ejab->epab", coefficients, picked, precision=highest).astype(jnp.bfloat16)
    kernels = lax.optimization_barrier(kernels).astype(jnp.float32)
    rows_unit = (2.0 * jnp.arange(height, dtype=jnp.float32) + 1.0) / height - 1.0
    cols_unit = (2.0 * jnp.arange(width, dtype=jnp.float32) + 1.0) / width - 1.0
    shapes = poly_terms(rows_unit[:, None], cols_unit[None, :])

    def one_model(item):
        tile, shift, kernel = item
        slab = lax.dynamic_index_in_dim(padded, tile.astype(jnp.int32), 0, keepdims=False)
        window = lax.dynamic_slice(slab, ((SHIFT + shift[0]).astype(jnp.int32), (SHIFT + shift[1]).astype(jnp.int32)), (height + 2 * HALF, width + 2 * HALF))
        conv = lax.conv_general_dilated(window[None, None], kernel[:, None], (1, 1), "VALID", precision=highest)[0]
        return jnp.sum(conv * shapes, axis=0)

    models = lax.map(one_model, (intersection, offsets, kernels))
    residual_image = science - models
    weight = bad_mask.astype(jnp.float32) / variance
    numer = jax.ops.segment_sum(weight * residual_image, intersection, num_segments=TILES)
    denom = jax.ops.segment_sum(weight, intersection, num_segments=TILES)
    return residual_image, numer / (denom + 1.0)
```

```python
import jax
import jax.numpy as jnp
from jax import lax
from jax.experimental import pallas as pl
from jax.experimental.pallas import tpu as pltpu
from jax.sharding import PartitionSpec as P

KS = 19
HALF = 9
SHIFT = 4
NPOLY = 6
REACH = HALF + SHIFT
SLOT = 8
CHUNK = 256
VMEM_LIMIT = 24 * 1024 * 1024

highest = lax.Precision.HIGHEST
f32 = jnp.float32
bf16 = jnp.bfloat16


def up(value, step):
    return -(-value // step) * step


class Sizes:
    def __init__(self, height, width):
        self.height, self.width = height, width
        self.rows = up(height + 2 * REACH, 8)
        self.lanes = up(width + 2 * REACH, 128)
        self.span = up(height + KS - 1, 16)
        self.per = CHUNK // self.span
        self.chunks = -(-KS // self.per)
        self.depth = self.chunks * CHUNK
        self.sw_rows = 4 * height
        self.r_rows = self.chunks * SLOT
        self.main_at = self.sw_rows + self.r_rows
        self.halo_at = self.main_at + self.rows
        self.groups = self.rows // 8
        self.halo_rows = up(self.groups * 32, width) // width * 8
        self.total = up(self.halo_at + self.halo_rows, 16)


def iota(shape, axis):
    return lax.broadcasted_iota(jnp.int32, shape, axis)


def split(value):
    high = value.astype(bf16).astype(f32)
    return high, value - high


def prepare(sz, count, nsel):
    lanes = count * SLOT
    nbasis = 128

    def body(sci, var, mask, offs, index, coef, basis, r_out, sw_out, table, place):
        for e in range(count):
            s_high, s_low = split(sci[e])
            w_high, w_low = split(mask[e].astype(f32) / var[e])
            sw_out[e] = jnp.concatenate([s_high, s_low, w_high, w_low], axis=0).astype(bf16)
        table[...] = jnp.zeros(table.shape, f32)
        for a in range(KS):
            table[a * 24 : a * 24 + KS, : basis.shape[2]] = basis[a]
        col = iota((24, sz.depth), 0)
        base = (col // sz.per) * CHUNK + (col % sz.per) * sz.span
        lane = iota((24, sz.depth), 1)
        base = jnp.where(col < KS, lane - base, -1)
        for a in range(0, KS + 1, 2):
            pair = jnp.concatenate([(base == a).astype(f32), (base == a + 1).astype(f32)], axis=0)
            if a + 1 == KS:
                pair = jnp.where(iota(pair.shape, 0) < 24, pair, 0.0)
            place[a * 24 : a * 24 + 48] = pair.astype(bf16)
        chosen = jnp.concatenate([index[e : e + 1, :] for e in range(count)], axis=1)
        onehot = (iota((nbasis, count * nsel), 0) == chosen).astype(f32)
        blocks = []
        for e in range(count):
            mine = jnp.concatenate([coef[:, e, :], jnp.zeros((SLOT - NPOLY, nsel), f32)], axis=0)
            wide = jnp.concatenate([mine] * count, axis=1)
            blocks.append(jnp.where(iota(wide.shape, 1) // nsel == e, wide, 0.0))
        combine = jnp.concatenate(blocks, axis=0)
        mixing = lax.dot_general(
            onehot, combine, (((1,), (1,)), ((), ())), precision=highest, preferred_element_type=f32
        )
        images = jnp.dot(table[...], mixing, precision=highest, preferred_element_type=f32)
        rows = lax.dot_general(
            images.astype(bf16), place[...], (((0,), (0,)), ((), ())), preferred_element_type=f32
        )
        for e in range(count):
            mine = rows[e * SLOT : (e + 1) * SLOT]
            mine = jnp.concatenate(
                [mine[:, i * CHUNK : (i + 1) * CHUNK] for i in range(sz.chunks)], axis=0
            )
            down, across = offs[0:1, e : e + 1].astype(f32), offs[1:2, e : e + 1].astype(f32)
            spot_row, spot = iota(mine.shape, 0), iota(mine.shape, 1)
            spare = spot_row == NPOLY
            mine = jnp.where(spare & (spot == 0), down, jnp.where(spare & (spot == 1), across, mine))
            r_out[e] = mine.astype(bf16)

    return pl.pallas_call(
        body,
        out_shape=(
            jax.ShapeDtypeStruct((count, sz.r_rows, CHUNK), bf16),
            jax.ShapeDtypeStruct((count, sz.sw_rows, sz.width), bf16),
        ),
        scratch_shapes=[
            pltpu.VMEM(((KS + 1) * 24, nbasis), f32),
            pltpu.VMEM(((KS + 1) * 24, sz.depth), bf16),
        ],
        compiler_params=pltpu.CompilerParams(vmem_limit_bytes=VMEM_LIMIT),
        cost_estimate=pl.CostEstimate(flops=200_000_000, bytes_accessed=3_000_000, transcendentals=0),
        name="prepare",
    )


def here(axis):
    return lax.axis_index(axis), lax.axis_size(axis)


def partner(me, n, k, back):
    if n & (n - 1) == 0:
        return me ^ k
    return (me + (n - k if back else k)) % n


def pack(sz, n_epoch, tiles, count, peers):
    per_owner = count // n_epoch
    h, w = sz.height, sz.width

    def body(inter, own, low, high, left, low_left, high_left, right, low_right, high_right, sw, r, *outs):
        slabs, sends = outs[0], outs[1:]
        me, _ = here("epoch")
        strip, strips = here("strip")
        band, bands = here("band")

        def column(middle, above, below, t, cut):
            above = jnp.where(strip > 0, above[t, h - 16 :, cut].astype(f32), 0.0)
            above = jnp.where(iota(above.shape, 0) >= 16 - REACH, above, 0.0)
            below = jnp.where(strip < strips - 1, below[t, :16, cut].astype(f32), 0.0)
            below = jnp.where(iota(below.shape, 0) < REACH, below, 0.0)
            parts = [middle[t, :, cut].astype(f32), below]
            gap = sz.rows - h - 32
            if gap:
                parts.append(jnp.zeros((gap, below.shape[1]), f32))
            return jnp.concatenate(parts + [above], axis=0)

        for t in range(tiles):
            slabs[t, :, :w] = column(own, low, high, t, slice(None)).astype(bf16)
            before = column(left, low_left, high_left, t, slice(w - 128, w))
            after = column(right, low_right, high_right, t, slice(0, 128))
            lane = iota(before.shape, 1)
            before = jnp.where((lane >= 128 - REACH) & (band > 0), before, 0.0)
            after = jnp.where((lane < REACH) & (band < bands - 1), after, 0.0)
            if sz.lanes - w == 128:
                slabs[t, :, w:] = (before + after).astype(bf16)
            else:
                slabs[t, :, w : w + 128] = after.astype(bf16)
                slabs[t, :, sz.lanes - 128 :] = before.astype(bf16)
        for k, out in zip(peers, sends):
            q = partner(me, n_epoch, k, False)
            for c in range(per_owner):
                tile = inter[q * count + me * per_owner + c] - me * tiles
                tile = jnp.clip(tile, 0, tiles - 1)
                mine = q * per_owner + c
                slab = slabs[tile].astype(f32)
                halo = pltpu.roll(slab[:, sz.lanes - 128 :], REACH, 1)
                if sz.lanes - w != 128:
                    halo = halo + pltpu.roll(slab[:, w : w + 128], REACH, 1)
                halo = jnp.where(iota(halo.shape, 1) < 32, halo, 0.0)
                bits = []
                for part in range(sz.halo_rows // 8 * (w // 128)):
                    piece = jnp.zeros((8, 128), f32)
                    for slot in range(4):
                        g = part * 4 + slot
                        if g < sz.groups:
                            piece = piece + pltpu.roll(halo[g * 8 : g * 8 + 8], slot * 32, 1)
                    bits.append(piece)
                wide = w // 128
                bits = [
                    jnp.concatenate(bits[i * wide : (i + 1) * wide], axis=1)
                    for i in range(sz.halo_rows // 8)
                ]
                parts = [r[mine].astype(f32), slab[:, :w]] + bits
                gap = sz.total - sz.halo_at - sz.halo_rows
                if gap:
                    parts.append(jnp.zeros((gap, w), f32))
                out[c, : sz.sw_rows] = sw[mine]
                out[c, sz.sw_rows :] = jnp.concatenate(parts, axis=0).astype(bf16)

    vmem, smem = pl.BlockSpec(memory_space=pltpu.VMEM), pl.BlockSpec(memory_space=pltpu.SMEM)
    return pl.pallas_call(
        body,
        in_specs=[smem] + [vmem] * 11,
        out_shape=(jax.ShapeDtypeStruct((tiles, sz.rows, sz.lanes), bf16),)
        + tuple(jax.ShapeDtypeStruct((per_owner, sz.total, w), bf16) for _ in peers),
        compiler_params=pltpu.CompilerParams(vmem_limit_bytes=VMEM_LIMIT),
        cost_estimate=pl.CostEstimate(flops=1_000_000, bytes_accessed=1_000_000, transcendentals=0),
        name="pack",
    )


def models(sz, n_epoch, tiles, count, ks, first, last, carried):
    per_owner = count // n_epoch
    h, w = sz.height, sz.width
    total_models = (2 * len(ks) + first) * per_owner

    def body(inter, sci, sw, r, slabs, *refs):
        refs = list(refs)
        pays = [refs.pop(0) for _ in ks]
        before = [] if first else [refs.pop(0) for _ in range(2)]
        done = [refs.pop(0) for _ in carried]
        if last:
            resid_out, coadd_out = refs.pop(0), refs.pop(0)
        else:
            numer_out, denom_out = refs.pop(0), refs.pop(0)
            resid_outs = [refs.pop(0) for _ in range(len(ks) + first)]
        rhs, lhs, numer, denom = refs
        me, _ = here("epoch")
        strip, strips = here("strip")
        band, bands = here("band")
        row = (strip * h + iota((h, w), 0)).astype(f32)
        col = (band * w + iota((h, w), 1)).astype(f32)
        r_unit = (2.0 * row + 1.0) / (h * strips) - 1.0
        c_unit = (2.0 * col + 1.0) / (w * bands) - 1.0
        for slot in range(2):
            for i in range(sz.chunks):
                used = min(sz.per, KS - i * sz.per) * sz.span
                if used < CHUNK:
                    rhs[slot, i * CHUNK + used : (i + 1) * CHUNK] = jnp.zeros((CHUNK - used, w), bf16)
        turn = [0]

        def model(slab, rows_of):
            slot = turn[0] % 2
            turn[0] += 1
            window, band_rows = rhs.at[slot], lhs.at[slot]
            down = rows_of[NPOLY, 0].astype(jnp.int32)
            across = rows_of[NPOLY, 1].astype(jnp.int32)
            slab = pltpu.roll(slab, lax.rem(sz.rows + HALF - down, sz.rows), 0)[: sz.span]
            slab = pltpu.roll(slab, lax.rem(sz.lanes + HALF - across, sz.lanes), 1).astype(bf16)
            for b in range(KS):
                at = b // sz.per * CHUNK + b % sz.per * sz.span
                window[at : at + sz.span] = slab[:, b : b + w]
            for p in range(NPOLY):
                for i in range(sz.chunks):
                    line = rows_of[i * SLOT + p : i * SLOT + p + 1]
                    line = pltpu.roll(
                        jnp.broadcast_to(line, (h, CHUNK)), 0, 1, stride=1, stride_axis=0
                    )
                    band_rows[p * h : (p + 1) * h, i * CHUNK : (i + 1) * CHUNK] = line
            conv = jnp.dot(band_rows[...].astype(bf16), window[...], preferred_element_type=f32)
            conv = [conv[p * h : (p + 1) * h] for p in range(NPOLY)]
            return (
                conv[0]
                + r_unit * (conv[1] + r_unit * conv[3] + c_unit * conv[4])
                + c_unit * (conv[2] + c_unit * conv[5])
            )

        def add(tile, pair, image):
            science = pair[:h] + pair[h : 2 * h]
            weight = pair[2 * h : 3 * h] + pair[3 * h : 4 * h]
            numer[tile] = numer[tile] + weight * (science - image)
            denom[tile] = denom[tile] + weight

        def tile_of(q, c):
            return jnp.clip(inter[q * count + me * per_owner + c] - me * tiles, 0, tiles - 1)

        def keep(j, c, mine, image):
            value = sci[mine] - image
            if last:
                resid_out[mine] = value
            else:
                resid_outs[j][c] = value

        if first:
            numer[...] = jnp.zeros(numer.shape, f32)
            denom[...] = jnp.zeros(denom.shape, f32)
        else:
            numer[...] = before[0][...]
            denom[...] = before[1][...]
        if first:
            for c in range(per_owner):
                mine = me * per_owner + c
                tile = tile_of(me, c)
                image = model(slabs[tile].astype(f32), r[mine].astype(f32))
                keep(len(ks), c, mine, image)
                add(tile, sw[mine].astype(f32), image)
        for j, (k, pay) in enumerate(zip(ks, pays)):
            q = partner(me, n_epoch, k, True)
            for c in range(per_owner):
                mine = q * per_owner + c
                got = pay[c, sz.sw_rows :].astype(f32)
                tile = tile_of(q, c)
                image = model(slabs[tile].astype(f32), got[: sz.r_rows])
                add(tile, pay[c, : sz.sw_rows].astype(f32), image)
                main = got[sz.r_rows : sz.r_rows + sz.rows]
                halo = got[sz.r_rows + sz.rows :]
                wide = w // 128
                bits = []
                for g in range(sz.groups):
                    part, slot = g // 4, g % 4
                    line, side = part // wide, part % wide
                    piece = halo[line * 8 : line * 8 + 8, side * 128 : side * 128 + 128]
                    piece = pltpu.roll(piece, (128 - slot * 32) % 128, 1)
                    bits.append(piece)
                halo = jnp.concatenate(bits, axis=0)
                lane = iota(halo.shape, 1)
                halo = pltpu.roll(jnp.where(lane < 2 * REACH, halo, 0.0), 128 - REACH, 1)
                if sz.lanes - w != 128:
                    lane = iota(halo.shape, 1)
                    gap = sz.lanes - w - 256
                    pieces = [jnp.where(lane < 64, halo, 0.0)]
                    if gap:
                        pieces.append(jnp.zeros((sz.rows, gap), f32))
                    halo = jnp.concatenate(pieces + [jnp.where(lane < 64, 0.0, halo)], axis=1)
                image = model(jnp.concatenate([main, halo], axis=1), r[mine].astype(f32))
                keep(j, c, mine, image)
        if last:
            for (k, where), value in zip(carried, done):
                q = me if k == 0 else partner(me, n_epoch, k, True)
                for c in range(per_owner):
                    resid_out[q * per_owner + c] = value[c]
            coadd_out[...] = numer[...] / (denom[...] + 1.0)
        else:
            numer_out[...] = numer[...]
            denom_out[...] = denom[...]

    image = jax.ShapeDtypeStruct((per_owner, h, w), f32)
    sums = jax.ShapeDtypeStruct((tiles, h, w), f32)
    if last:
        out_shape = (jax.ShapeDtypeStruct((count, h, w), f32), sums)
    else:
        out_shape = (sums, sums) + (image,) * (len(ks) + first)
    vmem, smem = pl.BlockSpec(memory_space=pltpu.VMEM), pl.BlockSpec(memory_space=pltpu.SMEM)
    return pl.pallas_call(
        body,
        in_specs=[smem] + [vmem] * (4 + len(ks) + (0 if first else 2) + len(carried)),
        out_shape=out_shape,
        scratch_shapes=[
            pltpu.VMEM((2, sz.depth, w), bf16),
            pltpu.VMEM((2, NPOLY * h, sz.depth), f32),
            pltpu.VMEM((tiles, h, w), f32),
            pltpu.VMEM((tiles, h, w), f32),
        ],
        compiler_params=pltpu.CompilerParams(vmem_limit_bytes=VMEM_LIMIT),
        cost_estimate=pl.CostEstimate(
            flops=total_models * 400_000_000, bytes_accessed=1_000_000, transcendentals=0
        ),
        name="models",
    )


def neighbours(block, axis):
    count = lax.axis_size(axis)
    if count == 1:
        return block, block
    if count == 2:
        other = lax.ppermute(block, axis, [(0, 1), (1, 0)])
        return other, other
    forward = [(i, i + 1) for i in range(count - 1)]
    backward = [(i + 1, i) for i in range(count - 1)]
    return lax.ppermute(block, axis, forward), lax.ppermute(block, axis, backward)


def local(
    template, science, variance, bad_mask, intersection, offsets, basis_index, coefficients, basis
):
    n_epoch = lax.axis_size("epoch")
    tiles = template.shape[0]
    count, height, width = science.shape
    sz = Sizes(height, width)
    low, high = neighbours(template, "strip")
    left, right = neighbours(template, "band")
    r, sw = prepare(sz, count, basis_index.shape[1])(
        science,
        variance,
        bad_mask,
        offsets.T,
        basis_index,
        coefficients.transpose(2, 0, 1),
        basis.transpose(1, 2, 0),
    )
    low_left, low_right = neighbours(low, "band")
    if high is low:
        high_left, high_right = low_left, low_right
    else:
        high_left, high_right = neighbours(high, "band")
    peers = list(range(1, n_epoch))
    slabs, *sends = pack(sz, n_epoch, tiles, count, peers)(
        intersection, template, low, high, left, low_left, high_left, right, low_right, high_right, sw, r
    )
    pays = {}
    for k, send in zip(peers, sends):
        pairs = [(i, partner(i, n_epoch, k, False)) for i in range(n_epoch)]
        pays[k] = lax.ppermute(send, "epoch", pairs)
    stages = [[]] + [[k] for k in reversed(peers)]
    sums, carried = [], []
    for i, ks in enumerate(stages):
        first, last = i == 0, i == len(stages) - 1
        kept = [(k, j) for j, (k, _) in enumerate(carried)] if last else []
        out = models(sz, n_epoch, tiles, count, ks, first, last, kept)(
            intersection,
            science,
            sw,
            r,
            slabs,
            *[pays[k] for k in ks],
            *sums,
            *([value for _, value in carried] if last else []),
        )
        if last:
            return out
        sums = list(out[:2])
        carried += list(zip(list(ks) + ([0] if first else []), out[2:]))


def solution(mesh):
    in_specs = (
        P(("groups", "epoch"), "strip", "band"),
        P(("groups", "epoch"), "strip", "band"),
        P(("groups", "epoch"), "strip", "band"),
        P(("groups", "epoch"), "strip", "band"),
        P("groups"),
        P(("groups", "epoch"), None),
        P(("groups", "epoch"), None),
        P(("groups", "epoch"), None, None),
        P(),
    )
    out_specs = (P(("groups", "epoch"), "strip", "band"), P(("groups", "epoch"), "strip", "band"))
    return jax.shard_map(local, mesh=mesh, in_specs=in_specs, out_specs=out_specs, check_vma=False)
```

```python
import jax
import jax.numpy as jnp
from jax import lax
from jax.experimental import pallas as pl
from jax.experimental.pallas import tpu as pltpu
from jax.sharding import PartitionSpec as P

KS = 19
HALF = 9
SHIFT = 4
NPOLY = 6
REACH = HALF + SHIFT
SLOT = 8
CHUNK = 256
FINE = 24
VMEM_LIMIT = 24 * 1024 * 1024

highest = lax.Precision.HIGHEST
f32 = jnp.float32
bf16 = jnp.bfloat16


def up(value, step):
    return -(-value // step) * step


class Sizes:
    def __init__(self, height, width, strips):
        self.height, self.width = height, width
        self.rows = up(height + 2 * REACH, 8)
        self.lanes = up(width + 2 * REACH, 128)
        self.span = up(height + KS - 1, 2 * FINE)
        self.phases = self.span // FINE
        self.per = CHUNK // self.span
        self.lines = -(-KS // (self.per * self.phases))
        self.chunks = self.lines * self.phases
        self.depth = self.chunks * CHUNK
        self.sw_rows = 4 * height
        self.r_rows = self.lines * SLOT
        self.one_side = strips <= 2
        self.sent = height + 16 if self.one_side else self.rows
        self.main_at = self.sw_rows + self.r_rows
        self.halo_at = self.main_at + self.sent
        self.groups = self.sent // 8
        self.halo_rows = up(self.groups * 32, width) // width * 8
        self.total = self.halo_at + self.halo_rows

    def columns(self, chunk):
        line, phase = divmod(chunk, self.phases)
        first = line * self.per * self.phases + phase
        return [b for b in range(first, first + self.per * self.phases, self.phases) if b < KS]


def iota(shape, axis):
    return lax.broadcasted_iota(jnp.int32, shape, axis)


def split(value):
    high = value.astype(bf16).astype(f32)
    return high, value - high


def prepare(sz, n_epoch, tiles, count, nsel):
    lanes = count * SLOT
    per_owner = count // n_epoch
    width = sz.lines * CHUNK
    nbasis = 128

    def body(*refs):
        sources, refs = refs[:9], refs[9:]
        r_out, sw_out, own_out, sci_out = refs[:4]
        var, mask, inter, offs, index, coef, basis, table, place, sems = refs[4:]
        targets = [own_out, sci_out, var, mask, inter, offs, index, coef, basis]
        copies = [
            pltpu.make_async_copy(source, target, sems.at[i])
            for i, (source, target) in enumerate(zip(sources, targets))
        ]
        for copy in reversed(copies):
            copy.start()
        me, _ = here("epoch")
        table[...] = jnp.zeros(table.shape, f32)
        col = iota((FINE, width), 0)
        whole = sz.per * sz.phases
        base = iota((FINE, width), 1) - (col // whole) * CHUNK - (col % whole) * FINE
        base = jnp.where(col < KS, base, -1)
        for a in range(0, KS + 1, 2):
            pair = jnp.concatenate([(base == a).astype(f32), (base == a + 1).astype(f32)], axis=0)
            if a + 1 == KS:
                pair = jnp.where(iota(pair.shape, 0) < FINE, pair, 0.0)
            place[a * FINE : (a + 2) * FINE] = pair.astype(bf16)
        for copy in reversed(copies[4:]):
            copy.wait()
        for a in range(KS):
            table[a * FINE : a * FINE + KS, : basis.shape[2]] = basis[a]
        chosen = jnp.concatenate([index[e : e + 1, :] for e in range(count)], axis=1)
        onehot = (iota((nbasis, count * nsel), 0) == chosen).astype(f32)
        blocks = []
        for e in range(count):
            mine = jnp.concatenate([coef[:, e, :], jnp.zeros((SLOT - NPOLY, nsel), f32)], axis=0)
            wide = jnp.concatenate([mine] * count, axis=1)
            blocks.append(jnp.where(iota(wide.shape, 1) // nsel == e, wide, 0.0))
        combine = jnp.concatenate(blocks, axis=0)
        mixing = lax.dot_general(
            onehot, combine, (((1,), (1,)), ((), ())), precision=highest, preferred_element_type=f32
        )
        images = jnp.dot(table[...], mixing, precision=highest, preferred_element_type=f32)
        rows = lax.dot_general(
            images.astype(bf16), place[...], (((0,), (0,)), ((), ())), preferred_element_type=f32
        )
        for e in range(count):
            mine = rows[e * SLOT : (e + 1) * SLOT]
            mine = jnp.concatenate(
                [mine[:, i * CHUNK : (i + 1) * CHUNK] for i in range(sz.lines)], axis=0
            )
            tile = inter[e // per_owner * count + me * per_owner + e % per_owner] - me * tiles
            tile = jnp.clip(tile, 0, tiles - 1).astype(f32)
            down, across = offs[0:1, e : e + 1].astype(f32), offs[1:2, e : e + 1].astype(f32)
            spare, spot = iota(mine.shape, 0) == NPOLY, iota(mine.shape, 1)
            for lane, value in enumerate((down, across, tile)):
                mine = jnp.where(spare & (spot == lane), value, mine)
            r_out[e] = mine.astype(bf16)
        for copy in reversed(copies[:4]):
            copy.wait()
        for e in range(count):
            s_high, s_low = split(sci_out[e])
            w_high, w_low = split(mask[e].astype(f32) / var[e])
            sw_out[e] = jnp.concatenate([s_high, s_low, w_high, w_low], axis=0).astype(bf16)

    hbm, vmem = pl.BlockSpec(memory_space=pltpu.HBM), pl.BlockSpec(memory_space=pltpu.VMEM)
    shape = (count, sz.height, sz.width)

    def call(template, science, variance, mask, inter, offs, index, coef, basis):
        return pl.pallas_call(
            body,
            in_specs=[hbm] * 9,
            out_specs=(vmem,) * 4,
            out_shape=(
                jax.ShapeDtypeStruct((count, sz.r_rows, CHUNK), bf16),
                jax.ShapeDtypeStruct((count, sz.sw_rows, sz.width), bf16),
                jax.ShapeDtypeStruct(template.shape, bf16),
                jax.ShapeDtypeStruct(shape, f32),
            ),
            scratch_shapes=[
                pltpu.VMEM(shape, f32),
                pltpu.VMEM(shape, jnp.int32),
                pltpu.SMEM(inter.shape, jnp.int32),
                pltpu.VMEM(offs.shape, jnp.int32),
                pltpu.VMEM(index.shape, jnp.int32),
                pltpu.VMEM(coef.shape, f32),
                pltpu.VMEM(basis.shape, f32),
                pltpu.VMEM(((KS + 1) * FINE, nbasis), f32),
                pltpu.VMEM(((KS + 1) * FINE, width), bf16),
                pltpu.SemaphoreType.DMA((9,)),
            ],
            compiler_params=pltpu.CompilerParams(vmem_limit_bytes=VMEM_LIMIT),
            cost_estimate=pl.CostEstimate(
                flops=1_000_000_000, bytes_accessed=6_000_000, transcendentals=0
            ),
            name="prepare",
        )(template, science, variance, mask, inter, offs, index, coef, basis)

    return call


def here(axis):
    return lax.axis_index(axis), lax.axis_size(axis)


def partner(me, n, k, back):
    if n & (n - 1) == 0:
        return me ^ k
    return (me + (n - k if back else k)) % n


def pack(sz, n_epoch, tiles, count, peers):
    per_owner = count // n_epoch
    h, w = sz.height, sz.width

    def body(own, low, high, left, low_left, high_left, right, low_right, high_right, sw, r, *outs):
        slabs, sends = outs[0], outs[1:]
        me, _ = here("epoch")
        strip, strips = here("strip")
        band, bands = here("band")

        def column(middle, above, below, t, cut):
            above = jnp.where(strip > 0, above[t, h - 16 :, cut].astype(f32), 0.0)
            above = jnp.where(iota(above.shape, 0) >= 16 - REACH, above, 0.0)
            below = jnp.where(strip < strips - 1, below[t, :16, cut].astype(f32), 0.0)
            below = jnp.where(iota(below.shape, 0) < REACH, below, 0.0)
            parts = [middle[t, :, cut].astype(f32), below]
            gap = sz.rows - h - 32
            if gap:
                parts.append(jnp.zeros((gap, below.shape[1]), f32))
            return jnp.concatenate(parts + [above], axis=0)

        for t in range(tiles):
            slabs[t, :, :w] = column(own, low, high, t, slice(None)).astype(bf16)
            before = column(left, low_left, high_left, t, slice(w - 128, w))
            after = column(right, low_right, high_right, t, slice(0, 128))
            lane = iota(before.shape, 1)
            before = jnp.where((lane >= 128 - REACH) & (band > 0), before, 0.0)
            after = jnp.where((lane < REACH) & (band < bands - 1), after, 0.0)
            if sz.lanes - w == 128:
                slabs[t, :, w:] = (before + after).astype(bf16)
            else:
                slabs[t, :, w : w + 128] = after.astype(bf16)
                slabs[t, :, sz.lanes - 128 :] = before.astype(bf16)
        for k, out in zip(peers, sends):
            q = partner(me, n_epoch, k, False)
            for c in range(per_owner):
                mine = q * per_owner + c
                lines = r[mine].astype(f32)
                tile = lines[NPOLY, 2].astype(jnp.int32)
                slab = slabs[tile].astype(f32)
                if sz.one_side:
                    side = jnp.where(strip == 0, slab[h : h + 16], slab[sz.rows - 16 :])
                    slab = jnp.concatenate([slab[:h], side], axis=0)
                halo = pltpu.roll(slab[:, sz.lanes - 128 :], REACH, 1)
                if sz.lanes - w != 128:
                    halo = halo + pltpu.roll(slab[:, w : w + 128], REACH, 1)
                halo = jnp.where(iota(halo.shape, 1) < 32, halo, 0.0)
                bits = []
                for part in range(sz.halo_rows // 8 * (w // 128)):
                    piece = jnp.zeros((8, 128), f32)
                    for slot in range(4):
                        g = part * 4 + slot
                        if g < sz.groups:
                            piece = piece + pltpu.roll(halo[g * 8 : g * 8 + 8], slot * 32, 1)
                    bits.append(piece)
                wide = w // 128
                bits = [
                    jnp.concatenate(bits[i * wide : (i + 1) * wide], axis=1)
                    for i in range(sz.halo_rows // 8)
                ]
                parts = [lines, slab[:, :w]] + bits
                out[c, : sz.sw_rows] = sw[mine]
                out[c, sz.sw_rows :] = jnp.concatenate(parts, axis=0).astype(bf16)

    vmem = pl.BlockSpec(memory_space=pltpu.VMEM)
    return pl.pallas_call(
        body,
        in_specs=[vmem] * 11,
        out_shape=(jax.ShapeDtypeStruct((tiles, sz.rows, sz.lanes), bf16),)
        + tuple(jax.ShapeDtypeStruct((per_owner, sz.total, w), bf16) for _ in peers),
        compiler_params=pltpu.CompilerParams(vmem_limit_bytes=VMEM_LIMIT),
        cost_estimate=pl.CostEstimate(flops=1_000_000, bytes_accessed=1_000_000, transcendentals=0),
        name="pack",
    )


def models(sz, n_epoch, tiles, count, ks, first, last, carried):
    per_owner = count // n_epoch
    h, w = sz.height, sz.width
    total_models = (2 * len(ks) + first) * per_owner

    def body(sci, sw, r, slabs, *refs):
        refs = list(refs)
        pays = [refs.pop(0) for _ in ks]
        before = [] if first else [refs.pop(0) for _ in range(2)]
        done = [refs.pop(0) for _ in carried]
        if last:
            resid_out, coadd_out = refs.pop(0), refs.pop(0)
        else:
            numer_out, denom_out = refs.pop(0), refs.pop(0)
            resid_outs = [refs.pop(0) for _ in range(len(ks) + first)]
        rhs, lhs, numer, denom = refs
        me, _ = here("epoch")
        strip, strips = here("strip")
        band, bands = here("band")
        row = (strip * h + iota((h, w), 0)).astype(f32)
        col = (band * w + iota((h, w), 1)).astype(f32)
        r_unit = (2.0 * row + 1.0) / (h * strips) - 1.0
        c_unit = (2.0 * col + 1.0) / (w * bands) - 1.0
        for slot in range(2):
            for i in range(sz.chunks):
                used = len(sz.columns(i)) * sz.span
                if used < CHUNK:
                    rhs[slot, i * CHUNK + used : (i + 1) * CHUNK] = jnp.zeros((CHUNK - used, w), bf16)
        turn = [0]

        def model(slab, rows_of):
            slot = turn[0] % 2
            turn[0] += 1
            window, band_rows = rhs.at[slot], lhs.at[slot]
            down = rows_of[NPOLY, 0].astype(jnp.int32)
            across = rows_of[NPOLY, 1].astype(jnp.int32)
            slab = pltpu.roll(slab, lax.rem(sz.rows + HALF - down, sz.rows), 0)[: sz.span]
            slab = pltpu.roll(slab, lax.rem(sz.lanes + HALF - across, sz.lanes), 1).astype(bf16)
            for i in range(sz.chunks):
                for slot, b in enumerate(sz.columns(i)):
                    at = i * CHUNK + slot * sz.span
                    window[at : at + sz.span] = slab[:, b : b + w]
            for i in range(sz.chunks):
                line, phase = divmod(i, sz.phases)
                lines = rows_of[line * SLOT : (line + 1) * SLOT]
                if phase:
                    lines = pltpu.roll(lines, CHUNK - phase * FINE, 1)
                spot = iota(lines.shape, 1)
                lines = jnp.where((spot % sz.span < FINE) & (spot < sz.per * sz.span), lines, 0.0)
                for p in range(NPOLY):
                    line = lines[p : p + 1]
                    line = pltpu.roll(
                        jnp.broadcast_to(line, (h, CHUNK)), 0, 1, stride=1, stride_axis=0
                    )
                    band_rows[p * h : (p + 1) * h, i * CHUNK : (i + 1) * CHUNK] = line
            conv = jnp.dot(band_rows[...].astype(bf16), window[...], preferred_element_type=f32)
            conv = [conv[p * h : (p + 1) * h] for p in range(NPOLY)]
            return (
                conv[0]
                + r_unit * (conv[1] + r_unit * conv[3] + c_unit * conv[4])
                + c_unit * (conv[2] + c_unit * conv[5])
            )

        def add(tile, pair, image):
            science = pair[:h] + pair[h : 2 * h]
            weight = pair[2 * h : 3 * h] + pair[3 * h : 4 * h]
            numer[tile] = numer[tile] + weight * (science - image)
            denom[tile] = denom[tile] + weight

        def tile_of(lines):
            return lines[NPOLY, 2].astype(jnp.int32)

        def keep(j, c, mine, image):
            value = sci[mine] - image
            if last:
                resid_out[mine] = value
            else:
                resid_outs[j][c] = value

        if first:
            numer[...] = jnp.zeros(numer.shape, f32)
            denom[...] = jnp.zeros(denom.shape, f32)
        else:
            numer[...] = before[0][...]
            denom[...] = before[1][...]
        if first:
            for c in range(per_owner):
                mine = me * per_owner + c
                lines = r[mine].astype(f32)
                tile = tile_of(lines)
                image = model(slabs[tile].astype(f32), lines)
                keep(len(ks), c, mine, image)
                add(tile, sw[mine].astype(f32), image)
        for j, (k, pay) in enumerate(zip(ks, pays)):
            q = partner(me, n_epoch, k, True)
            for c in range(per_owner):
                mine = q * per_owner + c
                got = pay[c, sz.sw_rows :].astype(f32)
                lines = r[mine].astype(f32)
                tile = tile_of(lines)
                image = model(slabs[tile].astype(f32), got[: sz.r_rows])
                add(tile, pay[c, : sz.sw_rows].astype(f32), image)
                main = got[sz.r_rows : sz.r_rows + sz.sent]
                halo = got[sz.r_rows + sz.sent :]
                wide = w // 128
                bits = []
                for g in range(sz.groups):
                    part, slot = g // 4, g % 4
                    line, side = part // wide, part % wide
                    piece = halo[line * 8 : line * 8 + 8, side * 128 : side * 128 + 128]
                    piece = pltpu.roll(piece, (128 - slot * 32) % 128, 1)
                    bits.append(piece)
                halo = jnp.concatenate(bits, axis=0)
                lane = iota(halo.shape, 1)
                halo = pltpu.roll(jnp.where(lane < 2 * REACH, halo, 0.0), 128 - REACH, 1)
                if sz.lanes - w != 128:
                    lane = iota(halo.shape, 1)
                    gap = sz.lanes - w - 256
                    pieces = [jnp.where(lane < 64, halo, 0.0)]
                    if gap:
                        pieces.append(jnp.zeros((sz.sent, gap), f32))
                    halo = jnp.concatenate(pieces + [jnp.where(lane < 64, 0.0, halo)], axis=1)
                slab = jnp.concatenate([main, halo], axis=1)
                if sz.one_side:
                    side, none = slab[h:], jnp.zeros((sz.rows - h - 32, sz.lanes), f32)
                    below, above = jnp.where(strip == 0, side, 0.0), jnp.where(strip == 0, 0.0, side)
                    slab = [slab[:h], below, none, above] if none.size else [slab[:h], below, above]
                    slab = jnp.concatenate(slab, axis=0)
                image = model(slab, lines)
                keep(j, c, mine, image)
        if last:
            for (k, where), value in zip(carried, done):
                q = me if k == 0 else partner(me, n_epoch, k, True)
                for c in range(per_owner):
                    resid_out[q * per_owner + c] = value[c]
            coadd_out[...] = numer[...] / (denom[...] + 1.0)
        else:
            numer_out[...] = numer[...]
            denom_out[...] = denom[...]

    image = jax.ShapeDtypeStruct((per_owner, h, w), f32)
    sums = jax.ShapeDtypeStruct((tiles, h, w), f32)
    if last:
        out_shape = (jax.ShapeDtypeStruct((count, h, w), f32), sums)
    else:
        out_shape = (sums, sums) + (image,) * (len(ks) + first)
    vmem = pl.BlockSpec(memory_space=pltpu.VMEM)
    return pl.pallas_call(
        body,
        in_specs=[vmem] * (4 + len(ks) + (0 if first else 2) + len(carried)),
        out_shape=out_shape,
        scratch_shapes=[
            pltpu.VMEM((2, sz.depth, w), bf16),
            pltpu.VMEM((2, NPOLY * h, sz.depth), f32),
            pltpu.VMEM((tiles, h, w), f32),
            pltpu.VMEM((tiles, h, w), f32),
        ],
        compiler_params=pltpu.CompilerParams(vmem_limit_bytes=VMEM_LIMIT),
        cost_estimate=pl.CostEstimate(
            flops=total_models * 400_000_000, bytes_accessed=1_000_000, transcendentals=0
        ),
        name="models",
    )


def neighbours(block, axis):
    count = lax.axis_size(axis)
    if count == 1:
        return block, block
    if count == 2:
        other = lax.ppermute(block, axis, [(0, 1), (1, 0)])
        return other, other
    forward = [(i, i + 1) for i in range(count - 1)]
    backward = [(i + 1, i) for i in range(count - 1)]
    return lax.ppermute(block, axis, forward), lax.ppermute(block, axis, backward)


def local(
    template, science, variance, bad_mask, intersection, offsets, basis_index, coefficients, basis
):
    n_epoch = lax.axis_size("epoch")
    tiles = template.shape[0]
    count, height, width = science.shape
    sz = Sizes(height, width, lax.axis_size("strip"))
    low, high = neighbours(template, "strip")
    left, right = neighbours(template, "band")
    r, sw, own, sci = prepare(sz, n_epoch, tiles, count, basis_index.shape[1])(
        template,
        science,
        variance,
        bad_mask,
        intersection,
        offsets.T,
        basis_index,
        coefficients.transpose(2, 0, 1),
        basis.transpose(1, 2, 0),
    )
    low_left, low_right = neighbours(low, "band")
    if high is low:
        high_left, high_right = low_left, low_right
    else:
        high_left, high_right = neighbours(high, "band")
    peers = list(range(1, n_epoch))
    order = peers[-1:] + peers[:-1]
    slabs, *sends = pack(sz, n_epoch, tiles, count, peers)(
        own, low, high, left, low_left, high_left, right, low_right, high_right, sw, r
    )
    pays = {}
    for k, send in zip(order, [sends[peers.index(k)] for k in order]):
        pairs = [(i, partner(i, n_epoch, k, False)) for i in range(n_epoch)]
        pays[k] = lax.ppermute(send, "epoch", pairs)
    stages = [[]] + [[k] for k in order]
    sums, carried = [], []
    for i, ks in enumerate(stages):
        first, last = i == 0, i == len(stages) - 1
        kept = [(k, j) for j, (k, _) in enumerate(carried)] if last else []
        out = models(sz, n_epoch, tiles, count, ks, first, last, kept)(
            sci,
            sw,
            r,
            slabs,
            *[pays[k] for k in ks],
            *sums,
            *([value for _, value in carried] if last else []),
        )
        if last:
            return out
        sums = list(out[:2])
        carried += list(zip(list(ks) + ([0] if first else []), out[2:]))


def solution(mesh):
    in_specs = (
        P(("groups", "epoch"), "strip", "band"),
        P(("groups", "epoch"), "strip", "band"),
        P(("groups", "epoch"), "strip", "band"),
        P(("groups", "epoch"), "strip", "band"),
        P("groups"),
        P(("groups", "epoch"), None),
        P(("groups", "epoch"), None),
        P(("groups", "epoch"), None, None),
        P(),
    )
    out_specs = (P(("groups", "epoch"), "strip", "band"), P(("groups", "epoch"), "strip", "band"))
    return jax.shard_map(local, mesh=mesh, in_specs=in_specs, out_specs=out_specs, check_vma=False)
```

```python
import jax
import jax.numpy as jnp
from jax import lax
from jax.experimental import pallas as pl
from jax.experimental.pallas import tpu as pltpu
from jax.sharding import PartitionSpec as P

KS = 19
HALF = 9
SHIFT = 4
NPOLY = 6
REACH = HALF + SHIFT
SLOT = 8
CHUNK = 256
FINE = 24
VMEM_LIMIT = 24 * 1024 * 1024

highest = lax.Precision.HIGHEST
f32 = jnp.float32
bf16 = jnp.bfloat16


def up(value, step):
    return -(-value // step) * step


class Sizes:
    def __init__(self, height, width, strips):
        self.height, self.width = height, width
        self.rows = up(height + 2 * REACH, 8)
        self.lanes = up(width + 2 * REACH, 128)
        self.span = up(height + KS - 1, 2 * FINE)
        self.phases = self.span // FINE
        self.per = CHUNK // self.span
        self.lines = -(-KS // (self.per * self.phases))
        self.chunks = self.lines * self.phases
        self.depth = self.chunks * CHUNK
        self.sw_rows = 4 * height
        self.r_rows = self.lines * SLOT
        self.one_side = strips <= 2
        self.sent = height + 16 if self.one_side else self.rows
        self.main_at = self.sw_rows + self.r_rows
        self.halo_at = self.main_at + self.sent
        self.groups = self.sent // 8
        self.halo_rows = up(self.groups * 32, width) // width * 8
        self.total = self.halo_at + self.halo_rows

    def columns(self, chunk):
        line, phase = divmod(chunk, self.phases)
        first = line * self.per * self.phases + phase
        return [b for b in range(first, first + self.per * self.phases, self.phases) if b < KS]


def iota(shape, axis):
    return lax.broadcasted_iota(jnp.int32, shape, axis)


def split(value):
    high = value.astype(bf16).astype(f32)
    return high, value - high


def prepare(sz, n_epoch, tiles, count, nsel):
    lanes = count * SLOT
    per_owner = count // n_epoch
    width = sz.lines * CHUNK
    nbasis = 128

    def body(*refs):
        sources, refs = refs[:9], refs[9:]
        r_out, sw_out, own_out, sci_out = refs[:4]
        var, mask, inter, offs, index, coef, basis, table, place, sems = refs[4:]
        targets = [own_out, sci_out, var, mask, inter, offs, index, coef, basis]
        copies = [
            pltpu.make_async_copy(source, target, sems.at[i])
            for i, (source, target) in enumerate(zip(sources, targets))
        ]
        for copy in reversed(copies):
            copy.start()
        me, _ = here("epoch")
        table[...] = jnp.zeros(table.shape, f32)
        col = iota((FINE, width), 0)
        whole = sz.per * sz.phases
        base = iota((FINE, width), 1) - (col // whole) * CHUNK - (col % whole) * FINE
        base = jnp.where(col < KS, base, -1)
        for a in range(0, KS + 1, 2):
            pair = jnp.concatenate([(base == a).astype(f32), (base == a + 1).astype(f32)], axis=0)
            if a + 1 == KS:
                pair = jnp.where(iota(pair.shape, 0) < FINE, pair, 0.0)
            place[a * FINE : (a + 2) * FINE] = pair.astype(bf16)
        for copy in reversed(copies[4:]):
            copy.wait()
        for a in range(KS):
            table[a * FINE : a * FINE + KS, : basis.shape[2]] = basis[a]
        chosen = jnp.concatenate([index[e : e + 1, :] for e in range(count)], axis=1)
        onehot = (iota((nbasis, count * nsel), 0) == chosen).astype(f32)
        blocks = []
        for e in range(count):
            mine = jnp.concatenate([coef[:, e, :], jnp.zeros((SLOT - NPOLY, nsel), f32)], axis=0)
            wide = jnp.concatenate([mine] * count, axis=1)
            blocks.append(jnp.where(iota(wide.shape, 1) // nsel == e, wide, 0.0))
        combine = jnp.concatenate(blocks, axis=0)
        mixing = lax.dot_general(
            onehot, combine, (((1,), (1,)), ((), ())), precision=highest, preferred_element_type=f32
        )
        images = jnp.dot(table[...], mixing, precision=highest, preferred_element_type=f32)
        rows = lax.dot_general(
            images.astype(bf16), place[...], (((0,), (0,)), ((), ())), preferred_element_type=f32
        )
        for e in range(count):
            mine = rows[e * SLOT : (e + 1) * SLOT]
            mine = jnp.concatenate(
                [mine[:, i * CHUNK : (i + 1) * CHUNK] for i in range(sz.lines)], axis=0
            )
            tile = inter[e // per_owner * count + me * per_owner + e % per_owner] - me * tiles
            tile = jnp.clip(tile, 0, tiles - 1).astype(f32)
            down, across = offs[0:1, e : e + 1].astype(f32), offs[1:2, e : e + 1].astype(f32)
            spare, spot = iota(mine.shape, 0) == NPOLY, iota(mine.shape, 1)
            for lane, value in enumerate((down, across, tile)):
                mine = jnp.where(spare & (spot == lane), value, mine)
            r_out[e] = mine.astype(bf16)
        for copy in reversed(copies[:4]):
            copy.wait()
        for e in range(count):
            s_high, s_low = split(sci_out[e])
            w_high, w_low = split(mask[e].astype(f32) / var[e])
            sw_out[e] = jnp.concatenate([s_high, s_low, w_high, w_low], axis=0).astype(bf16)

    hbm, vmem = pl.BlockSpec(memory_space=pltpu.HBM), pl.BlockSpec(memory_space=pltpu.VMEM)
    shape = (count, sz.height, sz.width)

    def call(*sources):
        template, _, _, _, inter, offs, index, coef, basis = sources
        return pl.pallas_call(
            body,
            in_specs=[hbm] * 9,
            out_specs=(vmem,) * 4,
            out_shape=(
                jax.ShapeDtypeStruct((count, sz.r_rows, CHUNK), bf16),
                jax.ShapeDtypeStruct((count, sz.sw_rows, sz.width), bf16),
                jax.ShapeDtypeStruct(template.shape, bf16),
                jax.ShapeDtypeStruct(shape, f32),
            ),
            scratch_shapes=[
                pltpu.VMEM(shape, f32),
                pltpu.VMEM(shape, jnp.int32),
                pltpu.SMEM(inter.shape, jnp.int32),
                pltpu.VMEM(offs.shape, jnp.int32),
                pltpu.VMEM(index.shape, jnp.int32),
                pltpu.VMEM(coef.shape, f32),
                pltpu.VMEM(basis.shape, f32),
                pltpu.VMEM(((KS + 1) * FINE, nbasis), f32),
                pltpu.VMEM(((KS + 1) * FINE, width), bf16),
                pltpu.SemaphoreType.DMA((9,)),
            ],
            compiler_params=pltpu.CompilerParams(vmem_limit_bytes=VMEM_LIMIT),
            cost_estimate=pl.CostEstimate(
                flops=1_000_000_000, bytes_accessed=6_000_000, transcendentals=0
            ),
            name="prepare",
        )(*[pltpu.with_memory_space_constraint(source, pltpu.HBM) for source in sources])

    return call


def here(axis):
    return lax.axis_index(axis), lax.axis_size(axis)


def partner(me, n, k, back):
    if n & (n - 1) == 0:
        return me ^ k
    return (me + (n - k if back else k)) % n


def pack(sz, n_epoch, tiles, count, peers):
    per_owner = count // n_epoch
    h, w = sz.height, sz.width

    def body(own, low, high, left, low_left, high_left, right, low_right, high_right, sw, r, *outs):
        slabs, sends = outs[0], outs[1:]
        me, _ = here("epoch")
        strip, strips = here("strip")
        band, bands = here("band")

        def column(middle, above, below, t, cut):
            above = jnp.where(strip > 0, above[t, h - 16 :, cut].astype(f32), 0.0)
            above = jnp.where(iota(above.shape, 0) >= 16 - REACH, above, 0.0)
            below = jnp.where(strip < strips - 1, below[t, :16, cut].astype(f32), 0.0)
            below = jnp.where(iota(below.shape, 0) < REACH, below, 0.0)
            parts = [middle[t, :, cut].astype(f32), below]
            gap = sz.rows - h - 32
            if gap:
                parts.append(jnp.zeros((gap, below.shape[1]), f32))
            return jnp.concatenate(parts + [above], axis=0)

        for t in range(tiles):
            slabs[t, :, :w] = column(own, low, high, t, slice(None)).astype(bf16)
            before = column(left, low_left, high_left, t, slice(w - 128, w))
            after = column(right, low_right, high_right, t, slice(0, 128))
            lane = iota(before.shape, 1)
            before = jnp.where((lane >= 128 - REACH) & (band > 0), before, 0.0)
            after = jnp.where((lane < REACH) & (band < bands - 1), after, 0.0)
            if sz.lanes - w == 128:
                slabs[t, :, w:] = (before + after).astype(bf16)
            else:
                slabs[t, :, w : w + 128] = after.astype(bf16)
                slabs[t, :, sz.lanes - 128 :] = before.astype(bf16)
        for k, out in zip(peers, sends):
            q = partner(me, n_epoch, k, False)
            for c in range(per_owner):
                mine = q * per_owner + c
                lines = r[mine].astype(f32)
                tile = lines[NPOLY, 2].astype(jnp.int32)
                slab = slabs[tile].astype(f32)
                if sz.one_side:
                    side = jnp.where(strip == 0, slab[h : h + 16], slab[sz.rows - 16 :])
                    slab = jnp.concatenate([slab[:h], side], axis=0)
                halo = pltpu.roll(slab[:, sz.lanes - 128 :], REACH, 1)
                if sz.lanes - w != 128:
                    halo = halo + pltpu.roll(slab[:, w : w + 128], REACH, 1)
                halo = jnp.where(iota(halo.shape, 1) < 32, halo, 0.0)
                bits = []
                for part in range(sz.halo_rows // 8 * (w // 128)):
                    piece = jnp.zeros((8, 128), f32)
                    for slot in range(4):
                        g = part * 4 + slot
                        if g < sz.groups:
                            piece = piece + pltpu.roll(halo[g * 8 : g * 8 + 8], slot * 32, 1)
                    bits.append(piece)
                wide = w // 128
                bits = [
                    jnp.concatenate(bits[i * wide : (i + 1) * wide], axis=1)
                    for i in range(sz.halo_rows // 8)
                ]
                parts = [lines, slab[:, :w]] + bits
                out[c, : sz.sw_rows] = sw[mine]
                out[c, sz.sw_rows :] = jnp.concatenate(parts, axis=0).astype(bf16)

    vmem = pl.BlockSpec(memory_space=pltpu.VMEM)
    return pl.pallas_call(
        body,
        in_specs=[vmem] * 11,
        out_shape=(jax.ShapeDtypeStruct((tiles, sz.rows, sz.lanes), bf16),)
        + tuple(jax.ShapeDtypeStruct((per_owner, sz.total, w), bf16) for _ in peers),
        compiler_params=pltpu.CompilerParams(vmem_limit_bytes=VMEM_LIMIT),
        cost_estimate=pl.CostEstimate(flops=1_000_000, bytes_accessed=1_000_000, transcendentals=0),
        name="pack",
    )


def models(sz, n_epoch, tiles, count, ks, first, last, carried):
    per_owner = count // n_epoch
    h, w = sz.height, sz.width
    total_models = (2 * len(ks) + first) * per_owner

    def body(sci, sw, r, slabs, *refs):
        refs = list(refs)
        pays = [refs.pop(0) for _ in ks]
        before = [] if first else [refs.pop(0) for _ in range(2)]
        done = [refs.pop(0) for _ in carried]
        if last:
            resid_out, coadd_out = refs.pop(0), refs.pop(0)
        else:
            numer_out, denom_out = refs.pop(0), refs.pop(0)
            resid_outs = [refs.pop(0) for _ in range(len(ks) + first)]
        rhs, lhs, numer, denom = refs
        me, _ = here("epoch")
        strip, strips = here("strip")
        band, bands = here("band")
        row = (strip * h + iota((h, w), 0)).astype(f32)
        col = (band * w + iota((h, w), 1)).astype(f32)
        r_unit = (2.0 * row + 1.0) / (h * strips) - 1.0
        c_unit = (2.0 * col + 1.0) / (w * bands) - 1.0
        for slot in range(2):
            for i in range(sz.chunks):
                used = len(sz.columns(i)) * sz.span
                if used < CHUNK:
                    rhs[slot, i * CHUNK + used : (i + 1) * CHUNK] = jnp.zeros((CHUNK - used, w), bf16)
        turn = [0]

        def model(slab, rows_of):
            slot = turn[0] % 2
            turn[0] += 1
            window, band_rows = rhs.at[slot], lhs.at[slot]
            down = rows_of[NPOLY, 0].astype(jnp.int32)
            across = rows_of[NPOLY, 1].astype(jnp.int32)
            slab = pltpu.roll(slab, lax.rem(sz.rows + HALF - down, sz.rows), 0)[: sz.span]
            slab = pltpu.roll(slab, lax.rem(sz.lanes + HALF - across, sz.lanes), 1).astype(bf16)
            for i in range(sz.chunks):
                for slot, b in enumerate(sz.columns(i)):
                    at = i * CHUNK + slot * sz.span
                    window[at : at + sz.span] = slab[:, b : b + w]
            for i in range(sz.chunks):
                line, phase = divmod(i, sz.phases)
                lines = rows_of[line * SLOT : (line + 1) * SLOT]
                if phase:
                    lines = pltpu.roll(lines, CHUNK - phase * FINE, 1)
                spot = iota(lines.shape, 1)
                lines = jnp.where((spot % sz.span < FINE) & (spot < sz.per * sz.span), lines, 0.0)
                for p in range(NPOLY):
                    line = lines[p : p + 1]
                    line = pltpu.roll(
                        jnp.broadcast_to(line, (h, CHUNK)), 0, 1, stride=1, stride_axis=0
                    )
                    band_rows[p * h : (p + 1) * h, i * CHUNK : (i + 1) * CHUNK] = line
            conv = jnp.dot(band_rows[...].astype(bf16), window[...], preferred_element_type=f32)
            conv = [conv[p * h : (p + 1) * h] for p in range(NPOLY)]
            return (
                conv[0]
                + r_unit * (conv[1] + r_unit * conv[3] + c_unit * conv[4])
                + c_unit * (conv[2] + c_unit * conv[5])
            )

        def add(tile, pair, image):
            science = pair[:h] + pair[h : 2 * h]
            weight = pair[2 * h : 3 * h] + pair[3 * h : 4 * h]
            numer[tile] = numer[tile] + weight * (science - image)
            denom[tile] = denom[tile] + weight

        def tile_of(lines):
            return lines[NPOLY, 2].astype(jnp.int32)

        def keep(j, c, mine, image):
            value = sci[mine] - image
            if last:
                resid_out[mine] = value
            else:
                resid_outs[j][c] = value

        if first:
            numer[...] = jnp.zeros(numer.shape, f32)
            denom[...] = jnp.zeros(denom.shape, f32)
        else:
            numer[...] = before[0][...]
            denom[...] = before[1][...]
        if first:
            for c in range(per_owner):
                mine = me * per_owner + c
                lines = r[mine].astype(f32)
                tile = tile_of(lines)
                image = model(slabs[tile].astype(f32), lines)
                keep(len(ks), c, mine, image)
                add(tile, sw[mine].astype(f32), image)
        for j, (k, pay) in enumerate(zip(ks, pays)):
            q = partner(me, n_epoch, k, True)
            for c in range(per_owner):
                mine = q * per_owner + c
                got = pay[c, sz.sw_rows :].astype(f32)
                lines = r[mine].astype(f32)
                tile = tile_of(lines)
                image = model(slabs[tile].astype(f32), got[: sz.r_rows])
                add(tile, pay[c, : sz.sw_rows].astype(f32), image)
                main = got[sz.r_rows : sz.r_rows + sz.sent]
                halo = got[sz.r_rows + sz.sent :]
                wide = w // 128
                bits = []
                for g in range(sz.groups):
                    part, slot = g // 4, g % 4
                    line, side = part // wide, part % wide
                    piece = halo[line * 8 : line * 8 + 8, side * 128 : side * 128 + 128]
                    piece = pltpu.roll(piece, (128 - slot * 32) % 128, 1)
                    bits.append(piece)
                halo = jnp.concatenate(bits, axis=0)
                lane = iota(halo.shape, 1)
                halo = pltpu.roll(jnp.where(lane < 2 * REACH, halo, 0.0), 128 - REACH, 1)
                if sz.lanes - w != 128:
                    lane = iota(halo.shape, 1)
                    gap = sz.lanes - w - 256
                    pieces = [jnp.where(lane < 64, halo, 0.0)]
                    if gap:
                        pieces.append(jnp.zeros((sz.sent, gap), f32))
                    halo = jnp.concatenate(pieces + [jnp.where(lane < 64, 0.0, halo)], axis=1)
                slab = jnp.concatenate([main, halo], axis=1)
                if sz.one_side:
                    side, none = slab[h:], jnp.zeros((sz.rows - h - 32, sz.lanes), f32)
                    below, above = jnp.where(strip == 0, side, 0.0), jnp.where(strip == 0, 0.0, side)
                    slab = [slab[:h], below, none, above] if none.size else [slab[:h], below, above]
                    slab = jnp.concatenate(slab, axis=0)
                image = model(slab, lines)
                keep(j, c, mine, image)
        if last:
            for (k, where), value in zip(carried, done):
                q = me if k == 0 else partner(me, n_epoch, k, True)
                for c in range(per_owner):
                    resid_out[q * per_owner + c] = value[c]
            coadd_out[...] = numer[...] / (denom[...] + 1.0)
        else:
            numer_out[...] = numer[...]
            denom_out[...] = denom[...]

    image = jax.ShapeDtypeStruct((per_owner, h, w), f32)
    sums = jax.ShapeDtypeStruct((tiles, h, w), f32)
    if last:
        out_shape = (jax.ShapeDtypeStruct((count, h, w), f32), sums)
    else:
        out_shape = (sums, sums) + (image,) * (len(ks) + first)
    vmem = pl.BlockSpec(memory_space=pltpu.VMEM)
    return pl.pallas_call(
        body,
        in_specs=[vmem] * (4 + len(ks) + (0 if first else 2) + len(carried)),
        out_shape=out_shape,
        scratch_shapes=[
            pltpu.VMEM((2, sz.depth, w), bf16),
            pltpu.VMEM((2, NPOLY * h, sz.depth), f32),
            pltpu.VMEM((tiles, h, w), f32),
            pltpu.VMEM((tiles, h, w), f32),
        ],
        compiler_params=pltpu.CompilerParams(vmem_limit_bytes=VMEM_LIMIT),
        cost_estimate=pl.CostEstimate(
            flops=total_models * 400_000_000, bytes_accessed=1_000_000, transcendentals=0
        ),
        name="models",
    )


def neighbours(block, axis):
    count = lax.axis_size(axis)
    if count == 1:
        return block, block
    if count == 2:
        other = lax.ppermute(block, axis, [(0, 1), (1, 0)])
        return other, other
    forward = [(i, i + 1) for i in range(count - 1)]
    backward = [(i + 1, i) for i in range(count - 1)]
    return lax.ppermute(block, axis, forward), lax.ppermute(block, axis, backward)


def local(
    template, science, variance, bad_mask, intersection, offsets, basis_index, coefficients, basis
):
    n_epoch = lax.axis_size("epoch")
    tiles = template.shape[0]
    count, height, width = science.shape
    sz = Sizes(height, width, lax.axis_size("strip"))
    low, high = neighbours(template, "strip")
    left, right = neighbours(template, "band")
    r, sw, own, sci = prepare(sz, n_epoch, tiles, count, basis_index.shape[1])(
        template,
        science,
        variance,
        bad_mask,
        intersection,
        offsets.T,
        basis_index,
        coefficients.transpose(2, 0, 1),
        basis.transpose(1, 2, 0),
    )
    if high is low:
        low, r = lax.optimization_barrier((low, r))
        high = low
        high_left, high_right = low_left, low_right = neighbours(low, "band")
    else:
        low, high, r = lax.optimization_barrier((low, high, r))
        low_left, low_right = neighbours(low, "band")
        high_left, high_right = neighbours(high, "band")
    peers = list(range(1, n_epoch))
    order = peers[-1:] + peers[:-1]
    slabs, *sends = pack(sz, n_epoch, tiles, count, peers)(
        own, low, high, left, low_left, high_left, right, low_right, high_right, sw, r
    )
    pays = {}
    for k, send in zip(order, [sends[peers.index(k)] for k in order]):
        pairs = [(i, partner(i, n_epoch, k, False)) for i in range(n_epoch)]
        pays[k] = lax.ppermute(send, "epoch", pairs)
    stages = [[]] + [[k] for k in order]
    sums, carried = [], []
    for i, ks in enumerate(stages):
        first, last = i == 0, i == len(stages) - 1
        kept = [(k, j) for j, (k, _) in enumerate(carried)] if last else []
        out = models(sz, n_epoch, tiles, count, ks, first, last, kept)(
            sci,
            sw,
            r,
            slabs,
            *[pays[k] for k in ks],
            *sums,
            *([value for _, value in carried] if last else []),
        )
        if last:
            return out
        sums = list(out[:2])
        carried += list(zip(list(ks) + ([0] if first else []), out[2:]))


def solution(mesh):
    in_specs = (
        P(("groups", "epoch"), "strip", "band"),
        P(("groups", "epoch"), "strip", "band"),
        P(("groups", "epoch"), "strip", "band"),
        P(("groups", "epoch"), "strip", "band"),
        P("groups"),
        P(("groups", "epoch"), None),
        P(("groups", "epoch"), None),
        P(("groups", "epoch"), None, None),
        P(),
    )
    out_specs = (P(("groups", "epoch"), "strip", "band"), P(("groups", "epoch"), "strip", "band"))
    return jax.shard_map(local, mesh=mesh, in_specs=in_specs, out_specs=out_specs, check_vma=False)
```

```python
import jax
import jax.numpy as jnp
from jax import lax
from jax.experimental import pallas as pl
from jax.experimental.pallas import tpu as pltpu
from jax.sharding import PartitionSpec as P

KS = 19
HALF = 9
SHIFT = 4
NPOLY = 6
REACH = HALF + SHIFT
SLOT = 8
CHUNK = 256
FINE = 24
VMEM_LIMIT = 24 * 1024 * 1024

highest = lax.Precision.HIGHEST
f32 = jnp.float32
bf16 = jnp.bfloat16


def up(value, step):
    return -(-value // step) * step


class Sizes:
    def __init__(self, height, width, strips):
        self.height, self.width = height, width
        self.rows = up(height + 2 * REACH, 8)
        self.lanes = up(width + 2 * REACH, 128)
        self.span = up(height + KS - 1, 2 * FINE)
        self.phases = self.span // FINE
        self.per = CHUNK // self.span
        self.lines = -(-KS // (self.per * self.phases))
        self.chunks = self.lines * self.phases
        self.depth = self.chunks * CHUNK
        self.sw_rows = 3 * height
        self.r_rows = self.lines * SLOT
        self.one_side = strips <= 2
        self.sent = height + 16 if self.one_side else self.rows
        self.main_at = self.sw_rows + self.r_rows
        self.halo_at = self.main_at + self.sent
        self.groups = self.sent // 8
        self.halo_rows = up(self.groups * 32, width) // width * 8
        self.total = self.halo_at + self.halo_rows

    def place(self, column):
        slot, chunk = column // self.chunks, column % self.chunks
        return chunk // self.phases * CHUNK + (slot * self.phases + chunk % self.phases) * FINE


def iota(shape, axis):
    return lax.broadcasted_iota(jnp.int32, shape, axis)


def split(value):
    high = value.astype(bf16).astype(f32)
    return high, value - high


def encode(weight):
    code = jnp.minimum((weight * 65536.0 + 0.5).astype(jnp.int32), 32767)
    value = (128 + ((code >> 1) & 127)).astype(f32) * 2.0**-70
    for bit in range(7):
        value = jnp.where((code >> (8 + bit)) & 1 == 1, value * 2.0 ** (1 << bit), value)
    return jnp.where(code & 1 == 1, -value, value)


def decode(value):
    size = jnp.abs(value)
    code = jnp.zeros_like(size)
    for bit in range(6, -1, -1):
        above = size >= 2.0 ** ((1 << bit) - 63)
        size = jnp.where(above, size * 2.0 ** -(1 << bit), size)
        code = jnp.where(above, code + (256 << bit), code)
    code = code + (size * 2.0**71 - 256.0)
    return jnp.where(value < 0.0, code + 1.0, code) * 2.0**-16


def prepare(sz, n_epoch, tiles, count, nsel):
    lanes = count * SLOT
    per_owner = count // n_epoch
    width = sz.lines * CHUNK
    nbasis = 128

    def body(*refs):
        sources, refs = refs[:9], refs[9:]
        r_out, sw_out, own_out, sci_out, weight_out = refs[:5]
        var, mask, inter, offs, index, coef, basis, table, place, sems = refs[5:]
        targets = [own_out, sci_out, var, mask, inter, offs, index, coef, basis]
        copies = [
            pltpu.make_async_copy(source, target, sems.at[i])
            for i, (source, target) in enumerate(zip(sources, targets))
        ]
        for copy in reversed(copies):
            copy.start()
        me, _ = here("epoch")
        table[...] = jnp.zeros(table.shape, f32)
        col = iota((FINE, width), 0)
        base = iota((FINE, width), 1) - sz.place(col)
        base = jnp.where(col < KS, base, -1)
        for a in range(0, KS + 1, 2):
            pair = jnp.concatenate([(base == a).astype(f32), (base == a + 1).astype(f32)], axis=0)
            if a + 1 == KS:
                pair = jnp.where(iota(pair.shape, 0) < FINE, pair, 0.0)
            place[a * FINE : (a + 2) * FINE] = pair.astype(bf16)
        for copy in reversed(copies[4:]):
            copy.wait()
        for a in range(KS):
            table[a * FINE : a * FINE + KS, : basis.shape[2]] = basis[a]
        chosen = jnp.concatenate([index[e : e + 1, :] for e in range(count)], axis=1)
        onehot = (iota((nbasis, count * nsel), 0) == chosen).astype(f32)
        blocks = []
        for e in range(count):
            mine = jnp.concatenate([coef[:, e, :], jnp.zeros((SLOT - NPOLY, nsel), f32)], axis=0)
            wide = jnp.concatenate([mine] * count, axis=1)
            blocks.append(jnp.where(iota(wide.shape, 1) // nsel == e, wide, 0.0))
        combine = jnp.concatenate(blocks, axis=0)
        mixing = lax.dot_general(
            onehot, combine, (((1,), (1,)), ((), ())), precision=highest, preferred_element_type=f32
        )
        images = jnp.dot(table[...], mixing, precision=highest, preferred_element_type=f32)
        rows = lax.dot_general(
            images.astype(bf16), place[...], (((0,), (0,)), ((), ())), preferred_element_type=f32
        )
        for e in range(count):
            mine = rows[e * SLOT : (e + 1) * SLOT]
            mine = jnp.concatenate(
                [mine[:, i * CHUNK : (i + 1) * CHUNK] for i in range(sz.lines)], axis=0
            )
            tile = inter[e // per_owner * count + me * per_owner + e % per_owner] - me * tiles
            tile = jnp.clip(tile, 0, tiles - 1).astype(f32)
            down, across = offs[0:1, e : e + 1].astype(f32), offs[1:2, e : e + 1].astype(f32)
            spare, spot = iota(mine.shape, 0) == NPOLY, iota(mine.shape, 1)
            for lane, value in enumerate((down, across, tile)):
                mine = jnp.where(spare & (spot == lane), value, mine)
            r_out[e] = mine.astype(bf16)
        for copy in reversed(copies[:4]):
            copy.wait()
        for e in range(count):
            weight_out[e] = mask[e].astype(f32) / var[e]
            parts = [*split(sci_out[e]), encode(weight_out[e])]
            sw_out[e] = jnp.concatenate(parts, axis=0).astype(bf16)

    hbm, vmem = pl.BlockSpec(memory_space=pltpu.HBM), pl.BlockSpec(memory_space=pltpu.VMEM)
    shape = (count, sz.height, sz.width)

    def call(*sources):
        template, _, _, _, inter, offs, index, coef, basis = sources
        return pl.pallas_call(
            body,
            in_specs=[hbm] * 9,
            out_specs=(vmem,) * 5,
            out_shape=(
                jax.ShapeDtypeStruct((count, sz.r_rows, CHUNK), bf16),
                jax.ShapeDtypeStruct((count, sz.sw_rows, sz.width), bf16),
                jax.ShapeDtypeStruct(template.shape, bf16),
                jax.ShapeDtypeStruct(shape, f32),
                jax.ShapeDtypeStruct(shape, f32),
            ),
            scratch_shapes=[
                pltpu.VMEM(shape, f32),
                pltpu.VMEM(shape, jnp.int32),
                pltpu.SMEM(inter.shape, jnp.int32),
                pltpu.VMEM(offs.shape, jnp.int32),
                pltpu.VMEM(index.shape, jnp.int32),
                pltpu.VMEM(coef.shape, f32),
                pltpu.VMEM(basis.shape, f32),
                pltpu.VMEM(((KS + 1) * FINE, nbasis), f32),
                pltpu.VMEM(((KS + 1) * FINE, width), bf16),
                pltpu.SemaphoreType.DMA((9,)),
            ],
            compiler_params=pltpu.CompilerParams(vmem_limit_bytes=VMEM_LIMIT),
            cost_estimate=pl.CostEstimate(
                flops=1_000_000_000, bytes_accessed=6_000_000, transcendentals=0
            ),
            name="prepare",
        )(*[pltpu.with_memory_space_constraint(source, pltpu.HBM) for source in sources])

    return call


def here(axis):
    return lax.axis_index(axis), lax.axis_size(axis)


def partner(me, n, k, back):
    if n & (n - 1) == 0:
        return me ^ k
    return (me + (n - k if back else k)) % n


def pack(sz, n_epoch, tiles, count, peers):
    per_owner = count // n_epoch
    h, w = sz.height, sz.width

    def body(own, low, high, left, low_left, high_left, right, low_right, high_right, sw, r, *outs):
        slabs, sends = outs[0], outs[1:]
        me, _ = here("epoch")
        strip, strips = here("strip")
        band, bands = here("band")

        def column(middle, above, below, t, cut):
            above = jnp.where(strip > 0, above[t, h - 16 :, cut].astype(f32), 0.0)
            above = jnp.where(iota(above.shape, 0) >= 16 - REACH, above, 0.0)
            below = jnp.where(strip < strips - 1, below[t, :16, cut].astype(f32), 0.0)
            below = jnp.where(iota(below.shape, 0) < REACH, below, 0.0)
            parts = [middle[t, :, cut].astype(f32), below]
            gap = sz.rows - h - 32
            if gap:
                parts.append(jnp.zeros((gap, below.shape[1]), f32))
            return jnp.concatenate(parts + [above], axis=0)

        for t in range(tiles):
            slabs[t, :, :w] = column(own, low, high, t, slice(None)).astype(bf16)
            before = column(left, low_left, high_left, t, slice(w - 128, w))
            after = column(right, low_right, high_right, t, slice(0, 128))
            lane = iota(before.shape, 1)
            before = jnp.where((lane >= 128 - REACH) & (band > 0), before, 0.0)
            after = jnp.where((lane < REACH) & (band < bands - 1), after, 0.0)
            if sz.lanes - w == 128:
                slabs[t, :, w:] = (before + after).astype(bf16)
            else:
                slabs[t, :, w : w + 128] = after.astype(bf16)
                slabs[t, :, sz.lanes - 128 :] = before.astype(bf16)
        for k, out in zip(peers, sends):
            q = partner(me, n_epoch, k, False)
            for c in range(per_owner):
                mine = q * per_owner + c
                lines = r[mine].astype(f32)
                tile = lines[NPOLY, 2].astype(jnp.int32)
                slab = slabs[tile].astype(f32)
                if sz.one_side:
                    side = jnp.where(strip == 0, slab[h : h + 16], slab[sz.rows - 16 :])
                    slab = jnp.concatenate([slab[:h], side], axis=0)
                halo = pltpu.roll(slab[:, sz.lanes - 128 :], REACH, 1)
                if sz.lanes - w != 128:
                    halo = halo + pltpu.roll(slab[:, w : w + 128], REACH, 1)
                halo = jnp.where(iota(halo.shape, 1) < 32, halo, 0.0)
                bits = []
                for part in range(sz.halo_rows // 8 * (w // 128)):
                    piece = jnp.zeros((8, 128), f32)
                    for slot in range(4):
                        g = part * 4 + slot
                        if g < sz.groups:
                            piece = piece + pltpu.roll(halo[g * 8 : g * 8 + 8], slot * 32, 1)
                    bits.append(piece)
                wide = w // 128
                bits = [
                    jnp.concatenate(bits[i * wide : (i + 1) * wide], axis=1)
                    for i in range(sz.halo_rows // 8)
                ]
                parts = [sw[mine].astype(f32), lines, slab[:, :w]] + bits
                out[c] = jnp.concatenate(parts, axis=0).astype(bf16)

    vmem = pl.BlockSpec(memory_space=pltpu.VMEM)
    return pl.pallas_call(
        body,
        in_specs=[vmem] * 11,
        out_shape=(jax.ShapeDtypeStruct((tiles, sz.rows, sz.lanes), bf16),)
        + tuple(jax.ShapeDtypeStruct((per_owner, sz.total, w), bf16) for _ in peers),
        compiler_params=pltpu.CompilerParams(vmem_limit_bytes=VMEM_LIMIT),
        cost_estimate=pl.CostEstimate(flops=1_000_000, bytes_accessed=1_000_000, transcendentals=0),
        name="pack",
    )


def models(sz, n_epoch, tiles, count, ks, first, last, carried):
    per_owner = count // n_epoch
    h, w = sz.height, sz.width
    total_models = (2 * len(ks) + first) * per_owner

    def body(sci, weight, r, slabs, *refs):
        refs = list(refs)
        pays = [refs.pop(0) for _ in ks]
        before = [] if first else [refs.pop(0) for _ in range(2)]
        done = [refs.pop(0) for _ in carried]
        if last:
            resid_out, coadd_out = refs.pop(0), refs.pop(0)
        else:
            numer_out, denom_out = refs.pop(0), refs.pop(0)
            resid_outs = [refs.pop(0) for _ in range(len(ks) + first)]
        rhs, lhs = refs
        me, _ = here("epoch")
        strip, strips = here("strip")
        band, bands = here("band")

        jobs = []

        def job(kind, q, c, slab, lines):
            mine = q * per_owner + c
            own = lines if kind == "local" else r[mine].astype(f32)
            scalars = [lines[NPOLY, lane].astype(jnp.int32) for lane in range(2)]
            tile = None if kind == "sent" else own[NPOLY, 2].astype(jnp.int32)
            jobs.append((kind, mine, slab, lines, scalars, tile, own))

        if first:
            for c in range(per_owner):
                job("local", me, c, None, r[me * per_owner + c].astype(f32))
        for k, pay in zip(ks, pays):
            q = partner(me, n_epoch, k, True)
            for c in range(per_owner):
                got = pay[c].astype(f32)
                job("owned", q, c, got, got[sz.sw_rows : sz.main_at])
                job("sent", q, c, got, r[q * per_owner + c].astype(f32))

        row = (strip * h + iota((h, sz.lanes), 0)).astype(f32)
        r_unit = (2.0 * row + 1.0) / (h * strips) - 1.0
        for slot in range(2):
            used = sz.per * sz.span
            if used < CHUNK:
                rhs[slot, used:] = jnp.zeros((CHUNK - used, sz.lanes), bf16)

        def model(turn, slab, lines, scalars):
            window, band_rows = rhs.at[turn % 2], lhs.at[turn % 2]
            down, across = scalars
            slab = pltpu.roll(slab, lax.rem(sz.rows + HALF - down, sz.rows), 0)[: sz.span]
            slab = pltpu.roll(slab.astype(bf16), lax.rem(sz.lanes + HALF - across, sz.lanes), 1)
            for slot in range(sz.per):
                moved = pltpu.roll(slab, sz.lanes - slot * sz.chunks, 1) if slot else slab
                window[slot * sz.span : (slot + 1) * sz.span] = moved
            image = None
            for i in reversed(range(sz.chunks)):
                line, phase = divmod(i, sz.phases)
                part = lines[line * SLOT : (line + 1) * SLOT]
                if phase:
                    part = pltpu.roll(part, CHUNK - phase * FINE, 1)
                spot = iota(part.shape, 1)
                part = jnp.where((spot % sz.span < FINE) & (spot < sz.per * sz.span), part, 0.0)
                at = i * NPOLY * h
                for p in range(NPOLY):
                    band_rows[at + p * h : at + (p + 1) * h] = pltpu.roll(
                        jnp.broadcast_to(part[p : p + 1], (h, CHUNK)), 0, 1, stride=1, stride_axis=0
                    )
                conv = jnp.dot(
                    band_rows[at : at + NPOLY * h].astype(bf16), window[...], preferred_element_type=f32
                )
                conv = [conv[p * h : (p + 1) * h] for p in range(NPOLY)]
                col = (band * w + iota((h, sz.lanes), 1) - i).astype(f32)
                c_unit = (2.0 * col + 1.0) / (w * bands) - 1.0
                value = (
                    conv[0]
                    + r_unit * (conv[1] + r_unit * conv[3] + c_unit * conv[4])
                    + c_unit * (conv[2] + c_unit * conv[5])
                )
                image = value if image is None else pltpu.roll(image, sz.lanes - 1, 1) + value
            return image[:, :w]

        def sent_slab(got):
            main, halo = got[sz.main_at : sz.halo_at], got[sz.halo_at :]
            wide = w // 128
            bits = []
            for g in range(sz.groups):
                part, slot = g // 4, g % 4
                line, side = part // wide, part % wide
                piece = halo[line * 8 : line * 8 + 8, side * 128 : side * 128 + 128]
                bits.append(pltpu.roll(piece, (128 - slot * 32) % 128, 1))
            halo = jnp.concatenate(bits, axis=0)
            lane = iota(halo.shape, 1)
            halo = pltpu.roll(jnp.where(lane < 2 * REACH, halo, 0.0), 128 - REACH, 1)
            if sz.lanes - w != 128:
                gap = sz.lanes - w - 256
                pieces = [jnp.where(lane < 64, halo, 0.0)]
                if gap:
                    pieces.append(jnp.zeros((sz.sent, gap), f32))
                halo = jnp.concatenate(pieces + [jnp.where(lane < 64, 0.0, halo)], axis=1)
            slab = jnp.concatenate([main, halo], axis=1)
            if sz.one_side:
                side, none = slab[h:], jnp.zeros((sz.rows - h - 32, sz.lanes), f32)
                below, above = jnp.where(strip == 0, side, 0.0), jnp.where(strip == 0, 0.0, side)
                slab = [slab[:h], below, none, above] if none.size else [slab[:h], below, above]
                slab = jnp.concatenate(slab, axis=0)
            return slab

        numer = [before[0][t] if before else jnp.zeros((h, w), f32) for t in range(tiles)]
        denom = [before[1][t] if before else jnp.zeros((h, w), f32) for t in range(tiles)]
        kept = 0
        for turn, (kind, mine, got, lines, scalars, tile, own) in enumerate(jobs):
            slab = sent_slab(got) if kind == "sent" else slabs[tile].astype(f32)
            image = model(turn, slab, lines, scalars)
            if kind == "owned":
                science, seen = got[:h] + got[h : 2 * h], decode(got[2 * h : 3 * h])
            else:
                science, seen = sci[mine], weight[mine]
                if last:
                    resid_out[mine] = science - image
                else:
                    resid_outs[kept // per_owner][kept % per_owner] = science - image
                kept += 1
            if kind != "sent":
                change = seen * (science - image)
                covered = jnp.broadcast_to(own[NPOLY : NPOLY + 1, 2:3], (h, w))
                for t in range(tiles):
                    numer[t] = numer[t] + jnp.where(covered == t, change, 0.0)
                    denom[t] = denom[t] + jnp.where(covered == t, seen, 0.0)
        for t in range(tiles):
            if last:
                coadd_out[t] = numer[t] / (denom[t] + 1.0)
            else:
                numer_out[t], denom_out[t] = numer[t], denom[t]
        if last:
            for k, value in zip(carried, done):
                q = me if k == 0 else partner(me, n_epoch, k, True)
                for c in range(per_owner):
                    resid_out[q * per_owner + c] = value[c]

    image = jax.ShapeDtypeStruct((per_owner, h, w), f32)
    sums = jax.ShapeDtypeStruct((tiles, h, w), f32)
    if last:
        out_shape = (jax.ShapeDtypeStruct((count, h, w), f32), sums)
    else:
        out_shape = (sums, sums) + (image,) * (len(ks) + first)
    vmem = pl.BlockSpec(memory_space=pltpu.VMEM)
    return pl.pallas_call(
        body,
        in_specs=[vmem] * (4 + len(ks) + (0 if first else 2) + len(carried)),
        out_shape=out_shape,
        scratch_shapes=[
            pltpu.VMEM((2, CHUNK, sz.lanes), bf16),
            pltpu.VMEM((2, sz.chunks * NPOLY * h, CHUNK), f32),
        ],
        compiler_params=pltpu.CompilerParams(vmem_limit_bytes=VMEM_LIMIT),
        cost_estimate=pl.CostEstimate(
            flops=total_models * 400_000_000, bytes_accessed=1_000_000, transcendentals=0
        ),
        name="models",
    )


def neighbours(block, axis):
    count = lax.axis_size(axis)
    if count == 1:
        return block, block
    if count == 2:
        other = lax.ppermute(block, axis, [(0, 1), (1, 0)])
        return other, other
    forward = [(i, i + 1) for i in range(count - 1)]
    backward = [(i + 1, i) for i in range(count - 1)]
    return lax.ppermute(block, axis, forward), lax.ppermute(block, axis, backward)


def local(
    template, science, variance, bad_mask, intersection, offsets, basis_index, coefficients, basis
):
    n_epoch = lax.axis_size("epoch")
    tiles = template.shape[0]
    count, height, width = science.shape
    sz = Sizes(height, width, lax.axis_size("strip"))
    low, high = neighbours(template, "strip")
    left, right = neighbours(template, "band")
    r, sw, own, sci, weight = prepare(sz, n_epoch, tiles, count, basis_index.shape[1])(
        template,
        science,
        variance,
        bad_mask,
        intersection,
        offsets.T,
        basis_index,
        coefficients.transpose(2, 0, 1),
        basis.transpose(1, 2, 0),
    )
    if high is low:
        low, r = lax.optimization_barrier((low, r))
        high = low
        high_left, high_right = low_left, low_right = neighbours(low, "band")
    else:
        low, high, r = lax.optimization_barrier((low, high, r))
        low_left, low_right = neighbours(low, "band")
        high_left, high_right = neighbours(high, "band")
    peers = list(range(1, n_epoch))
    order = peers[-1:] + peers[:-1]
    slabs, *sends = pack(sz, n_epoch, tiles, count, peers)(
        own, low, high, left, low_left, high_left, right, low_right, high_right, sw, r
    )
    pays = {}
    for k, send in zip(order, [sends[peers.index(k)] for k in order]):
        pairs = [(i, partner(i, n_epoch, k, False)) for i in range(n_epoch)]
        pays[k] = lax.ppermute(send, "epoch", pairs)
    stages = [[]] + [[k] for k in order]
    sums, carried = [], []
    for i, ks in enumerate(stages):
        first, last = i == 0, i == len(stages) - 1
        kept = [k for k, _ in carried] if last else []
        out = models(sz, n_epoch, tiles, count, ks, first, last, kept)(
            sci,
            weight,
            r,
            slabs,
            *[pays[k] for k in ks],
            *sums,
            *([value for _, value in carried] if last else []),
        )
        if last:
            return out
        sums = list(out[:2])
        carried += list(zip(list(ks) + ([0] if first else []), out[2:]))


def solution(mesh):
    in_specs = (
        P(("groups", "epoch"), "strip", "band"),
        P(("groups", "epoch"), "strip", "band"),
        P(("groups", "epoch"), "strip", "band"),
        P(("groups", "epoch"), "strip", "band"),
        P("groups"),
        P(("groups", "epoch"), None),
        P(("groups", "epoch"), None),
        P(("groups", "epoch"), None, None),
        P(),
    )
    out_specs = (P(("groups", "epoch"), "strip", "band"), P(("groups", "epoch"), "strip", "band"))
    return jax.shard_map(local, mesh=mesh, in_specs=in_specs, out_specs=out_specs, check_vma=False)
```

```python
import jax
import jax.numpy as jnp
from jax import lax
from jax.experimental import pallas as pl
from jax.experimental.pallas import tpu as pltpu
from jax.sharding import PartitionSpec as P

KS = 19
HALF = 9
SHIFT = 4
NPOLY = 6
REACH = HALF + SHIFT
SLOT = 8
CHUNK = 256
FINE = 24
VMEM_LIMIT = 24 * 1024 * 1024

highest = lax.Precision.HIGHEST
f32 = jnp.float32
bf16 = jnp.bfloat16


def up(value, step):
    return -(-value // step) * step


class Sizes:
    def __init__(self, height, width, strips):
        self.height, self.width = height, width
        self.rows = up(height + 2 * REACH, 8)
        self.lanes = up(width + 2 * REACH, 128)
        self.span = up(height + KS - 1, 2 * FINE)
        self.phases = self.span // FINE
        self.per = CHUNK // self.span
        self.lines = -(-KS // (self.per * self.phases))
        self.chunks = self.lines * self.phases
        self.depth = self.chunks * CHUNK
        self.sw_rows = 3 * height
        self.r_rows = self.lines * SLOT
        self.one_side = strips <= 2
        self.sent = height + 16 if self.one_side else self.rows
        self.main_at = self.sw_rows + self.r_rows
        self.halo_at = self.main_at + self.sent
        self.groups = self.sent // 8
        self.halo_rows = up(self.groups * 32, width) // width * 8
        self.total = self.halo_at + self.halo_rows

    def place(self, column):
        slot, chunk = column // self.chunks, column % self.chunks
        return chunk // self.phases * CHUNK + (slot * self.phases + chunk % self.phases) * FINE


def iota(shape, axis):
    return lax.broadcasted_iota(jnp.int32, shape, axis)


def split(value):
    high = value.astype(bf16).astype(f32)
    return high, value - high


def encode(weight):
    code = jnp.minimum((weight * 65536.0 + 0.5).astype(jnp.int32), 32767)
    value = (128 + ((code >> 1) & 127)).astype(f32) * 2.0**-70
    for bit in range(7):
        value = jnp.where((code >> (8 + bit)) & 1 == 1, value * 2.0 ** (1 << bit), value)
    return jnp.where(code & 1 == 1, -value, value)


def decode(value):
    size = jnp.abs(value)
    code = jnp.zeros_like(size)
    for bit in range(6, -1, -1):
        above = size >= 2.0 ** ((1 << bit) - 63)
        size = jnp.where(above, size * 2.0 ** -(1 << bit), size)
        code = jnp.where(above, code + (256 << bit), code)
    code = code + (size * 2.0**71 - 256.0)
    return jnp.where(value < 0.0, code + 1.0, code) * 2.0**-16


def prepare(sz, n_epoch, tiles, count, nsel):
    lanes = count * SLOT
    per_owner = count // n_epoch
    width = sz.lines * CHUNK
    nbasis = 128

    def body(*refs):
        sources, refs = refs[:9], refs[9:]
        r_out, sw_out, own_out, sci_out, weight_out = refs[:5]
        var, mask, inter, offs, index, coef, basis, table, place, sems = refs[5:]
        targets = [own_out, sci_out, var, mask, inter, offs, index, coef, basis]
        copies = [
            pltpu.make_async_copy(source, target, sems.at[i])
            for i, (source, target) in enumerate(zip(sources, targets))
        ]
        for copy in reversed(copies):
            copy.start()
        me, _ = here("epoch")
        table[...] = jnp.zeros(table.shape, f32)
        col = iota((FINE, width), 0)
        base = iota((FINE, width), 1) - sz.place(col)
        base = jnp.where(col < KS, base, -1)
        for a in range(0, KS + 1, 2):
            pair = jnp.concatenate([(base == a).astype(f32), (base == a + 1).astype(f32)], axis=0)
            if a + 1 == KS:
                pair = jnp.where(iota(pair.shape, 0) < FINE, pair, 0.0)
            place[a * FINE : (a + 2) * FINE] = pair.astype(bf16)
        for copy in reversed(copies[4:]):
            copy.wait()
        for a in range(KS):
            table[a * FINE : a * FINE + KS, : basis.shape[2]] = basis[a]
        chosen = jnp.concatenate([index[e : e + 1, :] for e in range(count)], axis=1)
        onehot = (iota((nbasis, count * nsel), 0) == chosen).astype(f32)
        blocks = []
        for e in range(count):
            mine = jnp.concatenate([coef[:, e, :], jnp.zeros((SLOT - NPOLY, nsel), f32)], axis=0)
            wide = jnp.concatenate([mine] * count, axis=1)
            blocks.append(jnp.where(iota(wide.shape, 1) // nsel == e, wide, 0.0))
        combine = jnp.concatenate(blocks, axis=0)
        mixing = lax.dot_general(
            onehot, combine, (((1,), (1,)), ((), ())), precision=highest, preferred_element_type=f32
        )
        images = jnp.dot(table[...], mixing, precision=highest, preferred_element_type=f32)
        rows = lax.dot_general(
            images.astype(bf16), place[...], (((0,), (0,)), ((), ())), preferred_element_type=f32
        )
        for e in range(count):
            mine = rows[e * SLOT : (e + 1) * SLOT]
            mine = jnp.concatenate(
                [mine[:, i * CHUNK : (i + 1) * CHUNK] for i in range(sz.lines)], axis=0
            )
            tile = inter[e // per_owner * count + me * per_owner + e % per_owner] - me * tiles
            tile = jnp.clip(tile, 0, tiles - 1).astype(f32)
            down, across = offs[0:1, e : e + 1].astype(f32), offs[1:2, e : e + 1].astype(f32)
            spare, spot = iota(mine.shape, 0) == NPOLY, iota(mine.shape, 1)
            for lane, value in enumerate((down, across, tile)):
                mine = jnp.where(spare & (spot == lane), value, mine)
            r_out[e] = mine.astype(bf16)
        for copy in reversed(copies[:4]):
            copy.wait()
        for e in range(count):
            weight_out[e] = mask[e].astype(f32) / var[e]
            parts = [*split(sci_out[e]), encode(weight_out[e])]
            sw_out[e] = jnp.concatenate(parts, axis=0).astype(bf16)

    hbm, vmem = pl.BlockSpec(memory_space=pltpu.HBM), pl.BlockSpec(memory_space=pltpu.VMEM)
    shape = (count, sz.height, sz.width)

    def call(*sources):
        template, _, _, _, inter, offs, index, coef, basis = sources
        return pl.pallas_call(
            body,
            in_specs=[hbm] * 9,
            out_specs=(vmem,) * 5,
            out_shape=(
                jax.ShapeDtypeStruct((count, sz.r_rows, CHUNK), bf16),
                jax.ShapeDtypeStruct((count, sz.sw_rows, sz.width), bf16),
                jax.ShapeDtypeStruct(template.shape, bf16),
                jax.ShapeDtypeStruct(shape, f32),
                jax.ShapeDtypeStruct(shape, f32),
            ),
            scratch_shapes=[
                pltpu.VMEM(shape, f32),
                pltpu.VMEM(shape, jnp.int32),
                pltpu.SMEM(inter.shape, jnp.int32),
                pltpu.VMEM(offs.shape, jnp.int32),
                pltpu.VMEM(index.shape, jnp.int32),
                pltpu.VMEM(coef.shape, f32),
                pltpu.VMEM(basis.shape, f32),
                pltpu.VMEM(((KS + 1) * FINE, nbasis), f32),
                pltpu.VMEM(((KS + 1) * FINE, width), bf16),
                pltpu.SemaphoreType.DMA((9,)),
            ],
            compiler_params=pltpu.CompilerParams(vmem_limit_bytes=VMEM_LIMIT),
            cost_estimate=pl.CostEstimate(
                flops=1_000_000_000, bytes_accessed=6_000_000, transcendentals=0
            ),
            name="prepare",
        )(*[pltpu.with_memory_space_constraint(source, pltpu.HBM) for source in sources])

    return call


def here(axis):
    return lax.axis_index(axis), lax.axis_size(axis)


def partner(me, n, k, back):
    if n & (n - 1) == 0:
        return me ^ k
    return (me + (n - k if back else k)) % n


def pack(sz, n_epoch, tiles, count, peers):
    per_owner = count // n_epoch
    h, w = sz.height, sz.width

    def body(own, low, high, left, low_left, high_left, right, low_right, high_right, sw, r, *outs):
        slabs, sends = outs[0], outs[1:]
        me, _ = here("epoch")
        strip, strips = here("strip")
        band, bands = here("band")

        def column(middle, above, below, t, cut):
            above = jnp.where(strip > 0, above[t, h - 16 :, cut].astype(f32), 0.0)
            above = jnp.where(iota(above.shape, 0) >= 16 - REACH, above, 0.0)
            below = jnp.where(strip < strips - 1, below[t, :16, cut].astype(f32), 0.0)
            below = jnp.where(iota(below.shape, 0) < REACH, below, 0.0)
            parts = [middle[t, :, cut].astype(f32), below]
            gap = sz.rows - h - 32
            if gap:
                parts.append(jnp.zeros((gap, below.shape[1]), f32))
            return jnp.concatenate(parts + [above], axis=0)

        for t in range(tiles):
            slabs[t, :, :w] = column(own, low, high, t, slice(None)).astype(bf16)
            before = column(left, low_left, high_left, t, slice(w - 128, w))
            after = column(right, low_right, high_right, t, slice(0, 128))
            lane = iota(before.shape, 1)
            before = jnp.where((lane >= 128 - REACH) & (band > 0), before, 0.0)
            after = jnp.where((lane < REACH) & (band < bands - 1), after, 0.0)
            if sz.lanes - w == 128:
                slabs[t, :, w:] = (before + after).astype(bf16)
            else:
                slabs[t, :, w : w + 128] = after.astype(bf16)
                slabs[t, :, sz.lanes - 128 :] = before.astype(bf16)
        for k, out in zip(peers, sends):
            q = partner(me, n_epoch, k, False)
            for c in range(per_owner):
                mine = q * per_owner + c
                lines = r[mine].astype(f32)
                tile = lines[NPOLY, 2].astype(jnp.int32)
                slab = slabs[tile].astype(f32)
                if sz.one_side:
                    side = jnp.where(strip == 0, slab[h : h + 16], slab[sz.rows - 16 :])
                    slab = jnp.concatenate([slab[:h], side], axis=0)
                halo = pltpu.roll(slab[:, sz.lanes - 128 :], REACH, 1)
                if sz.lanes - w != 128:
                    halo = halo + pltpu.roll(slab[:, w : w + 128], REACH, 1)
                halo = jnp.where(iota(halo.shape, 1) < 32, halo, 0.0)
                bits = []
                for part in range(sz.halo_rows // 8 * (w // 128)):
                    piece = jnp.zeros((8, 128), f32)
                    for slot in range(4):
                        g = part * 4 + slot
                        if g < sz.groups:
                            piece = piece + pltpu.roll(halo[g * 8 : g * 8 + 8], slot * 32, 1)
                    bits.append(piece)
                wide = w // 128
                bits = [
                    jnp.concatenate(bits[i * wide : (i + 1) * wide], axis=1)
                    for i in range(sz.halo_rows // 8)
                ]
                parts = [sw[mine].astype(f32), lines, slab[:, :w]] + bits
                out[c] = jnp.concatenate(parts, axis=0).astype(bf16)

    vmem = pl.BlockSpec(memory_space=pltpu.VMEM)
    return pl.pallas_call(
        body,
        in_specs=[vmem] * 11,
        out_shape=(jax.ShapeDtypeStruct((tiles, sz.rows, sz.lanes), bf16),)
        + tuple(jax.ShapeDtypeStruct((per_owner, sz.total, w), bf16) for _ in peers),
        compiler_params=pltpu.CompilerParams(vmem_limit_bytes=VMEM_LIMIT),
        cost_estimate=pl.CostEstimate(flops=1_000_000, bytes_accessed=1_000_000, transcendentals=0),
        name="pack",
    )


def models(sz, n_epoch, tiles, count, ks, first, last, carried):
    per_owner = count // n_epoch
    h, w = sz.height, sz.width
    total_models = (2 * len(ks) + first) * per_owner

    def body(sci, weight, r, slabs, *refs):
        refs = list(refs)
        pays = [refs.pop(0) for _ in ks]
        before = [] if first else [refs.pop(0) for _ in range(2)]
        done = [refs.pop(0) for _ in carried]
        if last:
            resid_out, coadd_out = refs.pop(0), refs.pop(0)
        else:
            numer_out, denom_out = refs.pop(0), refs.pop(0)
            resid_outs = [refs.pop(0) for _ in range(len(ks) + first)]
        rhs, lhs, *refs = refs
        me, _ = here("epoch")
        strip, strips = here("strip")
        band, bands = here("band")

        copies = []

        def send(source, target):
            copies.append(pltpu.make_async_copy(source, target, out_sems.at[len(copies)]))
            copies[-1].start()

        if last:
            fresh, sums, out_sems = refs
            for k, value in zip(carried, done):
                q = me if k == 0 else partner(me, n_epoch, k, True)
                send(value, resid_out.at[pl.ds(q * per_owner, per_owner)])

        jobs = []

        def job(kind, q, c, slab, lines):
            mine = q * per_owner + c
            own = lines if kind == "local" else r[mine].astype(f32)
            scalars = [lines[NPOLY, lane].astype(jnp.int32) for lane in range(2)]
            tile = None if kind == "sent" else own[NPOLY, 2].astype(jnp.int32)
            jobs.append((kind, mine, slab, lines, scalars, tile, own))

        if first:
            for c in range(per_owner):
                job("local", me, c, None, r[me * per_owner + c].astype(f32))
        for k, pay in zip(ks, pays):
            q = partner(me, n_epoch, k, True)
            for c in range(per_owner):
                got = pay[c].astype(f32)
                job("owned", q, c, got, got[sz.sw_rows : sz.main_at])
            for c in range(per_owner):
                job("sent", q, c, pay[c].astype(f32), r[q * per_owner + c].astype(f32))

        row = (strip * h + iota((h, sz.lanes), 0)).astype(f32)
        r_unit = (2.0 * row + 1.0) / (h * strips) - 1.0
        for slot in range(2):
            used = sz.per * sz.span
            if used < CHUNK:
                rhs[slot, used:] = jnp.zeros((CHUNK - used, sz.lanes), bf16)

        def model(turn, slab, lines, scalars):
            window, band_rows = rhs.at[turn % 2], lhs.at[turn % 2]
            down, across = scalars
            slab = pltpu.roll(slab, lax.rem(sz.rows + HALF - down, sz.rows), 0)[: sz.span]
            slab = pltpu.roll(slab.astype(bf16), lax.rem(sz.lanes + HALF - across, sz.lanes), 1)
            for slot in range(sz.per):
                moved = pltpu.roll(slab, sz.lanes - slot * sz.chunks, 1) if slot else slab
                window[slot * sz.span : (slot + 1) * sz.span] = moved
            image = None
            for i in reversed(range(sz.chunks)):
                line, phase = divmod(i, sz.phases)
                part = lines[line * SLOT : (line + 1) * SLOT]
                if phase:
                    part = pltpu.roll(part, CHUNK - phase * FINE, 1)
                spot = iota(part.shape, 1)
                part = jnp.where((spot % sz.span < FINE) & (spot < sz.per * sz.span), part, 0.0)
                at = i * NPOLY * h
                for p in range(NPOLY):
                    band_rows[at + p * h : at + (p + 1) * h] = pltpu.roll(
                        jnp.broadcast_to(part[p : p + 1], (h, CHUNK)), 0, 1, stride=1, stride_axis=0
                    )
                conv = jnp.dot(
                    band_rows[at : at + NPOLY * h].astype(bf16), window[...], preferred_element_type=f32
                )
                conv = [conv[p * h : (p + 1) * h] for p in range(NPOLY)]
                col = (band * w + iota((h, sz.lanes), 1) - i).astype(f32)
                c_unit = (2.0 * col + 1.0) / (w * bands) - 1.0
                value = (
                    conv[0]
                    + r_unit * (conv[1] + r_unit * conv[3] + c_unit * conv[4])
                    + c_unit * (conv[2] + c_unit * conv[5])
                )
                image = value if image is None else pltpu.roll(image, sz.lanes - 1, 1) + value
            return image[:, :w]

        def sent_slab(got):
            main, halo = got[sz.main_at : sz.halo_at], got[sz.halo_at :]
            wide = w // 128
            bits = []
            for g in range(sz.groups):
                part, slot = g // 4, g % 4
                line, side = part // wide, part % wide
                piece = halo[line * 8 : line * 8 + 8, side * 128 : side * 128 + 128]
                bits.append(pltpu.roll(piece, (128 - slot * 32) % 128, 1))
            halo = jnp.concatenate(bits, axis=0)
            lane = iota(halo.shape, 1)
            halo = pltpu.roll(jnp.where(lane < 2 * REACH, halo, 0.0), 128 - REACH, 1)
            if sz.lanes - w != 128:
                gap = sz.lanes - w - 256
                pieces = [jnp.where(lane < 64, halo, 0.0)]
                if gap:
                    pieces.append(jnp.zeros((sz.sent, gap), f32))
                halo = jnp.concatenate(pieces + [jnp.where(lane < 64, 0.0, halo)], axis=1)
            slab = jnp.concatenate([main, halo], axis=1)
            if sz.one_side:
                side, none = slab[h:], jnp.zeros((sz.rows - h - 32, sz.lanes), f32)
                below, above = jnp.where(strip == 0, side, 0.0), jnp.where(strip == 0, 0.0, side)
                slab = [slab[:h], below, none, above] if none.size else [slab[:h], below, above]
                slab = jnp.concatenate(slab, axis=0)
            return slab

        numer = [before[0][t] if before else jnp.zeros((h, w), f32) for t in range(tiles)]
        denom = [before[1][t] if before else jnp.zeros((h, w), f32) for t in range(tiles)]
        kept = 0
        settled = max(turn for turn, job in enumerate(jobs) if job[0] != "sent")
        for turn, (kind, mine, got, lines, scalars, tile, own) in enumerate(jobs):
            slab = sent_slab(got) if kind == "sent" else slabs[tile].astype(f32)
            image = model(turn, slab, lines, scalars)
            if kind == "owned":
                science, seen = got[:h] + got[h : 2 * h], decode(got[2 * h : 3 * h])
            else:
                science, seen = sci[mine], weight[mine]
                if last:
                    fresh[kept] = science - image
                    send(fresh.at[kept], resid_out.at[mine])
                else:
                    resid_outs[kept // per_owner][kept % per_owner] = science - image
                kept += 1
            if kind != "sent":
                change = seen * (science - image)
                covered = jnp.broadcast_to(own[NPOLY : NPOLY + 1, 2:3], (h, w))
                for t in range(tiles):
                    numer[t] = numer[t] + jnp.where(covered == t, change, 0.0)
                    denom[t] = denom[t] + jnp.where(covered == t, seen, 0.0)
            if turn == settled:
                for t in range(tiles):
                    if last:
                        sums[t] = numer[t] / (denom[t] + 1.0)
                    else:
                        numer_out[t], denom_out[t] = numer[t], denom[t]
                if last:
                    send(sums, coadd_out)
        for copy in copies:
            copy.wait()

    image = jax.ShapeDtypeStruct((per_owner, h, w), f32)
    sums = jax.ShapeDtypeStruct((tiles, h, w), f32)
    if last:
        out_shape = (jax.ShapeDtypeStruct((count, h, w), f32), sums)
    else:
        out_shape = (sums, sums) + (image,) * (len(ks) + first)
    vmem, hbm = pl.BlockSpec(memory_space=pltpu.VMEM), pl.BlockSpec(memory_space=pltpu.HBM)
    scratch = [
        pltpu.VMEM((2, CHUNK, sz.lanes), bf16),
        pltpu.VMEM((2, sz.chunks * NPOLY * h, CHUNK), f32),
    ]
    if last:
        new = len(ks) * per_owner
        scratch += [
            pltpu.VMEM((new, h, w), f32),
            pltpu.VMEM((tiles, h, w), f32),
            pltpu.SemaphoreType.DMA((len(carried) + new + 1,)),
        ]
    return pl.pallas_call(
        body,
        in_specs=[vmem] * (4 + len(ks) + (0 if first else 2) + len(carried)),
        out_specs=(hbm if last else vmem,) * len(out_shape),
        out_shape=out_shape,
        scratch_shapes=scratch,
        compiler_params=pltpu.CompilerParams(vmem_limit_bytes=VMEM_LIMIT),
        cost_estimate=pl.CostEstimate(
            flops=total_models * 400_000_000, bytes_accessed=1_000_000, transcendentals=0
        ),
        name="models",
    )


def surroundings(block):
    strips, bands = lax.axis_size("strip"), lax.axis_size("band")
    sent, found = {}, {}
    for down in (-1, 0, 1):
        for across in (-1, 0, 1):
            if down == 0 and across == 0:
                continue
            pairs = []
            for s in range(strips):
                for b in range(bands):
                    to_s = s ^ 1 if strips == 2 and down else s - down
                    to_b = b ^ 1 if bands == 2 and across else b - across
                    if 0 <= to_s < strips and 0 <= to_b < bands:
                        pairs.append((s * bands + b, to_s * bands + to_b))
            key = tuple(pairs)
            if key and key not in sent:
                sent[key] = lax.ppermute(block, ("strip", "band"), pairs)
            found[down, across] = key
    return {step: sent.get(key, block) for step, key in found.items()}


def local(
    template, science, variance, bad_mask, intersection, offsets, basis_index, coefficients, basis
):
    n_epoch = lax.axis_size("epoch")
    tiles = template.shape[0]
    count, height, width = science.shape
    sz = Sizes(height, width, lax.axis_size("strip"))
    around = surroundings(template)
    r, sw, own, sci, weight = prepare(sz, n_epoch, tiles, count, basis_index.shape[1])(
        template,
        science,
        variance,
        bad_mask,
        intersection,
        offsets.T,
        basis_index,
        coefficients.transpose(2, 0, 1),
        basis.transpose(1, 2, 0),
    )
    around[0, 0] = own
    peers = list(range(1, n_epoch))
    order = peers[-1:] + peers[:-1]
    slabs, *sends = pack(sz, n_epoch, tiles, count, peers)(
        *[around[down, across] for across in (0, -1, 1) for down in (0, -1, 1)], sw, r
    )
    pays = {}
    for k, send in zip(order, [sends[peers.index(k)] for k in order]):
        pairs = [(i, partner(i, n_epoch, k, False)) for i in range(n_epoch)]
        pays[k] = lax.ppermute(send, "epoch", pairs)
    stages = [[]] + [[k] for k in order]
    sums, carried = [], []
    for i, ks in enumerate(stages):
        first, last = i == 0, i == len(stages) - 1
        kept = [k for k, _ in carried] if last else []
        out = models(sz, n_epoch, tiles, count, ks, first, last, kept)(
            sci,
            weight,
            r,
            slabs,
            *[pays[k] for k in ks],
            *sums,
            *([value for _, value in carried] if last else []),
        )
        if last:
            return out
        sums = list(out[:2])
        carried += list(zip(list(ks) + ([0] if first else []), out[2:]))


def solution(mesh):
    in_specs = (
        P(("groups", "epoch"), "strip", "band"),
        P(("groups", "epoch"), "strip", "band"),
        P(("groups", "epoch"), "strip", "band"),
        P(("groups", "epoch"), "strip", "band"),
        P("groups"),
        P(("groups", "epoch"), None),
        P(("groups", "epoch"), None),
        P(("groups", "epoch"), None, None),
        P(),
    )
    out_specs = (P(("groups", "epoch"), "strip", "band"), P(("groups", "epoch"), "strip", "band"))
    return jax.shard_map(local, mesh=mesh, in_specs=in_specs, out_specs=out_specs, check_vma=False)
```

```python
import jax
import jax.numpy as jnp
from jax import lax
from jax.experimental import pallas as pl
from jax.experimental.pallas import tpu as pltpu
from jax.sharding import PartitionSpec as P

KS = 19
HALF = 9
SHIFT = 4
NPOLY = 6
REACH = HALF + SHIFT
SLOT = 8
CHUNK = 256
FINE = 24
VMEM_LIMIT = 24 * 1024 * 1024

highest = lax.Precision.HIGHEST
f32 = jnp.float32
bf16 = jnp.bfloat16


def up(value, step):
    return -(-value // step) * step


class Sizes:
    def __init__(self, height, width, strips):
        self.height, self.width = height, width
        self.rows = up(height + 2 * REACH, 8)
        self.lanes = up(width + 2 * REACH, 128)
        self.span = up(height + KS - 1, 2 * FINE)
        self.phases = self.span // FINE
        self.per = CHUNK // self.span
        self.lines = -(-KS // (self.per * self.phases))
        self.chunks = self.lines * self.phases
        self.depth = self.chunks * CHUNK
        self.sw_rows = 3 * height
        self.r_rows = self.lines * SLOT
        self.one_side = strips <= 2
        self.sent = height + 16 if self.one_side else self.rows
        self.main_at = self.sw_rows + self.r_rows
        self.halo_at = self.main_at + self.sent
        self.groups = self.sent // 8
        self.halo_rows = up(self.groups * 32, width) // width * 8
        self.total = self.halo_at + self.halo_rows

    def place(self, column):
        slot, chunk = column // self.chunks, column % self.chunks
        return chunk // self.phases * CHUNK + (slot * self.phases + chunk % self.phases) * FINE


def iota(shape, axis):
    return lax.broadcasted_iota(jnp.int32, shape, axis)


def split(value):
    high = value.astype(bf16).astype(f32)
    return high, value - high


def encode(weight):
    code = jnp.minimum((weight * 65536.0 + 0.5).astype(jnp.int32), 32767)
    value = (128 + ((code >> 1) & 127)).astype(f32) * 2.0**-70
    for bit in range(7):
        value = jnp.where((code >> (8 + bit)) & 1 == 1, value * 2.0 ** (1 << bit), value)
    return jnp.where(code & 1 == 1, -value, value)


def decode(value):
    size = jnp.abs(value)
    code = jnp.zeros_like(size)
    for bit in range(6, -1, -1):
        above = size >= 2.0 ** ((1 << bit) - 63)
        size = jnp.where(above, size * 2.0 ** -(1 << bit), size)
        code = jnp.where(above, code + (256 << bit), code)
    code = code + (size * 2.0**71 - 256.0)
    return jnp.where(value < 0.0, code + 1.0, code) * 2.0**-16


def prepare(sz, n_epoch, tiles, count, nsel):
    lanes = count * SLOT
    per_owner = count // n_epoch
    width = sz.lines * CHUNK
    nbasis = 128

    def body(*refs):
        sources, refs = refs[:9], refs[9:]
        r_out, sw_out, own_out, sci_out, weight_out = refs[:5]
        var, mask, inter, offs, index, coef, basis, table, place, sems = refs[5:]
        targets = [own_out, sci_out, var, mask, inter, offs, index, coef, basis]
        copies = [
            pltpu.make_async_copy(source, target, sems.at[i])
            for i, (source, target) in enumerate(zip(sources, targets))
        ]
        for copy in reversed(copies):
            copy.start()
        me, _ = here("epoch")
        table[...] = jnp.zeros(table.shape, f32)
        col = iota((FINE, width), 0)
        base = iota((FINE, width), 1) - sz.place(col)
        base = jnp.where(col < KS, base, -1)
        for a in range(0, KS + 1, 2):
            pair = jnp.concatenate([(base == a).astype(f32), (base == a + 1).astype(f32)], axis=0)
            if a + 1 == KS:
                pair = jnp.where(iota(pair.shape, 0) < FINE, pair, 0.0)
            place[a * FINE : (a + 2) * FINE] = pair.astype(bf16)
        for copy in reversed(copies[4:]):
            copy.wait()
        for a in range(KS):
            table[a * FINE : a * FINE + KS, : basis.shape[2]] = basis[a]
        chosen = jnp.concatenate([index[e : e + 1, :] for e in range(count)], axis=1)
        onehot = (iota((nbasis, count * nsel), 0) == chosen).astype(f32)
        blocks = []
        for e in range(count):
            mine = jnp.concatenate([coef[:, e, :], jnp.zeros((SLOT - NPOLY, nsel), f32)], axis=0)
            wide = jnp.concatenate([mine] * count, axis=1)
            blocks.append(jnp.where(iota(wide.shape, 1) // nsel == e, wide, 0.0))
        combine = jnp.concatenate(blocks, axis=0)
        mixing = lax.dot_general(
            onehot, combine, (((1,), (1,)), ((), ())), precision=highest, preferred_element_type=f32
        )
        images = jnp.dot(table[...], mixing, precision=highest, preferred_element_type=f32)
        rows = lax.dot_general(
            images.astype(bf16), place[...], (((0,), (0,)), ((), ())), preferred_element_type=f32
        )
        for e in range(count):
            mine = rows[e * SLOT : (e + 1) * SLOT]
            mine = jnp.concatenate(
                [mine[:, i * CHUNK : (i + 1) * CHUNK] for i in range(sz.lines)], axis=0
            )
            tile = inter[e // per_owner * count + me * per_owner + e % per_owner] - me * tiles
            tile = jnp.clip(tile, 0, tiles - 1).astype(f32)
            down, across = offs[0:1, e : e + 1].astype(f32), offs[1:2, e : e + 1].astype(f32)
            spare, spot = iota(mine.shape, 0) == NPOLY, iota(mine.shape, 1)
            for lane, value in enumerate((down, across, tile)):
                mine = jnp.where(spare & (spot == lane), value, mine)
            r_out[e] = mine.astype(bf16)
        for copy in reversed(copies[:4]):
            copy.wait()
        for e in range(count):
            weight_out[e] = mask[e].astype(f32) / var[e]
            parts = [*split(sci_out[e]), encode(weight_out[e])]
            sw_out[e] = jnp.concatenate(parts, axis=0).astype(bf16)

    hbm, vmem = pl.BlockSpec(memory_space=pltpu.HBM), pl.BlockSpec(memory_space=pltpu.VMEM)
    shape = (count, sz.height, sz.width)

    def call(*sources):
        template, _, _, _, inter, offs, index, coef, basis = sources
        return pl.pallas_call(
            body,
            in_specs=[hbm] * 9,
            out_specs=(vmem,) * 5,
            out_shape=(
                jax.ShapeDtypeStruct((count, sz.r_rows, CHUNK), bf16),
                jax.ShapeDtypeStruct((count, sz.sw_rows, sz.width), bf16),
                jax.ShapeDtypeStruct(template.shape, bf16),
                jax.ShapeDtypeStruct(shape, f32),
                jax.ShapeDtypeStruct(shape, f32),
            ),
            scratch_shapes=[
                pltpu.VMEM(shape, f32),
                pltpu.VMEM(shape, jnp.int32),
                pltpu.SMEM(inter.shape, jnp.int32),
                pltpu.VMEM(offs.shape, jnp.int32),
                pltpu.VMEM(index.shape, jnp.int32),
                pltpu.VMEM(coef.shape, f32),
                pltpu.VMEM(basis.shape, f32),
                pltpu.VMEM(((KS + 1) * FINE, nbasis), f32),
                pltpu.VMEM(((KS + 1) * FINE, width), bf16),
                pltpu.SemaphoreType.DMA((9,)),
            ],
            compiler_params=pltpu.CompilerParams(vmem_limit_bytes=VMEM_LIMIT),
            cost_estimate=pl.CostEstimate(
                flops=1_000_000_000, bytes_accessed=6_000_000, transcendentals=0
            ),
            name="prepare",
        )(*[pltpu.with_memory_space_constraint(source, pltpu.HBM) for source in sources])

    return call


def here(axis):
    return lax.axis_index(axis), lax.axis_size(axis)


def partner(me, n, k, back):
    if n & (n - 1) == 0:
        return me ^ k
    return (me + (n - k if back else k)) % n


def pack(sz, n_epoch, tiles, count, peers):
    per_owner = count // n_epoch
    h, w = sz.height, sz.width

    def body(own, low, high, left, low_left, high_left, right, low_right, high_right, sw, r, *outs):
        slabs, sends = outs[0], outs[1:]
        me, _ = here("epoch")
        strip, strips = here("strip")
        band, bands = here("band")

        def column(middle, above, below, t, cut):
            above = jnp.where(strip > 0, above[t, h - 16 :, cut].astype(f32), 0.0)
            above = jnp.where(iota(above.shape, 0) >= 16 - REACH, above, 0.0)
            below = jnp.where(strip < strips - 1, below[t, :16, cut].astype(f32), 0.0)
            below = jnp.where(iota(below.shape, 0) < REACH, below, 0.0)
            parts = [middle[t, :, cut].astype(f32), below]
            gap = sz.rows - h - 32
            if gap:
                parts.append(jnp.zeros((gap, below.shape[1]), f32))
            return jnp.concatenate(parts + [above], axis=0)

        for t in range(tiles):
            slabs[t, :, :w] = column(own, low, high, t, slice(None)).astype(bf16)
            before = column(left, low_left, high_left, t, slice(w - 128, w))
            after = column(right, low_right, high_right, t, slice(0, 128))
            lane = iota(before.shape, 1)
            before = jnp.where((lane >= 128 - REACH) & (band > 0), before, 0.0)
            after = jnp.where((lane < REACH) & (band < bands - 1), after, 0.0)
            if sz.lanes - w == 128:
                slabs[t, :, w:] = (before + after).astype(bf16)
            else:
                slabs[t, :, w : w + 128] = after.astype(bf16)
                slabs[t, :, sz.lanes - 128 :] = before.astype(bf16)
        for k, out in zip(peers, sends):
            q = partner(me, n_epoch, k, False)
            for c in range(per_owner):
                mine = q * per_owner + c
                lines = r[mine].astype(f32)
                tile = lines[NPOLY, 2].astype(jnp.int32)
                slab = slabs[tile].astype(f32)
                if sz.one_side:
                    side = jnp.where(strip == 0, slab[h : h + 16], slab[sz.rows - 16 :])
                    slab = jnp.concatenate([slab[:h], side], axis=0)
                halo = pltpu.roll(slab[:, sz.lanes - 128 :], REACH, 1)
                if sz.lanes - w != 128:
                    halo = halo + pltpu.roll(slab[:, w : w + 128], REACH, 1)
                halo = jnp.where(iota(halo.shape, 1) < 32, halo, 0.0)
                bits = []
                for part in range(sz.halo_rows // 8 * (w // 128)):
                    piece = jnp.zeros((8, 128), f32)
                    for slot in range(4):
                        g = part * 4 + slot
                        if g < sz.groups:
                            piece = piece + pltpu.roll(halo[g * 8 : g * 8 + 8], slot * 32, 1)
                    bits.append(piece)
                wide = w // 128
                bits = [
                    jnp.concatenate(bits[i * wide : (i + 1) * wide], axis=1)
                    for i in range(sz.halo_rows // 8)
                ]
                parts = [sw[mine].astype(f32), lines, slab[:, :w]] + bits
                out[c] = jnp.concatenate(parts, axis=0).astype(bf16)

    vmem = pl.BlockSpec(memory_space=pltpu.VMEM)
    return pl.pallas_call(
        body,
        in_specs=[vmem] * 11,
        out_shape=(jax.ShapeDtypeStruct((tiles, sz.rows, sz.lanes), bf16),)
        + tuple(jax.ShapeDtypeStruct((per_owner, sz.total, w), bf16) for _ in peers),
        compiler_params=pltpu.CompilerParams(vmem_limit_bytes=VMEM_LIMIT),
        cost_estimate=pl.CostEstimate(flops=1_000_000, bytes_accessed=1_000_000, transcendentals=0),
        name="pack",
    )


def models(sz, n_epoch, tiles, count, ks, first, last, carried):
    per_owner = count // n_epoch
    h, w = sz.height, sz.width
    total_models = (2 * len(ks) + first) * per_owner

    def body(sci, weight, r, slabs, *refs):
        refs = list(refs)
        pays = [refs.pop(0) for _ in ks]
        before = [] if first else [refs.pop(0) for _ in range(2)]
        done = [refs.pop(0) for _ in carried]
        if last:
            resid_out, coadd_out = refs.pop(0), refs.pop(0)
        else:
            numer_out, denom_out = refs.pop(0), refs.pop(0)
            resid_outs = [refs.pop(0) for _ in range(len(ks) + first)]
        rhs, lhs, *refs = refs
        me, _ = here("epoch")
        strip, strips = here("strip")
        band, bands = here("band")

        copies = []

        def send(source, target):
            copies.append(pltpu.make_async_copy(source, target, out_sems.at[len(copies)]))
            copies[-1].start()

        if last:
            fresh, sums, out_sems = refs
            for k, value in zip(carried, done):
                q = me if k == 0 else partner(me, n_epoch, k, True)
                send(value, resid_out.at[pl.ds(q * per_owner, per_owner)])

        jobs = []

        def job(kind, q, c, slab, lines):
            mine = q * per_owner + c
            own = lines if kind == "local" else r[mine].astype(f32)
            scalars = [lines[NPOLY, lane].astype(jnp.int32) for lane in range(2)]
            tile = None if kind == "sent" else own[NPOLY, 2].astype(jnp.int32)
            jobs.append((kind, mine, slab, lines, scalars, tile, own))

        if first:
            for c in range(per_owner):
                job("local", me, c, None, r[me * per_owner + c].astype(f32))
        for k, pay in zip(ks, pays):
            q = partner(me, n_epoch, k, True)
            for c in range(per_owner):
                got = pay[c].astype(f32)
                job("owned", q, c, got, got[sz.sw_rows : sz.main_at])
            for c in range(per_owner):
                job("sent", q, c, pay[c].astype(f32), r[q * per_owner + c].astype(f32))

        row = (strip * h + iota((h, 128), 0)).astype(f32)
        r_unit = (2.0 * row + 1.0) / (h * strips) - 1.0
        r_unit = jnp.concatenate([r_unit] * (sz.lanes // 128), axis=1)
        spot = iota((SLOT, CHUNK), 1)
        filled = (spot % sz.span < FINE) & (spot < sz.per * sz.span)
        c_units = []
        for i in range(sz.chunks):
            col = (band * w + iota((8, sz.lanes), 1) - i).astype(f32)
            col = (2.0 * col + 1.0) / (w * bands) - 1.0
            c_units.append(jnp.concatenate([col] * (h // 8), axis=0))
        for slot in range(2):
            used = sz.per * sz.span
            if used < CHUNK:
                rhs[slot, used:] = jnp.zeros((CHUNK - used, sz.lanes), bf16)

        def windows(turn, slab, scalars):
            window = rhs.at[turn % 2]
            down, across = scalars
            slab = pltpu.roll(slab, lax.rem(sz.rows + HALF - down, sz.rows), 0)[: sz.span]
            slab = pltpu.roll(slab.astype(bf16), lax.rem(sz.lanes + HALF - across, sz.lanes), 1)
            for slot in range(sz.per):
                moved = pltpu.roll(slab, sz.lanes - slot * sz.chunks, 1) if slot else slab
                window[slot * sz.span : (slot + 1) * sz.span] = moved

        def band_matrix(turn, lines):
            band_rows = lhs.at[turn % 2]
            for i in range(sz.chunks):
                line, phase = divmod(i, sz.phases)
                part = lines[line * SLOT : (line + 1) * SLOT]
                if phase:
                    part = pltpu.roll(part, CHUNK - phase * FINE, 1)
                part = jnp.where(filled, part, 0.0)
                at = i * NPOLY * h
                for p in range(NPOLY):
                    band_rows[at + p * h : at + (p + 1) * h] = pltpu.roll(
                        jnp.broadcast_to(part[p : p + 1], (h, CHUNK)), 0, 1, stride=1, stride_axis=0
                    )

        def chunk_image(turn, i):
            at = i * NPOLY * h
            conv = jnp.dot(
                lhs[turn % 2, at : at + NPOLY * h].astype(bf16), rhs[turn % 2], preferred_element_type=f32
            )
            conv = [conv[p * h : (p + 1) * h] for p in range(NPOLY)]
            c_unit = c_units[i]
            return (
                conv[0]
                + r_unit * (conv[1] + r_unit * conv[3] + c_unit * conv[4])
                + c_unit * (conv[2] + c_unit * conv[5])
            )

        def sent_slab(got):
            main, halo = got[sz.main_at : sz.halo_at], got[sz.halo_at :]
            wide = w // 128
            bits = []
            for g in range(sz.groups):
                part, slot = g // 4, g % 4
                line, side = part // wide, part % wide
                piece = halo[line * 8 : line * 8 + 8, side * 128 : side * 128 + 128]
                bits.append(pltpu.roll(piece, (128 - slot * 32) % 128, 1))
            halo = jnp.concatenate(bits, axis=0)
            lane = iota(halo.shape, 1)
            halo = pltpu.roll(jnp.where(lane < 2 * REACH, halo, 0.0), 128 - REACH, 1)
            if sz.lanes - w != 128:
                gap = sz.lanes - w - 256
                pieces = [jnp.where(lane < 64, halo, 0.0)]
                if gap:
                    pieces.append(jnp.zeros((sz.sent, gap), f32))
                halo = jnp.concatenate(pieces + [jnp.where(lane < 64, 0.0, halo)], axis=1)
            slab = jnp.concatenate([main, halo], axis=1)
            if sz.one_side:
                side, none = slab[h:], jnp.zeros((sz.rows - h - 32, sz.lanes), f32)
                below, above = jnp.where(strip == 0, side, 0.0), jnp.where(strip == 0, 0.0, side)
                slab = [slab[:h], below, none, above] if none.size else [slab[:h], below, above]
                slab = jnp.concatenate(slab, axis=0)
            return slab

        numer = [before[0][t] if before else jnp.zeros((h, w), f32) for t in range(tiles)]
        denom = [before[1][t] if before else jnp.zeros((h, w), f32) for t in range(tiles)]
        kept = 0
        settled = max(turn for turn, job in enumerate(jobs) if job[0] != "sent")
        images = []
        for turn in range(0, len(jobs), 2):
            pair = list(enumerate(jobs))[turn : turn + 2]
            for at, (kind, mine, got, lines, scalars, tile, own) in pair:
                band_matrix(at, lines)
            for at, (kind, mine, got, lines, scalars, tile, own) in pair:
                windows(at, sent_slab(got) if kind == "sent" else slabs[tile].astype(f32), scalars)
            parts = [None for _ in pair]
            for i in reversed(range(sz.chunks)):
                for slot, (at, _) in enumerate(pair):
                    value = chunk_image(at, i)
                    value = pltpu.roll(value, sz.lanes - i, 1) if i else value
                    parts[slot] = value if parts[slot] is None else parts[slot] + value
            images += [part[:, :w] for part in parts]
        for turn, (kind, mine, got, lines, scalars, tile, own) in enumerate(jobs):
            image = images[turn]
            if kind == "owned":
                science, seen = got[:h] + got[h : 2 * h], decode(got[2 * h : 3 * h])
            else:
                science, seen = sci[mine], weight[mine]
                if last:
                    fresh[kept] = science - image
                    send(fresh.at[kept], resid_out.at[mine])
                else:
                    resid_outs[kept // per_owner][kept % per_owner] = science - image
                kept += 1
            if kind != "sent":
                change = seen * (science - image)
                covered = jnp.broadcast_to(own[NPOLY : NPOLY + 1, 2:3], (h, w))
                for t in range(tiles):
                    numer[t] = numer[t] + jnp.where(covered == t, change, 0.0)
                    denom[t] = denom[t] + jnp.where(covered == t, seen, 0.0)
            if turn == settled:
                for t in range(tiles):
                    if last:
                        sums[t] = numer[t] / (denom[t] + 1.0)
                    else:
                        numer_out[t], denom_out[t] = numer[t], denom[t]
                if last:
                    send(sums, coadd_out)
        for copy in copies:
            copy.wait()

    image = jax.ShapeDtypeStruct((per_owner, h, w), f32)
    sums = jax.ShapeDtypeStruct((tiles, h, w), f32)
    if last:
        out_shape = (jax.ShapeDtypeStruct((count, h, w), f32), sums)
    else:
        out_shape = (sums, sums) + (image,) * (len(ks) + first)
    vmem, hbm = pl.BlockSpec(memory_space=pltpu.VMEM), pl.BlockSpec(memory_space=pltpu.HBM)
    scratch = [
        pltpu.VMEM((2, CHUNK, sz.lanes), bf16),
        pltpu.VMEM((2, sz.chunks * NPOLY * h, CHUNK), f32),
    ]
    if last:
        new = len(ks) * per_owner
        scratch += [
            pltpu.VMEM((new, h, w), f32),
            pltpu.VMEM((tiles, h, w), f32),
            pltpu.SemaphoreType.DMA((len(carried) + new + 1,)),
        ]
    return pl.pallas_call(
        body,
        in_specs=[vmem] * (4 + len(ks) + (0 if first else 2) + len(carried)),
        out_specs=(hbm if last else vmem,) * len(out_shape),
        out_shape=out_shape,
        scratch_shapes=scratch,
        compiler_params=pltpu.CompilerParams(vmem_limit_bytes=VMEM_LIMIT),
        cost_estimate=pl.CostEstimate(
            flops=total_models * 400_000_000, bytes_accessed=1_000_000, transcendentals=0
        ),
        name="models",
    )


def surroundings(block):
    strips, bands = lax.axis_size("strip"), lax.axis_size("band")
    sent, found = {}, {}
    for down in (-1, 0, 1):
        for across in (-1, 0, 1):
            if down == 0 and across == 0:
                continue
            pairs = []
            for s in range(strips):
                for b in range(bands):
                    to_s = s ^ 1 if strips == 2 and down else s - down
                    to_b = b ^ 1 if bands == 2 and across else b - across
                    if 0 <= to_s < strips and 0 <= to_b < bands:
                        pairs.append((s * bands + b, to_s * bands + to_b))
            key = tuple(pairs)
            if key and key not in sent:
                sent[key] = lax.ppermute(block, ("strip", "band"), pairs)
            found[down, across] = key
    return {step: sent.get(key, block) for step, key in found.items()}


def local(
    template, science, variance, bad_mask, intersection, offsets, basis_index, coefficients, basis
):
    n_epoch = lax.axis_size("epoch")
    tiles = template.shape[0]
    count, height, width = science.shape
    sz = Sizes(height, width, lax.axis_size("strip"))
    around = surroundings(template)
    r, sw, own, sci, weight = prepare(sz, n_epoch, tiles, count, basis_index.shape[1])(
        template,
        science,
        variance,
        bad_mask,
        intersection,
        offsets.T,
        basis_index,
        coefficients.transpose(2, 0, 1),
        basis.transpose(1, 2, 0),
    )
    around[0, 0] = own
    peers = list(range(1, n_epoch))
    order = peers[-1:] + peers[:-1]
    slabs, *sends = pack(sz, n_epoch, tiles, count, peers)(
        *[around[down, across] for across in (0, -1, 1) for down in (0, -1, 1)], sw, r
    )
    pays = {}
    for k, send in zip(order, [sends[peers.index(k)] for k in order]):
        pairs = [(i, partner(i, n_epoch, k, False)) for i in range(n_epoch)]
        pays[k] = lax.ppermute(send, "epoch", pairs)
    stages = [[]] + [[k] for k in order]
    sums, carried = [], []
    for i, ks in enumerate(stages):
        first, last = i == 0, i == len(stages) - 1
        kept = [k for k, _ in carried] if last else []
        out = models(sz, n_epoch, tiles, count, ks, first, last, kept)(
            sci,
            weight,
            r,
            slabs,
            *[pays[k] for k in ks],
            *sums,
            *([value for _, value in carried] if last else []),
        )
        if last:
            return out
        sums = list(out[:2])
        carried += list(zip(list(ks) + ([0] if first else []), out[2:]))


def solution(mesh):
    in_specs = (
        P(("groups", "epoch"), "strip", "band"),
        P(("groups", "epoch"), "strip", "band"),
        P(("groups", "epoch"), "strip", "band"),
        P(("groups", "epoch"), "strip", "band"),
        P("groups"),
        P(("groups", "epoch"), None),
        P(("groups", "epoch"), None),
        P(("groups", "epoch"), None, None),
        P(),
    )
    out_specs = (P(("groups", "epoch"), "strip", "band"), P(("groups", "epoch"), "strip", "band"))
    return jax.shard_map(local, mesh=mesh, in_specs=in_specs, out_specs=out_specs, check_vma=False)
```

```python
import jax
import jax.numpy as jnp
from jax import lax
from jax.experimental import pallas as pl
from jax.experimental.pallas import tpu as pltpu
from jax.sharding import PartitionSpec as P

KS = 19
HALF = 9
SHIFT = 4
NPOLY = 6
REACH = HALF + SHIFT
SLOT = 8
CHUNK = 256
FINE = 24
VMEM_LIMIT = 24 * 1024 * 1024

highest = lax.Precision.HIGHEST
f32 = jnp.float32
bf16 = jnp.bfloat16


def up(value, step):
    return -(-value // step) * step


class Sizes:
    def __init__(self, height, width, strips):
        self.height, self.width = height, width
        self.rows = up(height + 2 * REACH, 8)
        self.lanes = up(width + 2 * REACH, 128)
        self.span = up(height + KS - 1, 2 * FINE)
        self.phases = self.span // FINE
        self.per = CHUNK // self.span
        self.lines = -(-KS // (self.per * self.phases))
        self.chunks = self.lines * self.phases
        self.depth = self.chunks * CHUNK
        self.sw_rows = 2 * height
        self.r_rows = self.lines * SLOT
        self.one_side = strips <= 2
        self.sent = height + 16 if self.one_side else self.rows
        self.main_at = self.sw_rows + self.r_rows
        self.halo_at = self.main_at + self.sent
        self.groups = self.sent // 8
        self.halo_rows = up(self.groups * 32, width) // width * 8
        self.total = self.halo_at + self.halo_rows

    def place(self, column):
        slot, chunk = column // self.chunks, column % self.chunks
        return chunk // self.phases * CHUNK + (slot * self.phases + chunk % self.phases) * FINE


def iota(shape, axis):
    return lax.broadcasted_iota(jnp.int32, shape, axis)


def raised(value, power, bits):
    for bit in range(bits):
        more = (power >> bit) & 1 == 1
        for _ in range(2 if bit == 7 else 1):
            value = jnp.where(more, value * 2.0 ** (1 << min(bit, 6)), value)
    return value


def lowered(value, least, bits):
    power = jnp.zeros(value.shape, jnp.int32)
    for bit in reversed(range(bits)):
        more = value >= 2.0 ** ((1 << bit) + least)
        for _ in range(2 if bit == 7 else 1):
            value = jnp.where(more, value * 2.0 ** -(1 << min(bit, 6)), value)
        power = jnp.where(more, power + (1 << bit), power)
    return value, power


def encode_weight(weight):
    code = jnp.minimum((weight * 65536.0 + 0.5).astype(jnp.int32), 32767)
    value = raised((128 + ((code >> 1) & 127)).astype(f32) * 2.0**-70, code >> 8, 7)
    return jnp.where(code & 1 == 1, -value, value)


def decode_weight(value):
    size, power = lowered(jnp.abs(value), -63, 7)
    code = (power * 256).astype(f32) + (size * 2.0**71 - 256.0)
    return jnp.where(value < 0.0, code + 1.0, code) * 2.0**-16


def encode_science(science):
    size, power = lowered(jnp.abs(science) * 2.0**26, 0, 5)
    fine = power >= 14
    code = ((size - 1.0) * jnp.where(fine, 2048.0, 128.0) + 0.5).astype(jnp.int32)
    code = jnp.minimum(code, jnp.where(fine, 2047, 127))
    exponent = jnp.where(fine, (power - 14) * 16 + (code & 15), 240 + power)
    value = (128 + jnp.where(fine, code >> 4, code)).astype(f32) * 2.0**-66 * 2.0**-67
    value = jnp.where(size >= 1.0, raised(value, exponent, 8), 0.0)
    return jnp.where(science < 0.0, -value, value)


def decode_science(value):
    size, exponent = lowered(jnp.abs(value), -126, 8)
    coarse = size * 2.0**66 * 2.0**67
    fine = exponent < 240
    mantissa = jnp.where(fine, coarse * 16.0 + (exponent & 15).astype(f32), coarse * 16.0)
    power = jnp.where(fine, (exponent >> 4) + 14, exponent - 240)
    size = jnp.where(value == 0.0, 0.0, raised(mantissa * 2.0**-37, power, 5))
    return jnp.where(value < 0.0, -size, size)


def prepare(sz, n_epoch, tiles, count, nsel):
    lanes = count * SLOT
    per_owner = count // n_epoch
    width = sz.lines * CHUNK
    nbasis = 128

    def body(*refs):
        sources, refs = refs[:9], refs[9:]
        r_out, sw_out, own_out, sci_out, weight_out = refs[:5]
        var, mask, inter, offs, index, coef, basis, table, place, sems = refs[5:]
        targets = [own_out, sci_out, var, mask, inter, offs, index, coef, basis]
        copies = [
            pltpu.make_async_copy(source, target, sems.at[i])
            for i, (source, target) in enumerate(zip(sources, targets))
        ]
        for copy in reversed(copies):
            copy.start()
        me, _ = here("epoch")
        table[...] = jnp.zeros(table.shape, f32)
        col = iota((FINE, width), 0)
        base = iota((FINE, width), 1) - sz.place(col)
        base = jnp.where(col < KS, base, -1)
        for a in range(0, KS + 1, 2):
            pair = jnp.concatenate([(base == a).astype(f32), (base == a + 1).astype(f32)], axis=0)
            if a + 1 == KS:
                pair = jnp.where(iota(pair.shape, 0) < FINE, pair, 0.0)
            place[a * FINE : (a + 2) * FINE] = pair.astype(bf16)
        for copy in reversed(copies[4:]):
            copy.wait()
        for a in range(KS):
            table[a * FINE : a * FINE + KS, : basis.shape[2]] = basis[a]
        chosen = jnp.concatenate([index[e : e + 1, :] for e in range(count)], axis=1)
        onehot = (iota((nbasis, count * nsel), 0) == chosen).astype(f32)
        blocks = []
        for e in range(count):
            mine = jnp.concatenate([coef[:, e, :], jnp.zeros((SLOT - NPOLY, nsel), f32)], axis=0)
            wide = jnp.concatenate([mine] * count, axis=1)
            blocks.append(jnp.where(iota(wide.shape, 1) // nsel == e, wide, 0.0))
        combine = jnp.concatenate(blocks, axis=0)
        mixing = lax.dot_general(
            onehot, combine, (((1,), (1,)), ((), ())), precision=highest, preferred_element_type=f32
        )
        images = jnp.dot(table[...], mixing, precision=highest, preferred_element_type=f32)
        rows = lax.dot_general(
            images.astype(bf16), place[...], (((0,), (0,)), ((), ())), preferred_element_type=f32
        )
        for copy in reversed(copies[:4]):
            copy.wait()
        for e in range(count):
            weight_out[e] = mask[e].astype(f32) / var[e]
            science = jnp.where(mask[e] == 0, 0.0, sci_out[e])
            top = jnp.max(jnp.abs(science), axis=(0, 1), keepdims=True)
            _, power = lowered(top * 2.0**100, 0, 7)
            science = science * raised(jnp.ones_like(top), 102 - power, 7)
            parts = [encode_science(science), encode_weight(weight_out[e])]
            sw_out[e] = jnp.concatenate(parts, axis=0).astype(bf16)
            mine = rows[e * SLOT : (e + 1) * SLOT]
            mine = jnp.concatenate(
                [mine[:, i * CHUNK : (i + 1) * CHUNK] for i in range(sz.lines)], axis=0
            )
            tile = inter[e // per_owner * count + me * per_owner + e % per_owner] - me * tiles
            tile = jnp.clip(tile, 0, tiles - 1).astype(f32)
            down, across = offs[0:1, e : e + 1].astype(f32), offs[1:2, e : e + 1].astype(f32)
            scale = raised(jnp.full_like(top, 2.0**-102), power, 7)
            spare, spot = iota(mine.shape, 0) == NPOLY, iota(mine.shape, 1)
            for lane, value in enumerate((down, across, tile, scale)):
                mine = jnp.where(spare & (spot == lane), value, mine)
            r_out[e] = mine.astype(bf16)

    hbm, vmem = pl.BlockSpec(memory_space=pltpu.HBM), pl.BlockSpec(memory_space=pltpu.VMEM)
    shape = (count, sz.height, sz.width)

    def call(*sources):
        template, _, _, _, inter, offs, index, coef, basis = sources
        return pl.pallas_call(
            body,
            in_specs=[hbm] * 9,
            out_specs=(vmem,) * 5,
            out_shape=(
                jax.ShapeDtypeStruct((count, sz.r_rows, CHUNK), bf16),
                jax.ShapeDtypeStruct((count, sz.sw_rows, sz.width), bf16),
                jax.ShapeDtypeStruct(template.shape, bf16),
                jax.ShapeDtypeStruct(shape, f32),
                jax.ShapeDtypeStruct(shape, f32),
            ),
            scratch_shapes=[
                pltpu.VMEM(shape, f32),
                pltpu.VMEM(shape, jnp.int32),
                pltpu.SMEM(inter.shape, jnp.int32),
                pltpu.VMEM(offs.shape, jnp.int32),
                pltpu.VMEM(index.shape, jnp.int32),
                pltpu.VMEM(coef.shape, f32),
                pltpu.VMEM(basis.shape, f32),
                pltpu.VMEM(((KS + 1) * FINE, nbasis), f32),
                pltpu.VMEM(((KS + 1) * FINE, width), bf16),
                pltpu.SemaphoreType.DMA((9,)),
            ],
            compiler_params=pltpu.CompilerParams(vmem_limit_bytes=VMEM_LIMIT),
            cost_estimate=pl.CostEstimate(
                flops=1_000_000_000, bytes_accessed=6_000_000, transcendentals=0
            ),
            name="prepare",
        )(*[pltpu.with_memory_space_constraint(source, pltpu.HBM) for source in sources])

    return call


def here(axis):
    return lax.axis_index(axis), lax.axis_size(axis)


def partner(me, n, k, back):
    if n & (n - 1) == 0:
        return me ^ k
    return (me + (n - k if back else k)) % n


def pack(sz, n_epoch, tiles, count, peers):
    per_owner = count // n_epoch
    h, w = sz.height, sz.width

    def body(own, low, high, left, low_left, high_left, right, low_right, high_right, sw, r, *outs):
        slabs, sends = outs[0], outs[1:]
        me, _ = here("epoch")
        strip, strips = here("strip")
        band, bands = here("band")

        def column(middle, above, below, t, cut):
            above = jnp.where(strip > 0, above[t, h - 16 :, cut].astype(f32), 0.0)
            above = jnp.where(iota(above.shape, 0) >= 16 - REACH, above, 0.0)
            below = jnp.where(strip < strips - 1, below[t, :16, cut].astype(f32), 0.0)
            below = jnp.where(iota(below.shape, 0) < REACH, below, 0.0)
            parts = [middle[t, :, cut].astype(f32), below]
            gap = sz.rows - h - 32
            if gap:
                parts.append(jnp.zeros((gap, below.shape[1]), f32))
            return jnp.concatenate(parts + [above], axis=0)

        for t in range(tiles):
            slabs[t, :, :w] = column(own, low, high, t, slice(None)).astype(bf16)
            before = column(left, low_left, high_left, t, slice(w - 128, w))
            after = column(right, low_right, high_right, t, slice(0, 128))
            lane = iota(before.shape, 1)
            before = jnp.where((lane >= 128 - REACH) & (band > 0), before, 0.0)
            after = jnp.where((lane < REACH) & (band < bands - 1), after, 0.0)
            if sz.lanes - w == 128:
                slabs[t, :, w:] = (before + after).astype(bf16)
            else:
                slabs[t, :, w : w + 128] = after.astype(bf16)
                slabs[t, :, sz.lanes - 128 :] = before.astype(bf16)
        for k, out in zip(peers, sends):
            q = partner(me, n_epoch, k, False)
            for c in range(per_owner):
                mine = q * per_owner + c
                lines = r[mine].astype(f32)
                tile = lines[NPOLY, 2].astype(jnp.int32)
                slab = slabs[tile].astype(f32)
                if sz.one_side:
                    side = jnp.where(strip == 0, slab[h : h + 16], slab[sz.rows - 16 :])
                    slab = jnp.concatenate([slab[:h], side], axis=0)
                halo = pltpu.roll(slab[:, sz.lanes - 128 :], REACH, 1)
                if sz.lanes - w != 128:
                    halo = halo + pltpu.roll(slab[:, w : w + 128], REACH, 1)
                halo = jnp.where(iota(halo.shape, 1) < 32, halo, 0.0)
                bits = []
                for part in range(sz.halo_rows // 8 * (w // 128)):
                    piece = jnp.zeros((8, 128), f32)
                    for slot in range(4):
                        g = part * 4 + slot
                        if g < sz.groups:
                            piece = piece + pltpu.roll(halo[g * 8 : g * 8 + 8], slot * 32, 1)
                    bits.append(piece)
                wide = w // 128
                bits = [
                    jnp.concatenate(bits[i * wide : (i + 1) * wide], axis=1)
                    for i in range(sz.halo_rows // 8)
                ]
                parts = [sw[mine].astype(f32), lines, slab[:, :w]] + bits
                out[c] = jnp.concatenate(parts, axis=0).astype(bf16)

    vmem = pl.BlockSpec(memory_space=pltpu.VMEM)
    return pl.pallas_call(
        body,
        in_specs=[vmem] * 11,
        out_shape=(jax.ShapeDtypeStruct((tiles, sz.rows, sz.lanes), bf16),)
        + tuple(jax.ShapeDtypeStruct((per_owner, sz.total, w), bf16) for _ in peers),
        compiler_params=pltpu.CompilerParams(vmem_limit_bytes=VMEM_LIMIT),
        cost_estimate=pl.CostEstimate(flops=1_000_000, bytes_accessed=1_000_000, transcendentals=0),
        name="pack",
    )


def models(sz, n_epoch, tiles, count, ks, first, last, carried):
    per_owner = count // n_epoch
    h, w = sz.height, sz.width
    total_models = (2 * len(ks) + first) * per_owner

    def body(sci, weight, r, slabs, *refs):
        refs = list(refs)
        pays = [refs.pop(0) for _ in ks]
        before = [] if first else [refs.pop(0) for _ in range(2)]
        done = [refs.pop(0) for _ in carried]
        if last:
            resid_out, coadd_out = refs.pop(0), refs.pop(0)
        else:
            numer_out, denom_out = refs.pop(0), refs.pop(0)
            resid_outs = [refs.pop(0) for _ in range(len(ks) + first)]
        rhs, lhs, *refs = refs
        me, _ = here("epoch")
        strip, strips = here("strip")
        band, bands = here("band")

        copies = []

        def send(source, target):
            copies.append(pltpu.make_async_copy(source, target, out_sems.at[len(copies)]))
            copies[-1].start()

        if last:
            fresh, sums, out_sems = refs
            for k, value in zip(carried, done):
                q = me if k == 0 else partner(me, n_epoch, k, True)
                send(value, resid_out.at[pl.ds(q * per_owner, per_owner)])

        jobs = []

        def job(kind, q, c, slab, lines):
            mine = q * per_owner + c
            own = lines if kind == "local" else r[mine].astype(f32)
            scalars = [lines[NPOLY, lane].astype(jnp.int32) for lane in range(2)]
            tile = None if kind == "sent" else own[NPOLY, 2].astype(jnp.int32)
            jobs.append((kind, mine, slab, lines, scalars, tile, own))

        if first:
            for c in range(per_owner):
                job("local", me, c, None, r[me * per_owner + c].astype(f32))
        for k, pay in zip(ks, pays):
            q = partner(me, n_epoch, k, True)
            for c in range(per_owner):
                got = pay[c].astype(f32)
                job("owned", q, c, got, got[sz.sw_rows : sz.main_at])
            for c in range(per_owner):
                job("sent", q, c, pay[c].astype(f32), r[q * per_owner + c].astype(f32))

        row = (strip * h + iota((h, 128), 0)).astype(f32)
        r_unit = (2.0 * row + 1.0) / (h * strips) - 1.0
        r_unit = jnp.concatenate([r_unit] * (sz.lanes // 128), axis=1)
        spot = iota((SLOT, CHUNK), 1)
        filled = (spot % sz.span < FINE) & (spot < sz.per * sz.span)
        c_units = []
        for i in range(sz.chunks):
            col = (band * w + iota((8, sz.lanes), 1) - i).astype(f32)
            col = (2.0 * col + 1.0) / (w * bands) - 1.0
            c_units.append(jnp.concatenate([col] * (h // 8), axis=0))
        for slot in range(2):
            used = sz.per * sz.span
            if used < CHUNK:
                rhs[slot, used:] = jnp.zeros((CHUNK - used, sz.lanes), bf16)

        def windows(turn, slab, scalars):
            window = rhs.at[turn % 2]
            down, across = scalars
            slab = pltpu.roll(slab, lax.rem(sz.rows + HALF - down, sz.rows), 0)[: sz.span]
            slab = pltpu.roll(slab.astype(bf16), lax.rem(sz.lanes + HALF - across, sz.lanes), 1)
            for slot in range(sz.per):
                moved = pltpu.roll(slab, sz.lanes - slot * sz.chunks, 1) if slot else slab
                window[slot * sz.span : (slot + 1) * sz.span] = moved

        def band_matrix(turn, lines):
            band_rows = lhs.at[turn % 2]
            for i in range(sz.chunks):
                line, phase = divmod(i, sz.phases)
                part = lines[line * SLOT : (line + 1) * SLOT]
                if phase:
                    part = pltpu.roll(part, CHUNK - phase * FINE, 1)
                part = jnp.where(filled, part, 0.0)
                at = i * NPOLY * h
                for p in range(NPOLY):
                    band_rows[at + p * h : at + (p + 1) * h] = pltpu.roll(
                        jnp.broadcast_to(part[p : p + 1], (h, CHUNK)), 0, 1, stride=1, stride_axis=0
                    )

        def chunk_image(turn, i):
            at = i * NPOLY * h
            conv = jnp.dot(
                lhs[turn % 2, at : at + NPOLY * h].astype(bf16), rhs[turn % 2], preferred_element_type=f32
            )
            conv = [conv[p * h : (p + 1) * h] for p in range(NPOLY)]
            c_unit = c_units[i]
            return (
                conv[0]
                + r_unit * (conv[1] + r_unit * conv[3] + c_unit * conv[4])
                + c_unit * (conv[2] + c_unit * conv[5])
            )

        def sent_slab(got):
            main, halo = got[sz.main_at : sz.halo_at], got[sz.halo_at :]
            wide = w // 128
            bits = []
            for g in range(sz.groups):
                part, slot = g // 4, g % 4
                line, side = part // wide, part % wide
                piece = halo[line * 8 : line * 8 + 8, side * 128 : side * 128 + 128]
                bits.append(pltpu.roll(piece, (128 - slot * 32) % 128, 1))
            halo = jnp.concatenate(bits, axis=0)
            lane = iota(halo.shape, 1)
            halo = pltpu.roll(jnp.where(lane < 2 * REACH, halo, 0.0), 128 - REACH, 1)
            if sz.lanes - w != 128:
                gap = sz.lanes - w - 256
                pieces = [jnp.where(lane < 64, halo, 0.0)]
                if gap:
                    pieces.append(jnp.zeros((sz.sent, gap), f32))
                halo = jnp.concatenate(pieces + [jnp.where(lane < 64, 0.0, halo)], axis=1)
            slab = jnp.concatenate([main, halo], axis=1)
            if sz.one_side:
                side, none = slab[h:], jnp.zeros((sz.rows - h - 32, sz.lanes), f32)
                below, above = jnp.where(strip == 0, side, 0.0), jnp.where(strip == 0, 0.0, side)
                slab = [slab[:h], below, none, above] if none.size else [slab[:h], below, above]
                slab = jnp.concatenate(slab, axis=0)
            return slab

        numer = [before[0][t] if before else jnp.zeros((h, w), f32) for t in range(tiles)]
        denom = [before[1][t] if before else jnp.zeros((h, w), f32) for t in range(tiles)]
        kept = 0
        settled = max(turn for turn, job in enumerate(jobs) if job[0] != "sent")
        images = []
        for turn in range(0, len(jobs), 2):
            pair = list(enumerate(jobs))[turn : turn + 2]
            for at, (kind, mine, got, lines, scalars, tile, own) in pair:
                band_matrix(at, lines)
            for at, (kind, mine, got, lines, scalars, tile, own) in pair:
                windows(at, sent_slab(got) if kind == "sent" else slabs[tile].astype(f32), scalars)
            parts = [None for _ in pair]
            for i in reversed(range(sz.chunks)):
                for slot, (at, _) in enumerate(pair):
                    value = chunk_image(at, i)
                    value = pltpu.roll(value, sz.lanes - i, 1) if i else value
                    parts[slot] = value if parts[slot] is None else parts[slot] + value
            images += [part[:, :w] for part in parts]
        for turn, (kind, mine, got, lines, scalars, tile, own) in enumerate(jobs):
            image = images[turn]
            if kind == "owned":
                scale = jnp.broadcast_to(lines[NPOLY : NPOLY + 1, 3:4], (h, w))
                science, seen = decode_science(got[:h]) * scale, decode_weight(got[h : 2 * h])
            else:
                science, seen = sci[mine], weight[mine]
                if last:
                    fresh[kept] = science - image
                    send(fresh.at[kept], resid_out.at[mine])
                else:
                    resid_outs[kept // per_owner][kept % per_owner] = science - image
                kept += 1
            if kind != "sent":
                change = seen * (science - image)
                covered = jnp.broadcast_to(own[NPOLY : NPOLY + 1, 2:3], (h, w))
                for t in range(tiles):
                    numer[t] = numer[t] + jnp.where(covered == t, change, 0.0)
                    denom[t] = denom[t] + jnp.where(covered == t, seen, 0.0)
            if turn == settled:
                for t in range(tiles):
                    if last:
                        sums[t] = numer[t] / (denom[t] + 1.0)
                    else:
                        numer_out[t], denom_out[t] = numer[t], denom[t]
                if last:
                    send(sums, coadd_out)
        for copy in copies:
            copy.wait()

    image = jax.ShapeDtypeStruct((per_owner, h, w), f32)
    sums = jax.ShapeDtypeStruct((tiles, h, w), f32)
    if last:
        out_shape = (jax.ShapeDtypeStruct((count, h, w), f32), sums)
    else:
        out_shape = (sums, sums) + (image,) * (len(ks) + first)
    vmem, hbm = pl.BlockSpec(memory_space=pltpu.VMEM), pl.BlockSpec(memory_space=pltpu.HBM)
    scratch = [
        pltpu.VMEM((2, CHUNK, sz.lanes), bf16),
        pltpu.VMEM((2, sz.chunks * NPOLY * h, CHUNK), f32),
    ]
    if last:
        new = len(ks) * per_owner
        scratch += [
            pltpu.VMEM((new, h, w), f32),
            pltpu.VMEM((tiles, h, w), f32),
            pltpu.SemaphoreType.DMA((len(carried) + new + 1,)),
        ]
    return pl.pallas_call(
        body,
        in_specs=[vmem] * (4 + len(ks) + (0 if first else 2) + len(carried)),
        out_specs=(hbm if last else vmem,) * len(out_shape),
        out_shape=out_shape,
        scratch_shapes=scratch,
        compiler_params=pltpu.CompilerParams(vmem_limit_bytes=VMEM_LIMIT),
        cost_estimate=pl.CostEstimate(
            flops=total_models * 400_000_000, bytes_accessed=1_000_000, transcendentals=0
        ),
        name="models",
    )


def surroundings(block):
    strips, bands = lax.axis_size("strip"), lax.axis_size("band")
    sent, found = {}, {}
    for down in (-1, 0, 1):
        for across in (-1, 0, 1):
            if down == 0 and across == 0:
                continue
            pairs = []
            for s in range(strips):
                for b in range(bands):
                    to_s = s ^ 1 if strips == 2 and down else s - down
                    to_b = b ^ 1 if bands == 2 and across else b - across
                    if 0 <= to_s < strips and 0 <= to_b < bands:
                        pairs.append((s * bands + b, to_s * bands + to_b))
            key = tuple(pairs)
            if key and key not in sent:
                sent[key] = lax.ppermute(block, ("strip", "band"), pairs)
            found[down, across] = key
    return {step: sent.get(key, block) for step, key in found.items()}


def local(
    template, science, variance, bad_mask, intersection, offsets, basis_index, coefficients, basis
):
    n_epoch = lax.axis_size("epoch")
    tiles = template.shape[0]
    count, height, width = science.shape
    sz = Sizes(height, width, lax.axis_size("strip"))
    around = surroundings(template)
    r, sw, own, sci, weight = prepare(sz, n_epoch, tiles, count, basis_index.shape[1])(
        template,
        science,
        variance,
        bad_mask,
        intersection,
        offsets.T,
        basis_index,
        coefficients.transpose(2, 0, 1),
        basis.transpose(1, 2, 0),
    )
    around[0, 0] = own
    peers = list(range(1, n_epoch))
    order = peers[-1:] + peers[:-1]
    slabs, *sends = pack(sz, n_epoch, tiles, count, peers)(
        *[around[down, across] for across in (0, -1, 1) for down in (0, -1, 1)], sw, r
    )
    pays = {}
    for k, send in zip(order, [sends[peers.index(k)] for k in order]):
        pairs = [(i, partner(i, n_epoch, k, False)) for i in range(n_epoch)]
        pays[k] = lax.ppermute(send, "epoch", pairs)
    stages = [[]] + [[k] for k in order]
    sums, carried = [], []
    for i, ks in enumerate(stages):
        first, last = i == 0, i == len(stages) - 1
        kept = [k for k, _ in carried] if last else []
        out = models(sz, n_epoch, tiles, count, ks, first, last, kept)(
            sci,
            weight,
            r,
            slabs,
            *[pays[k] for k in ks],
            *sums,
            *([value for _, value in carried] if last else []),
        )
        if last:
            return out
        sums = list(out[:2])
        carried += list(zip(list(ks) + ([0] if first else []), out[2:]))


def solution(mesh):
    in_specs = (
        P(("groups", "epoch"), "strip", "band"),
        P(("groups", "epoch"), "strip", "band"),
        P(("groups", "epoch"), "strip", "band"),
        P(("groups", "epoch"), "strip", "band"),
        P("groups"),
        P(("groups", "epoch"), None),
        P(("groups", "epoch"), None),
        P(("groups", "epoch"), None, None),
        P(),
    )
    out_specs = (P(("groups", "epoch"), "strip", "band"), P(("groups", "epoch"), "strip", "band"))
    return jax.shard_map(local, mesh=mesh, in_specs=in_specs, out_specs=out_specs, check_vma=False)
```

```python
import jax
import jax.numpy as jnp
from jax import lax
from jax.experimental import pallas as pl
from jax.experimental.pallas import tpu as pltpu
from jax.sharding import PartitionSpec as P

KS = 19
HALF = 9
SHIFT = 4
NPOLY = 6
REACH = HALF + SHIFT
SLOT = 8
CHUNK = 256
FINE = 24
VMEM_LIMIT = 24 * 1024 * 1024

highest = lax.Precision.HIGHEST
f32 = jnp.float32
bf16 = jnp.bfloat16


def up(value, step):
    return -(-value // step) * step


class Sizes:
    def __init__(self, height, width, strips):
        self.height, self.width = height, width
        self.rows = up(height + 2 * REACH, 8)
        self.lanes = up(width + 2 * REACH, 128)
        self.span = up(height + KS - 1, 2 * FINE)
        self.phases = self.span // FINE
        self.per = CHUNK // self.span
        self.lines = -(-KS // (self.per * self.phases))
        self.depth = self.lines * CHUNK
        self.sw_rows = 2 * height
        self.r_rows = self.lines * SLOT
        self.one_side = strips <= 2
        self.sent = height + 16 if self.one_side else self.rows
        self.main_at = self.sw_rows + self.r_rows
        self.halo_at = self.main_at + self.sent
        self.groups = self.sent // 8
        self.halo_rows = up(self.groups * 32, width) // width * 8
        self.total = self.halo_at + self.halo_rows

    def place(self, column):
        slot, phase = column // self.phases, column % self.phases
        return slot // self.per * CHUNK + (slot % self.per * self.phases + phase) * FINE


def iota(shape, axis):
    return lax.broadcasted_iota(jnp.int32, shape, axis)


def whole(value):
    return jnp.floor(value + 0.5)


def exponent_of(value):
    return jnp.floor(jnp.log2(value))


def join(mantissa, exponent):
    return (1.0 + mantissa * 2.0**-7) * jnp.exp2(exponent)


def part(value):
    exponent = jnp.floor(jnp.log2(value) + 0.003)
    return whole((value * jnp.exp2(-exponent) - 1.0) * 128.0), exponent


def encode_weight(weight):
    code = jnp.minimum(whole(weight * 65536.0), 32767.0)
    half = jnp.floor(code * 0.5)
    exponent = jnp.floor(half * 2.0**-7)
    value = join(half - exponent * 128.0, exponent - 63.0)
    return jnp.where(code > 2.0 * half, -value, value)


def decode_weight(value):
    mantissa, exponent = part(jnp.abs(value))
    code = (exponent + 63.0) * 256.0 + mantissa * 2.0
    return jnp.where(value < 0.0, code + 1.0, code) * 2.0**-16


def encode_science(science):
    size = jnp.abs(science)
    power = jnp.clip(exponent_of(jnp.maximum(size, 2.0**-30)), -24.0, 2.0)
    fine = power >= -12.0
    steps = jnp.where(fine, 2048.0, 128.0)
    code = jnp.clip(whole((size * jnp.exp2(-power) - 1.0) * steps), 0.0, steps - 1.0)
    high = jnp.floor(code * 0.0625)
    exponent = jnp.where(fine, power * 16.0 + (code - 16.0 * high) + 192.0, power + 264.0)
    value = join(jnp.where(fine, high, code), exponent - 125.0)
    value = jnp.where(size < 2.0**-24, 0.0, value)
    return jnp.where(science < 0.0, -value, value)


def decode_science(value):
    size = jnp.abs(value)
    mantissa, exponent = part(jnp.maximum(size, 2.0**-125))
    exponent = exponent + 125.0
    high = jnp.floor(exponent * 0.0625)
    fine = exponent < 240.0
    low = jnp.where(fine, exponent - 16.0 * high, 0.0)
    power = jnp.where(fine, high - 12.0, exponent - 264.0)
    size = jnp.where(size == 0.0, 0.0, (2048.0 + mantissa * 16.0 + low) * 2.0**-11 * jnp.exp2(power))
    return jnp.where(value < 0.0, -size, size)


def prepare(sz, n_epoch, tiles, count, nsel):
    lanes = count * SLOT
    per_owner = count // n_epoch
    width = sz.lines * CHUNK
    nbasis = 128

    def body(*refs):
        sources, refs = refs[:9], refs[9:]
        r_out, sw_out, own_out, sci_out, weight_out = refs[:5]
        var, mask, inter, offs, index, coef, basis, table, place, sems = refs[5:]
        targets = [own_out, sci_out, var, mask, inter, offs, index, coef, basis]
        copies = [
            pltpu.make_async_copy(source, target, sems.at[i])
            for i, (source, target) in enumerate(zip(sources, targets))
        ]
        for copy in reversed(copies):
            copy.start()
        me, _ = here("epoch")
        table[...] = jnp.zeros(table.shape, f32)
        col = iota((FINE, width), 0)
        base = iota((FINE, width), 1) - sz.place(col)
        base = jnp.where(col < KS, base, -1)
        for a in range(0, KS + 1, 2):
            pair = jnp.concatenate([(base == a).astype(f32), (base == a + 1).astype(f32)], axis=0)
            if a + 1 == KS:
                pair = jnp.where(iota(pair.shape, 0) < FINE, pair, 0.0)
            place[a * FINE : (a + 2) * FINE] = pair.astype(bf16)
        for copy in reversed(copies[4:]):
            copy.wait()
        for a in range(KS):
            table[a * FINE : a * FINE + KS, : basis.shape[2]] = basis[a]
        chosen = jnp.concatenate([index[e : e + 1, :] for e in range(count)], axis=1)
        onehot = (iota((nbasis, count * nsel), 0) == chosen).astype(f32)
        blocks = []
        for e in range(count):
            mine = jnp.concatenate([coef[:, e, :], jnp.zeros((SLOT - NPOLY, nsel), f32)], axis=0)
            wide = jnp.concatenate([mine] * count, axis=1)
            blocks.append(jnp.where(iota(wide.shape, 1) // nsel == e, wide, 0.0))
        combine = jnp.concatenate(blocks, axis=0)
        mixing = lax.dot_general(
            onehot, combine, (((1,), (1,)), ((), ())), precision=highest, preferred_element_type=f32
        )
        images = jnp.dot(table[...], mixing, precision=highest, preferred_element_type=f32)
        rows = lax.dot_general(
            images.astype(bf16), place[...], (((0,), (0,)), ((), ())), preferred_element_type=f32
        )
        for copy in reversed(copies[:4]):
            copy.wait()
        for e in range(count):
            weight_out[e] = mask[e].astype(f32) / var[e]
            science = jnp.where(mask[e] == 0, 0.0, sci_out[e])
            top = jnp.max(jnp.abs(science), axis=(0, 1), keepdims=True)
            scale = jnp.exp2(exponent_of(jnp.maximum(top, 2.0**-100)) - 2.0).astype(bf16).astype(f32)
            science = science / scale
            parts = [encode_science(science), encode_weight(weight_out[e])]
            sw_out[e] = jnp.concatenate(parts, axis=0).astype(bf16)
            mine = rows[e * SLOT : (e + 1) * SLOT]
            mine = jnp.concatenate(
                [mine[:, i * CHUNK : (i + 1) * CHUNK] for i in range(sz.lines)], axis=0
            )
            tile = inter[e // per_owner * count + me * per_owner + e % per_owner] - me * tiles
            tile = jnp.clip(tile, 0, tiles - 1).astype(f32)
            down, across = offs[0:1, e : e + 1].astype(f32), offs[1:2, e : e + 1].astype(f32)
            spare, spot = iota(mine.shape, 0) == NPOLY, iota(mine.shape, 1)
            for lane, value in enumerate((down, across, tile, scale)):
                mine = jnp.where(spare & (spot == lane), value, mine)
            r_out[e] = mine.astype(bf16)

    hbm, vmem = pl.BlockSpec(memory_space=pltpu.HBM), pl.BlockSpec(memory_space=pltpu.VMEM)
    shape = (count, sz.height, sz.width)

    def call(*sources):
        template, _, _, _, inter, offs, index, coef, basis = sources
        return pl.pallas_call(
            body,
            in_specs=[hbm] * 9,
            out_specs=(vmem,) * 5,
            out_shape=(
                jax.ShapeDtypeStruct((count, sz.r_rows, CHUNK), bf16),
                jax.ShapeDtypeStruct((count, sz.sw_rows, sz.width), bf16),
                jax.ShapeDtypeStruct(template.shape, bf16),
                jax.ShapeDtypeStruct(shape, f32),
                jax.ShapeDtypeStruct(shape, f32),
            ),
            scratch_shapes=[
                pltpu.VMEM(shape, f32),
                pltpu.VMEM(shape, jnp.int32),
                pltpu.SMEM(inter.shape, jnp.int32),
                pltpu.VMEM(offs.shape, jnp.int32),
                pltpu.VMEM(index.shape, jnp.int32),
                pltpu.VMEM(coef.shape, f32),
                pltpu.VMEM(basis.shape, f32),
                pltpu.VMEM(((KS + 1) * FINE, nbasis), f32),
                pltpu.VMEM(((KS + 1) * FINE, width), bf16),
                pltpu.SemaphoreType.DMA((9,)),
            ],
            compiler_params=pltpu.CompilerParams(vmem_limit_bytes=VMEM_LIMIT),
            cost_estimate=pl.CostEstimate(
                flops=1_000_000_000, bytes_accessed=6_000_000, transcendentals=0
            ),
            name="prepare",
        )(*[pltpu.with_memory_space_constraint(source, pltpu.HBM) for source in sources])

    return call


def here(axis):
    return lax.axis_index(axis), lax.axis_size(axis)


def partner(me, n, k, back):
    if n & (n - 1) == 0:
        return me ^ k
    return (me + (n - k if back else k)) % n


def pack(sz, n_epoch, tiles, count, peers):
    per_owner = count // n_epoch
    h, w = sz.height, sz.width

    def body(own, low, high, left, low_left, high_left, right, low_right, high_right, sw, r, *outs):
        slabs, sends = outs[0], outs[1:]
        me, _ = here("epoch")
        strip, strips = here("strip")
        band, bands = here("band")

        def column(middle, above, below, t, cut):
            above = jnp.where(strip > 0, above[t, h - 16 :, cut].astype(f32), 0.0)
            above = jnp.where(iota(above.shape, 0) >= 16 - REACH, above, 0.0)
            below = jnp.where(strip < strips - 1, below[t, :16, cut].astype(f32), 0.0)
            below = jnp.where(iota(below.shape, 0) < REACH, below, 0.0)
            parts = [middle[t, :, cut].astype(f32), below]
            gap = sz.rows - h - 32
            if gap:
                parts.append(jnp.zeros((gap, below.shape[1]), f32))
            return jnp.concatenate(parts + [above], axis=0)

        for t in range(tiles):
            slabs[t, :, :w] = column(own, low, high, t, slice(None)).astype(bf16)
            before = column(left, low_left, high_left, t, slice(w - 128, w))
            after = column(right, low_right, high_right, t, slice(0, 128))
            lane = iota(before.shape, 1)
            before = jnp.where((lane >= 128 - REACH) & (band > 0), before, 0.0)
            after = jnp.where((lane < REACH) & (band < bands - 1), after, 0.0)
            if sz.lanes - w == 128:
                slabs[t, :, w:] = (before + after).astype(bf16)
            else:
                slabs[t, :, w : w + 128] = after.astype(bf16)
                slabs[t, :, sz.lanes - 128 :] = before.astype(bf16)
        for k, out in zip(peers, sends):
            q = partner(me, n_epoch, k, False)
            for c in range(per_owner):
                mine = q * per_owner + c
                lines = r[mine].astype(f32)
                tile = lines[NPOLY, 2].astype(jnp.int32)
                slab = slabs[tile].astype(f32)
                if sz.one_side:
                    side = jnp.where(strip == 0, slab[h : h + 16], slab[sz.rows - 16 :])
                    slab = jnp.concatenate([slab[:h], side], axis=0)
                halo = pltpu.roll(slab[:, sz.lanes - 128 :], REACH, 1)
                if sz.lanes - w != 128:
                    halo = halo + pltpu.roll(slab[:, w : w + 128], REACH, 1)
                halo = jnp.where(iota(halo.shape, 1) < 32, halo, 0.0)
                bits = []
                for part in range(sz.halo_rows // 8 * (w // 128)):
                    piece = jnp.zeros((8, 128), f32)
                    for slot in range(4):
                        g = part * 4 + slot
                        if g < sz.groups:
                            piece = piece + pltpu.roll(halo[g * 8 : g * 8 + 8], slot * 32, 1)
                    bits.append(piece)
                wide = w // 128
                bits = [
                    jnp.concatenate(bits[i * wide : (i + 1) * wide], axis=1)
                    for i in range(sz.halo_rows // 8)
                ]
                parts = [sw[mine].astype(f32), lines, slab[:, :w]] + bits
                out[c] = jnp.concatenate(parts, axis=0).astype(bf16)

    vmem = pl.BlockSpec(memory_space=pltpu.VMEM)
    return pl.pallas_call(
        body,
        in_specs=[vmem] * 11,
        out_shape=(jax.ShapeDtypeStruct((tiles, sz.rows, sz.lanes), bf16),)
        + tuple(jax.ShapeDtypeStruct((per_owner, sz.total, w), bf16) for _ in peers),
        compiler_params=pltpu.CompilerParams(vmem_limit_bytes=VMEM_LIMIT),
        cost_estimate=pl.CostEstimate(flops=1_000_000, bytes_accessed=1_000_000, transcendentals=0),
        name="pack",
    )


def models(sz, n_epoch, tiles, count, ks, first, last, carried):
    per_owner = count // n_epoch
    h, w = sz.height, sz.width
    total_models = (2 * len(ks) + first) * per_owner

    def body(sci, weight, r, slabs, *refs):
        refs = list(refs)
        ready = None if first else refs.pop(0)
        pays = [refs.pop(0) for _ in ks]
        before = [] if first else [refs.pop(0) for _ in range(2)]
        done = [refs.pop(0) for _ in carried]
        if last:
            resid_out, coadd_out = refs.pop(0), refs.pop(0)
        else:
            numer_out, denom_out = refs.pop(0), refs.pop(0)
            resid_outs = [refs.pop(0) for _ in range(len(ks) + first)]
            ready_out = refs.pop(0) if first else None
        rhs, lhs, *refs = refs
        me, _ = here("epoch")
        strip, strips = here("strip")
        band, bands = here("band")

        copies = []

        def send(source, target):
            copies.append(pltpu.make_async_copy(source, target, out_sems.at[len(copies)]))
            copies[-1].start()

        if last:
            fresh, sums, out_sems = refs
            for k, value in zip(carried, done):
                q = me if k == 0 else partner(me, n_epoch, k, True)
                send(value, resid_out.at[pl.ds(q * per_owner, per_owner)])

        jobs = []

        def job(kind, q, c, slab, lines):
            mine = q * per_owner + c
            own = lines if kind == "local" else r[mine].astype(f32)
            scalars = [lines[NPOLY, lane].astype(jnp.int32) for lane in range(2)]
            tile = None if kind == "sent" else own[NPOLY, 2].astype(jnp.int32)
            jobs.append((kind, mine, slab, lines, scalars, tile, own))

        if first:
            for c in range(per_owner):
                job("local", me, c, None, r[me * per_owner + c].astype(f32))
        for k, pay in zip(ks, pays):
            q = partner(me, n_epoch, k, True)
            for c in range(per_owner):
                got = pay[c].astype(f32)
                job("owned", q, c, got, got[sz.sw_rows : sz.main_at])
            for c in range(per_owner):
                job("sent", q, c, pay[c].astype(f32), r[q * per_owner + c].astype(f32))

        row = (strip * h + iota((h, 128), 0)).astype(f32)
        r_unit = (2.0 * row + 1.0) / (h * strips) - 1.0
        r_unit = jnp.concatenate([r_unit] * (sz.lanes // 128), axis=1)
        spot = iota((SLOT, CHUNK), 1)
        filled = (spot % sz.span < FINE) & (spot < sz.per * sz.span)
        c_units = []
        for i in range(sz.phases):
            col = (band * w + iota((8, sz.lanes), 1) - i).astype(f32)
            col = (2.0 * col + 1.0) / (w * bands) - 1.0
            c_units.append(jnp.concatenate([col] * (h // 8), axis=0))
        for slot in range(2):
            for line in range(sz.lines):
                at = line * CHUNK + sz.per * sz.span
                if at < (line + 1) * CHUNK:
                    rhs[slot, at : (line + 1) * CHUNK] = jnp.zeros(((line + 1) * CHUNK - at, sz.lanes), bf16)

        def windows(turn, slab, scalars):
            window = rhs.at[turn % 2]
            down, across = scalars
            slab = pltpu.roll(slab, lax.rem(sz.rows + HALF - down, sz.rows), 0)[: sz.span]
            slab = pltpu.roll(slab.astype(bf16), lax.rem(sz.lanes + HALF - across, sz.lanes), 1)
            for slot in range(sz.lines * sz.per):
                moved = pltpu.roll(slab, sz.lanes - slot * sz.phases, 1) if slot else slab
                at = slot // sz.per * CHUNK + slot % sz.per * sz.span
                window[at : at + sz.span] = moved

        def band_matrix(turn, lines):
            band_rows = lhs.at[turn % 2]
            for i in range(sz.phases * sz.lines):
                phase, line = divmod(i, sz.lines)
                part = lines[line * SLOT : (line + 1) * SLOT]
                if phase:
                    part = pltpu.roll(part, CHUNK - phase * FINE, 1)
                part = jnp.where(filled, part, 0.0)
                for p in range(NPOLY):
                    at = (phase * NPOLY + p) * h
                    band_rows[at : at + h, line * CHUNK : (line + 1) * CHUNK] = pltpu.roll(
                        jnp.broadcast_to(part[p : p + 1], (h, CHUNK)), 0, 1, stride=1, stride_axis=0
                    )

        def chunk_image(turn, i, matrix):
            at = i * NPOLY * h
            conv = jnp.dot(
                matrix[at : at + NPOLY * h].astype(bf16), rhs[turn % 2], preferred_element_type=f32
            )
            conv = [conv[p * h : (p + 1) * h] for p in range(NPOLY)]
            c_unit = c_units[i]
            return (
                conv[0]
                + r_unit * (conv[1] + r_unit * conv[3] + c_unit * conv[4])
                + c_unit * (conv[2] + c_unit * conv[5])
            )

        def sent_slab(got):
            main, halo = got[sz.main_at : sz.halo_at], got[sz.halo_at :]
            wide = w // 128
            bits = []
            for g in range(sz.groups):
                part, slot = g // 4, g % 4
                line, side = part // wide, part % wide
                piece = halo[line * 8 : line * 8 + 8, side * 128 : side * 128 + 128]
                bits.append(pltpu.roll(piece, (128 - slot * 32) % 128, 1))
            halo = jnp.concatenate(bits, axis=0)
            lane = iota(halo.shape, 1)
            halo = pltpu.roll(jnp.where(lane < 2 * REACH, halo, 0.0), 128 - REACH, 1)
            if sz.lanes - w != 128:
                gap = sz.lanes - w - 256
                pieces = [jnp.where(lane < 64, halo, 0.0)]
                if gap:
                    pieces.append(jnp.zeros((sz.sent, gap), f32))
                halo = jnp.concatenate(pieces + [jnp.where(lane < 64, 0.0, halo)], axis=1)
            slab = jnp.concatenate([main, halo], axis=1)
            if sz.one_side:
                side, none = slab[h:], jnp.zeros((sz.rows - h - 32, sz.lanes), f32)
                below, above = jnp.where(strip == 0, side, 0.0), jnp.where(strip == 0, 0.0, side)
                slab = [slab[:h], below, none, above] if none.size else [slab[:h], below, above]
                slab = jnp.concatenate(slab, axis=0)
            return slab

        numer = [before[0][t] if before else jnp.zeros((h, w), f32) for t in range(tiles)]
        denom = [before[1][t] if before else jnp.zeros((h, w), f32) for t in range(tiles)]
        kept = 0
        settled = max(turn for turn, job in enumerate(jobs) if job[0] != "sent")
        images = []
        for turn in range(0, len(jobs), 2):
            pair = list(enumerate(jobs))[turn : turn + 2]
            for at, (kind, mine, got, lines, scalars, tile, own) in pair:
                if kind != "sent":
                    band_matrix(at, lines)
            for at, (kind, mine, got, lines, scalars, tile, own) in pair:
                windows(at, sent_slab(got) if kind == "sent" else slabs[tile].astype(f32), scalars)
            parts = [None for _ in pair]
            for i in reversed(range(sz.phases)):
                for slot, (at, _) in enumerate(pair):
                    value = chunk_image(at, i, ready.at[pair[slot][1][1]] if pair[slot][1][0] == "sent" else lhs.at[at % 2])
                    value = pltpu.roll(value, sz.lanes - i, 1) if i else value
                    parts[slot] = value if parts[slot] is None else parts[slot] + value
            images += [part[:, :w] for part in parts]
        for turn, (kind, mine, got, lines, scalars, tile, own) in enumerate(jobs):
            image = images[turn]
            if kind == "owned":
                scale = jnp.broadcast_to(lines[NPOLY : NPOLY + 1, 3:4], (h, w))
                science, seen = decode_science(got[:h]) * scale, decode_weight(got[h : 2 * h])
            else:
                science, seen = sci[mine], weight[mine]
                if last:
                    fresh[kept] = science - image
                    send(fresh.at[kept], resid_out.at[mine])
                else:
                    resid_outs[kept // per_owner][kept % per_owner] = science - image
                kept += 1
            if kind != "sent":
                change = seen * (science - image)
                covered = jnp.broadcast_to(own[NPOLY : NPOLY + 1, 2:3], (h, w))
                for t in range(tiles):
                    numer[t] = numer[t] + jnp.where(covered == t, change, 0.0)
                    denom[t] = denom[t] + jnp.where(covered == t, seen, 0.0)
            if turn == settled:
                for t in range(tiles):
                    if last:
                        sums[t] = numer[t] / (denom[t] + 1.0)
                    else:
                        numer_out[t], denom_out[t] = numer[t], denom[t]
                if last:
                    send(sums, coadd_out)
        for copy in copies:
            copy.wait()
        if first:
            for e in range(count):
                band_matrix(0, r[e].astype(f32))
                ready_out[e] = lhs[0].astype(bf16)

    image = jax.ShapeDtypeStruct((per_owner, h, w), f32)
    sums = jax.ShapeDtypeStruct((tiles, h, w), f32)
    if last:
        out_shape = (jax.ShapeDtypeStruct((count, h, w), f32), sums)
    else:
        out_shape = (sums, sums) + (image,) * (len(ks) + first)
        if first:
            out_shape += (jax.ShapeDtypeStruct((count, sz.phases * NPOLY * h, sz.depth), bf16),)
    vmem, hbm = pl.BlockSpec(memory_space=pltpu.VMEM), pl.BlockSpec(memory_space=pltpu.HBM)
    scratch = [
        pltpu.VMEM((2, sz.depth, sz.lanes), bf16),
        pltpu.VMEM((2, sz.phases * NPOLY * h, sz.depth), f32),
    ]
    if last:
        new = len(ks) * per_owner
        scratch += [
            pltpu.VMEM((new, h, w), f32),
            pltpu.VMEM((tiles, h, w), f32),
            pltpu.SemaphoreType.DMA((len(carried) + new + 1,)),
        ]
    return pl.pallas_call(
        body,
        in_specs=[vmem] * (4 + len(ks) + (0 if first else 3) + len(carried)),
        out_specs=(hbm if last else vmem,) * len(out_shape),
        out_shape=out_shape,
        scratch_shapes=scratch,
        compiler_params=pltpu.CompilerParams(vmem_limit_bytes=VMEM_LIMIT),
        cost_estimate=pl.CostEstimate(
            flops=total_models * 400_000_000, bytes_accessed=1_000_000, transcendentals=0
        ),
        name="models",
    )


def surroundings(block):
    strips, bands = lax.axis_size("strip"), lax.axis_size("band")
    sent, found = {}, {}
    for down in (-1, 0, 1):
        for across in (-1, 0, 1):
            if down == 0 and across == 0:
                continue
            pairs = []
            for s in range(strips):
                for b in range(bands):
                    to_s = s ^ 1 if strips == 2 and down else s - down
                    to_b = b ^ 1 if bands == 2 and across else b - across
                    if 0 <= to_s < strips and 0 <= to_b < bands:
                        pairs.append((s * bands + b, to_s * bands + to_b))
            key = tuple(pairs)
            if key and key not in sent:
                sent[key] = lax.ppermute(block, ("strip", "band"), pairs)
            found[down, across] = key
    return {step: sent.get(key, block) for step, key in found.items()}


def local(
    template, science, variance, bad_mask, intersection, offsets, basis_index, coefficients, basis
):
    n_epoch = lax.axis_size("epoch")
    tiles = template.shape[0]
    count, height, width = science.shape
    sz = Sizes(height, width, lax.axis_size("strip"))
    around = surroundings(template)
    r, sw, own, sci, weight = prepare(sz, n_epoch, tiles, count, basis_index.shape[1])(
        template,
        science,
        variance,
        bad_mask,
        intersection,
        offsets.T,
        basis_index,
        coefficients.transpose(2, 0, 1),
        basis.transpose(1, 2, 0),
    )
    around[0, 0] = own
    peers = list(range(1, n_epoch))
    order = peers[-1:] + peers[:-1]
    slabs, *sends = pack(sz, n_epoch, tiles, count, peers)(
        *[around[down, across] for across in (0, -1, 1) for down in (0, -1, 1)], sw, r
    )
    pays = {}
    for k, send in zip(order, [sends[peers.index(k)] for k in order]):
        pairs = [(i, partner(i, n_epoch, k, False)) for i in range(n_epoch)]
        pays[k] = lax.ppermute(send, "epoch", pairs)
    stages = [[]] + [[k] for k in order]
    sums, carried, ready = [], [], []
    for i, ks in enumerate(stages):
        first, last = i == 0, i == len(stages) - 1
        kept = [k for k, _ in carried] if last else []
        out = models(sz, n_epoch, tiles, count, ks, first, last, kept)(
            sci,
            weight,
            r,
            slabs,
            *ready,
            *[pays[k] for k in ks],
            *sums,
            *([value for _, value in carried] if last else []),
        )
        if last:
            return out
        sums = list(out[:2])
        if first:
            *out, matrices = out
            ready = [matrices]
        carried += list(zip(list(ks) + ([0] if first else []), out[2:]))


def solution(mesh):
    in_specs = (
        P(("groups", "epoch"), "strip", "band"),
        P(("groups", "epoch"), "strip", "band"),
        P(("groups", "epoch"), "strip", "band"),
        P(("groups", "epoch"), "strip", "band"),
        P("groups"),
        P(("groups", "epoch"), None),
        P(("groups", "epoch"), None),
        P(("groups", "epoch"), None, None),
        P(),
    )
    out_specs = (P(("groups", "epoch"), "strip", "band"), P(("groups", "epoch"), "strip", "band"))
    return jax.shard_map(local, mesh=mesh, in_specs=in_specs, out_specs=out_specs, check_vma=False)
```

```python
import jax
import jax.numpy as jnp
from jax import lax
from jax.experimental import pallas as pl
from jax.experimental.pallas import tpu as pltpu
from jax.sharding import PartitionSpec as P

KS = 19
HALF = 9
SHIFT = 4
NPOLY = 6
REACH = HALF + SHIFT
SLOT = 8
CHUNK = 256
FINE = 24
VMEM_LIMIT = 24 * 1024 * 1024

highest = lax.Precision.HIGHEST
f32 = jnp.float32
bf16 = jnp.bfloat16


def up(value, step):
    return -(-value // step) * step


class Sizes:
    def __init__(self, height, width, strips):
        self.height, self.width = height, width
        self.rows = up(height + 2 * REACH, 8)
        self.lanes = up(width + 2 * REACH, 128)
        self.span = up(height + KS - 1, 2 * FINE)
        self.phases = self.span // FINE
        self.per = CHUNK // self.span
        self.lines = -(-KS // (self.per * self.phases))
        self.depth = self.lines * CHUNK
        self.sw_rows = 2 * height
        self.r_rows = self.lines * SLOT
        self.one_side = strips <= 2
        self.sent = height + 16 if self.one_side else self.rows
        self.main_at = self.sw_rows + self.r_rows
        self.halo_at = self.main_at + self.sent
        self.groups = self.sent // 8
        self.halo_rows = up(self.groups * 32, width) // width * 8
        self.total = self.halo_at + self.halo_rows

    def place(self, column):
        slot, phase = column // self.phases, column % self.phases
        return slot // self.per * CHUNK + (slot % self.per * self.phases + phase) * FINE


def iota(shape, axis):
    return lax.broadcasted_iota(jnp.int32, shape, axis)


def whole(value):
    return jnp.floor(value + 0.5)


def exponent_of(value):
    return jnp.floor(jnp.log2(value))


def join(mantissa, exponent):
    return (1.0 + mantissa * 2.0**-7) * jnp.exp2(exponent)


def part(value):
    exponent = jnp.floor(jnp.log2(value) + 0.003)
    return whole((value * jnp.exp2(-exponent) - 1.0) * 128.0), exponent


def encode_weight(weight):
    code = jnp.minimum(whole(weight * 65536.0), 32767.0)
    half = jnp.floor(code * 0.5)
    exponent = jnp.floor(half * 2.0**-7)
    value = join(half - exponent * 128.0, exponent - 63.0)
    return jnp.where(code > 2.0 * half, -value, value)


def decode_weight(value):
    mantissa, exponent = part(jnp.abs(value))
    code = (exponent + 63.0) * 256.0 + mantissa * 2.0
    return jnp.where(value < 0.0, code + 1.0, code) * 2.0**-16


def encode_science(science):
    size = jnp.abs(science)
    power = jnp.clip(exponent_of(jnp.maximum(size, 2.0**-30)), -24.0, 2.0)
    fine = power >= -12.0
    steps = jnp.where(fine, 2048.0, 128.0)
    code = jnp.clip(whole((size * jnp.exp2(-power) - 1.0) * steps), 0.0, steps - 1.0)
    high = jnp.floor(code * 0.0625)
    exponent = jnp.where(fine, power * 16.0 + (code - 16.0 * high) + 192.0, power + 264.0)
    value = join(jnp.where(fine, high, code), exponent - 125.0)
    value = jnp.where(size < 2.0**-24, 0.0, value)
    return jnp.where(science < 0.0, -value, value)


def decode_science(value):
    size = jnp.abs(value)
    mantissa, exponent = part(jnp.maximum(size, 2.0**-125))
    exponent = exponent + 125.0
    high = jnp.floor(exponent * 0.0625)
    fine = exponent < 240.0
    low = jnp.where(fine, exponent - 16.0 * high, 0.0)
    power = jnp.where(fine, high - 12.0, exponent - 264.0)
    size = jnp.where(size == 0.0, 0.0, (2048.0 + mantissa * 16.0 + low) * 2.0**-11 * jnp.exp2(power))
    return jnp.where(value < 0.0, -size, size)


def prepare(sz, n_epoch, tiles, count, nsel):
    lanes = count * SLOT
    per_owner = count // n_epoch
    width = sz.lines * CHUNK
    nbasis = 128

    def body(*refs):
        sources, refs = refs[:9], refs[9:]
        r_out, sw_out, own_out, sci_out, weight_out = refs[:5]
        var, mask, inter, offs, index, coef, basis, table, place, sems = refs[5:]
        targets = [own_out, sci_out, var, mask, inter, offs, index, coef, basis]
        copies = [
            pltpu.make_async_copy(source, target, sems.at[i])
            for i, (source, target) in enumerate(zip(sources, targets))
        ]
        for copy in reversed(copies):
            copy.start()
        me, _ = here("epoch")
        table[...] = jnp.zeros(table.shape, f32)
        col = iota((FINE, width), 0)
        base = iota((FINE, width), 1) - sz.place(col)
        base = jnp.where(col < KS, base, -1)
        for a in range(0, KS + 1, 2):
            pair = jnp.concatenate([(base == a).astype(f32), (base == a + 1).astype(f32)], axis=0)
            if a + 1 == KS:
                pair = jnp.where(iota(pair.shape, 0) < FINE, pair, 0.0)
            place[a * FINE : (a + 2) * FINE] = pair.astype(bf16)
        for copy in reversed(copies[4:]):
            copy.wait()
        for a in range(KS):
            table[a * FINE : a * FINE + KS, : basis.shape[2]] = basis[a]
        chosen = jnp.concatenate([index[e : e + 1, :] for e in range(count)], axis=1)
        onehot = (iota((nbasis, count * nsel), 0) == chosen).astype(f32)
        blocks = []
        for e in range(count):
            mine = jnp.concatenate([coef[:, e, :], jnp.zeros((SLOT - NPOLY, nsel), f32)], axis=0)
            wide = jnp.concatenate([mine] * count, axis=1)
            blocks.append(jnp.where(iota(wide.shape, 1) // nsel == e, wide, 0.0))
        combine = jnp.concatenate(blocks, axis=0)
        mixing = lax.dot_general(
            onehot, combine, (((1,), (1,)), ((), ())), precision=highest, preferred_element_type=f32
        )
        images = jnp.dot(table[...], mixing, precision=highest, preferred_element_type=f32)
        rows = lax.dot_general(
            images.astype(bf16), place[...], (((0,), (0,)), ((), ())), preferred_element_type=f32
        )
        for copy in reversed(copies[:4]):
            copy.wait()
        for e in range(count):
            weight_out[e] = mask[e].astype(f32) / var[e]
            science = jnp.where(mask[e] == 0, 0.0, sci_out[e])
            top = jnp.max(jnp.abs(science), axis=(0, 1), keepdims=True)
            scale = jnp.exp2(exponent_of(jnp.maximum(top, 2.0**-100)) - 2.0).astype(bf16).astype(f32)
            science = science / scale
            parts = [encode_science(science), encode_weight(weight_out[e])]
            sw_out[e] = jnp.concatenate(parts, axis=0).astype(bf16)
            mine = rows[e * SLOT : (e + 1) * SLOT]
            mine = jnp.concatenate(
                [mine[:, i * CHUNK : (i + 1) * CHUNK] for i in range(sz.lines)], axis=0
            )
            tile = inter[e // per_owner * count + me * per_owner + e % per_owner] - me * tiles
            tile = jnp.clip(tile, 0, tiles - 1).astype(f32)
            down, across = offs[0:1, e : e + 1].astype(f32), offs[1:2, e : e + 1].astype(f32)
            spare, spot = iota(mine.shape, 0) == NPOLY, iota(mine.shape, 1)
            for lane, value in enumerate((down, across, tile, scale)):
                mine = jnp.where(spare & (spot == lane), value, mine)
            r_out[e] = mine.astype(bf16)

    hbm, vmem = pl.BlockSpec(memory_space=pltpu.HBM), pl.BlockSpec(memory_space=pltpu.VMEM)
    shape = (count, sz.height, sz.width)

    def call(*sources):
        template, _, _, _, inter, offs, index, coef, basis = sources
        return pl.pallas_call(
            body,
            in_specs=[hbm] * 9,
            out_specs=(vmem,) * 5,
            out_shape=(
                jax.ShapeDtypeStruct((count, sz.r_rows, CHUNK), bf16),
                jax.ShapeDtypeStruct((count, sz.sw_rows, sz.width), bf16),
                jax.ShapeDtypeStruct(template.shape, bf16),
                jax.ShapeDtypeStruct(shape, f32),
                jax.ShapeDtypeStruct(shape, f32),
            ),
            scratch_shapes=[
                pltpu.VMEM(shape, f32),
                pltpu.VMEM(shape, jnp.int32),
                pltpu.SMEM(inter.shape, jnp.int32),
                pltpu.VMEM(offs.shape, jnp.int32),
                pltpu.VMEM(index.shape, jnp.int32),
                pltpu.VMEM(coef.shape, f32),
                pltpu.VMEM(basis.shape, f32),
                pltpu.VMEM(((KS + 1) * FINE, nbasis), f32),
                pltpu.VMEM(((KS + 1) * FINE, width), bf16),
                pltpu.SemaphoreType.DMA((9,)),
            ],
            compiler_params=pltpu.CompilerParams(vmem_limit_bytes=VMEM_LIMIT),
            cost_estimate=pl.CostEstimate(
                flops=1_000_000_000, bytes_accessed=6_000_000, transcendentals=0
            ),
            name="prepare",
        )(*[pltpu.with_memory_space_constraint(source, pltpu.HBM) for source in sources])

    return call


def here(axis):
    return lax.axis_index(axis), lax.axis_size(axis)


def partner(me, n, k, back):
    if n & (n - 1) == 0:
        return me ^ k
    return (me + (n - k if back else k)) % n


def pack(sz, n_epoch, tiles, count, peers):
    per_owner = count // n_epoch
    h, w = sz.height, sz.width

    def body(own, low, high, left, low_left, high_left, right, low_right, high_right, sw, r, *outs):
        slabs, sends = outs[0], outs[1:]
        me, _ = here("epoch")
        strip, strips = here("strip")
        band, bands = here("band")

        def column(middle, above, below, t, cut):
            above = jnp.where(strip > 0, above[t, h - 16 :, cut].astype(f32), 0.0)
            above = jnp.where(iota(above.shape, 0) >= 16 - REACH, above, 0.0)
            below = jnp.where(strip < strips - 1, below[t, :16, cut].astype(f32), 0.0)
            below = jnp.where(iota(below.shape, 0) < REACH, below, 0.0)
            parts = [middle[t, :, cut].astype(f32), below]
            gap = sz.rows - h - 32
            if gap:
                parts.append(jnp.zeros((gap, below.shape[1]), f32))
            return jnp.concatenate(parts + [above], axis=0)

        whole_slabs = []
        for t in range(tiles):
            parts = [column(own, low, high, t, slice(None))]
            before = column(left, low_left, high_left, t, slice(w - 128, w))
            after = column(right, low_right, high_right, t, slice(0, 128))
            lane = iota(before.shape, 1)
            before = jnp.where((lane >= 128 - REACH) & (band > 0), before, 0.0)
            after = jnp.where((lane < REACH) & (band < bands - 1), after, 0.0)
            if sz.lanes - w == 128:
                parts.append(before + after)
            else:
                gap = sz.lanes - w - 256
                parts += [after] + ([jnp.zeros((sz.rows, gap), f32)] if gap else []) + [before]
            slab = jnp.concatenate(parts, axis=1)
            slabs[t] = slab.astype(bf16)
            if sz.one_side:
                side = jnp.where(strip == 0, slab[h : h + 16], slab[sz.rows - 16 :])
                slab = jnp.concatenate([slab[:h], side], axis=0)
            whole_slabs.append(slab)
        for k, out in zip(peers, sends):
            q = partner(me, n_epoch, k, False)
            for c in range(per_owner):
                mine = q * per_owner + c
                lines = r[mine].astype(f32)
                covered = lines[NPOLY : NPOLY + 1, 2:3]
                slab = whole_slabs[0]
                for t in range(1, tiles):
                    pick = jnp.broadcast_to(covered, slab.shape) == t
                    slab = jnp.where(pick, whole_slabs[t], slab)
                halo = slab[:, sz.lanes - 128 :]
                if sz.lanes - w != 128:
                    halo = halo + slab[:, w : w + 128]
                bits = []
                for part in range(sz.halo_rows // 8 * (w // 128)):
                    piece = jnp.zeros((8, 128), f32)
                    for slot in range(4):
                        g = part * 4 + slot
                        if g < sz.groups:
                            piece = piece + pltpu.roll(halo[g * 8 : g * 8 + 8], slot * 32 + REACH, 1)
                    bits.append(piece)
                wide = w // 128
                bits = [
                    jnp.concatenate(bits[i * wide : (i + 1) * wide], axis=1)
                    for i in range(sz.halo_rows // 8)
                ]
                parts = [sw[mine].astype(f32), lines, slab[:, :w]] + bits
                out[c] = jnp.concatenate(parts, axis=0).astype(bf16)

    vmem = pl.BlockSpec(memory_space=pltpu.VMEM)
    return pl.pallas_call(
        body,
        in_specs=[vmem] * 11,
        out_shape=(jax.ShapeDtypeStruct((tiles, sz.rows, sz.lanes), bf16),)
        + tuple(jax.ShapeDtypeStruct((per_owner, sz.total, w), bf16) for _ in peers),
        compiler_params=pltpu.CompilerParams(vmem_limit_bytes=VMEM_LIMIT),
        cost_estimate=pl.CostEstimate(flops=1_000_000, bytes_accessed=1_000_000, transcendentals=0),
        name="pack",
    )


def models(sz, n_epoch, tiles, count, ks, first, last, carried):
    per_owner = count // n_epoch
    h, w = sz.height, sz.width
    total_models = (2 * len(ks) + first) * per_owner

    def body(sci, weight, r, slabs, *refs):
        refs = list(refs)
        ready = None if first else refs.pop(0)
        pays = [refs.pop(0) for _ in ks]
        before = [] if first else [refs.pop(0) for _ in range(2)]
        done = [refs.pop(0) for _ in carried]
        if last:
            resid_out, coadd_out = refs.pop(0), refs.pop(0)
        else:
            numer_out, denom_out = refs.pop(0), refs.pop(0)
            resid_outs = [refs.pop(0) for _ in range(len(ks) + first)]
            ready_out = refs.pop(0) if first else None
        rhs, lhs, *refs = refs
        me, _ = here("epoch")
        strip, strips = here("strip")
        band, bands = here("band")

        copies = []

        def send(source, target):
            copies.append(pltpu.make_async_copy(source, target, out_sems.at[len(copies)]))
            copies[-1].start()

        if last:
            fresh, sums, out_sems = refs
            for k, value in zip(carried, done):
                q = me if k == 0 else partner(me, n_epoch, k, True)
                send(value, resid_out.at[pl.ds(q * per_owner, per_owner)])

        jobs = []

        def job(kind, q, c, slab, lines):
            mine = q * per_owner + c
            own = lines if kind == "local" else r[mine].astype(f32)
            scalars = [lines[NPOLY, lane].astype(jnp.int32) for lane in range(2)]
            tile = None if kind == "sent" else own[NPOLY, 2].astype(jnp.int32)
            jobs.append((kind, mine, slab, lines, scalars, tile, own))

        if first:
            for c in range(per_owner):
                job("local", me, c, None, r[me * per_owner + c].astype(f32))
        for k, pay in zip(ks, pays):
            q = partner(me, n_epoch, k, True)
            for c in range(per_owner):
                got = pay[c].astype(f32)
                job("owned", q, c, got, got[sz.sw_rows : sz.main_at])
            for c in range(per_owner):
                job("sent", q, c, pay[c].astype(f32), r[q * per_owner + c].astype(f32))

        row = (strip * h + iota((h, 128), 0)).astype(f32)
        r_unit = (2.0 * row + 1.0) / (h * strips) - 1.0
        r_unit = jnp.concatenate([r_unit] * (sz.lanes // 128), axis=1)
        spot = iota((SLOT, CHUNK), 1)
        filled = (spot % sz.span < FINE) & (spot < sz.per * sz.span)
        c_units = []
        for i in range(sz.phases):
            col = (band * w + iota((8, sz.lanes), 1) - i).astype(f32)
            col = (2.0 * col + 1.0) / (w * bands) - 1.0
            c_units.append(jnp.concatenate([col] * (h // 8), axis=0))
        for slot in range(2):
            for line in range(sz.lines):
                at = line * CHUNK + sz.per * sz.span
                if at < (line + 1) * CHUNK:
                    rhs[slot, at : (line + 1) * CHUNK] = jnp.zeros(((line + 1) * CHUNK - at, sz.lanes), bf16)

        def windows(turn, slab, scalars):
            window = rhs.at[turn % 2]
            down, across = scalars
            slab = pltpu.roll(slab, lax.rem(sz.rows + HALF - down, sz.rows), 0)[: sz.span]
            slab = pltpu.roll(slab.astype(bf16), lax.rem(sz.lanes + HALF - across, sz.lanes), 1)
            for slot in range(sz.lines * sz.per):
                moved = pltpu.roll(slab, sz.lanes - slot * sz.phases, 1) if slot else slab
                at = slot // sz.per * CHUNK + slot % sz.per * sz.span
                window[at : at + sz.span] = moved

        def band_matrix(turn, lines):
            band_rows = lhs.at[turn % 2]
            for i in range(sz.phases * sz.lines):
                phase, line = divmod(i, sz.lines)
                part = lines[line * SLOT : (line + 1) * SLOT]
                if phase:
                    part = pltpu.roll(part, CHUNK - phase * FINE, 1)
                part = jnp.where(filled, part, 0.0)
                for p in range(NPOLY):
                    at = (phase * NPOLY + p) * h
                    band_rows[at : at + h, line * CHUNK : (line + 1) * CHUNK] = pltpu.roll(
                        jnp.broadcast_to(part[p : p + 1], (h, CHUNK)), 0, 1, stride=1, stride_axis=0
                    )

        def chunk_image(turn, i, matrix):
            at = i * NPOLY * h
            conv = jnp.dot(
                matrix[at : at + NPOLY * h].astype(bf16), rhs[turn % 2], preferred_element_type=f32
            )
            conv = [conv[p * h : (p + 1) * h] for p in range(NPOLY)]
            c_unit = c_units[i]
            return (
                conv[0]
                + r_unit * (conv[1] + r_unit * conv[3] + c_unit * conv[4])
                + c_unit * (conv[2] + c_unit * conv[5])
            )

        def sent_slab(got):
            main, halo = got[sz.main_at : sz.halo_at], got[sz.halo_at :]
            wide = w // 128
            bits = []
            for g in range(sz.groups):
                part, slot = g // 4, g % 4
                line, side = part // wide, part % wide
                piece = halo[line * 8 : line * 8 + 8, side * 128 : side * 128 + 128]
                bits.append(pltpu.roll(piece, (256 - slot * 32 - REACH) % 128, 1))
            halo = jnp.concatenate(bits, axis=0)
            lane = iota(halo.shape, 1)
            halo = jnp.where((lane < REACH) | (lane >= 128 - REACH), halo, 0.0)
            if sz.lanes - w != 128:
                gap = sz.lanes - w - 256
                pieces = [jnp.where(lane < 64, halo, 0.0)]
                if gap:
                    pieces.append(jnp.zeros((sz.sent, gap), f32))
                halo = jnp.concatenate(pieces + [jnp.where(lane < 64, 0.0, halo)], axis=1)
            slab = jnp.concatenate([main, halo], axis=1)
            if sz.one_side:
                side, none = slab[h:], jnp.zeros((sz.rows - h - 32, sz.lanes), f32)
                below, above = jnp.where(strip == 0, side, 0.0), jnp.where(strip == 0, 0.0, side)
                slab = [slab[:h], below, none, above] if none.size else [slab[:h], below, above]
                slab = jnp.concatenate(slab, axis=0)
            return slab

        numer = [before[0][t] if before else jnp.zeros((h, w), f32) for t in range(tiles)]
        denom = [before[1][t] if before else jnp.zeros((h, w), f32) for t in range(tiles)]
        kept = 0
        settled = max(turn for turn, job in enumerate(jobs) if job[0] != "sent")
        images = []
        for turn in range(0, len(jobs), 2):
            pair = list(enumerate(jobs))[turn : turn + 2]
            for at, (kind, mine, got, lines, scalars, tile, own) in pair:
                if kind != "sent":
                    band_matrix(at, lines)
            for at, (kind, mine, got, lines, scalars, tile, own) in pair:
                windows(at, sent_slab(got) if kind == "sent" else slabs[tile].astype(f32), scalars)
            parts = [None for _ in pair]
            for i in reversed(range(sz.phases)):
                for slot, (at, _) in enumerate(pair):
                    value = chunk_image(at, i, ready.at[pair[slot][1][1]] if pair[slot][1][0] == "sent" else lhs.at[at % 2])
                    value = pltpu.roll(value, sz.lanes - i, 1) if i else value
                    parts[slot] = value if parts[slot] is None else parts[slot] + value
            images += [part[:, :w] for part in parts]
        for turn, (kind, mine, got, lines, scalars, tile, own) in enumerate(jobs):
            image = images[turn]
            if kind == "owned":
                scale = jnp.broadcast_to(lines[NPOLY : NPOLY + 1, 3:4], (h, w))
                science, seen = decode_science(got[:h]) * scale, decode_weight(got[h : 2 * h])
            else:
                science, seen = sci[mine], weight[mine]
                if last:
                    fresh[kept] = science - image
                    send(fresh.at[kept], resid_out.at[mine])
                else:
                    resid_outs[kept // per_owner][kept % per_owner] = science - image
                kept += 1
            if kind != "sent":
                change = seen * (science - image)
                covered = jnp.broadcast_to(own[NPOLY : NPOLY + 1, 2:3], (h, w))
                for t in range(tiles):
                    numer[t] = numer[t] + jnp.where(covered == t, change, 0.0)
                    denom[t] = denom[t] + jnp.where(covered == t, seen, 0.0)
            if turn == settled:
                for t in range(tiles):
                    if last:
                        sums[t] = numer[t] / (denom[t] + 1.0)
                    else:
                        numer_out[t], denom_out[t] = numer[t], denom[t]
                if last:
                    send(sums, coadd_out)
        for copy in copies:
            copy.wait()
        if first:
            for e in range(count):
                band_matrix(0, r[e].astype(f32))
                ready_out[e] = lhs[0].astype(bf16)

    image = jax.ShapeDtypeStruct((per_owner, h, w), f32)
    sums = jax.ShapeDtypeStruct((tiles, h, w), f32)
    if last:
        out_shape = (jax.ShapeDtypeStruct((count, h, w), f32), sums)
    else:
        out_shape = (sums, sums) + (image,) * (len(ks) + first)
        if first:
            out_shape += (jax.ShapeDtypeStruct((count, sz.phases * NPOLY * h, sz.depth), bf16),)
    vmem, hbm = pl.BlockSpec(memory_space=pltpu.VMEM), pl.BlockSpec(memory_space=pltpu.HBM)
    scratch = [
        pltpu.VMEM((2, sz.depth, sz.lanes), bf16),
        pltpu.VMEM((2, sz.phases * NPOLY * h, sz.depth), f32),
    ]
    if last:
        new = len(ks) * per_owner
        scratch += [
            pltpu.VMEM((new, h, w), f32),
            pltpu.VMEM((tiles, h, w), f32),
            pltpu.SemaphoreType.DMA((len(carried) + new + 1,)),
        ]
    return pl.pallas_call(
        body,
        in_specs=[vmem] * (4 + len(ks) + (0 if first else 3) + len(carried)),
        out_specs=(hbm if last else vmem,) * len(out_shape),
        out_shape=out_shape,
        scratch_shapes=scratch,
        compiler_params=pltpu.CompilerParams(vmem_limit_bytes=VMEM_LIMIT),
        cost_estimate=pl.CostEstimate(
            flops=total_models * 400_000_000, bytes_accessed=1_000_000, transcendentals=0
        ),
        name="models",
    )


def surroundings(block):
    strips, bands = lax.axis_size("strip"), lax.axis_size("band")
    sent, found = {}, {}
    for down in (-1, 0, 1):
        for across in (-1, 0, 1):
            if down == 0 and across == 0:
                continue
            pairs = []
            for s in range(strips):
                for b in range(bands):
                    to_s = s ^ 1 if strips == 2 and down else s - down
                    to_b = b ^ 1 if bands == 2 and across else b - across
                    if 0 <= to_s < strips and 0 <= to_b < bands:
                        pairs.append((s * bands + b, to_s * bands + to_b))
            key = tuple(pairs)
            if key and key not in sent:
                sent[key] = lax.ppermute(block, ("strip", "band"), pairs)
            found[down, across] = key
    return {step: sent.get(key, block) for step, key in found.items()}


def local(
    template, science, variance, bad_mask, intersection, offsets, basis_index, coefficients, basis
):
    n_epoch = lax.axis_size("epoch")
    tiles = template.shape[0]
    count, height, width = science.shape
    sz = Sizes(height, width, lax.axis_size("strip"))
    around = surroundings(template)
    r, sw, own, sci, weight = prepare(sz, n_epoch, tiles, count, basis_index.shape[1])(
        template,
        science,
        variance,
        bad_mask,
        intersection,
        offsets.T,
        basis_index,
        coefficients.transpose(2, 0, 1),
        basis.transpose(1, 2, 0),
    )
    around[0, 0] = own
    peers = list(range(1, n_epoch))
    order = peers[-1:] + peers[:-1]
    slabs, *sends = pack(sz, n_epoch, tiles, count, peers)(
        *[around[down, across] for across in (0, -1, 1) for down in (0, -1, 1)], sw, r
    )
    pays = {}
    for k, send in zip(order, [sends[peers.index(k)] for k in order]):
        pairs = [(i, partner(i, n_epoch, k, False)) for i in range(n_epoch)]
        pays[k] = lax.ppermute(send, "epoch", pairs)
    stages = [[]] + [[k] for k in order]
    sums, carried, ready = [], [], []
    for i, ks in enumerate(stages):
        first, last = i == 0, i == len(stages) - 1
        kept = [k for k, _ in carried] if last else []
        out = models(sz, n_epoch, tiles, count, ks, first, last, kept)(
            sci,
            weight,
            r,
            slabs,
            *ready,
            *[pays[k] for k in ks],
            *sums,
            *([value for _, value in carried] if last else []),
        )
        if last:
            return out
        sums = list(out[:2])
        if first:
            *out, matrices = out
            ready = [matrices]
        carried += list(zip(list(ks) + ([0] if first else []), out[2:]))


def solution(mesh):
    in_specs = (
        P(("groups", "epoch"), "strip", "band"),
        P(("groups", "epoch"), "strip", "band"),
        P(("groups", "epoch"), "strip", "band"),
        P(("groups", "epoch"), "strip", "band"),
        P("groups"),
        P(("groups", "epoch"), None),
        P(("groups", "epoch"), None),
        P(("groups", "epoch"), None, None),
        P(),
    )
    out_specs = (P(("groups", "epoch"), "strip", "band"), P(("groups", "epoch"), "strip", "band"))
    return jax.shard_map(local, mesh=mesh, in_specs=in_specs, out_specs=out_specs, check_vma=False)
```

```python
import jax
import jax.numpy as jnp
from jax import lax
from jax.experimental import pallas as pl
from jax.experimental.pallas import tpu as pltpu
from jax.sharding import PartitionSpec as P

KS = 19
HALF = 9
SHIFT = 4
NPOLY = 6
REACH = HALF + SHIFT
SLOT = 8
CHUNK = 256
FINE = 24
VMEM_LIMIT = 24 * 1024 * 1024

highest = lax.Precision.HIGHEST
f32 = jnp.float32
bf16 = jnp.bfloat16


def up(value, step):
    return -(-value // step) * step


class Sizes:
    def __init__(self, height, width, strips):
        self.height, self.width = height, width
        self.rows = up(height + 2 * REACH, 8)
        self.lanes = up(width + 2 * REACH, 128)
        self.span = up(height + KS - 1, 2 * FINE)
        self.phases = self.span // FINE
        self.per = CHUNK // self.span
        self.lines = -(-KS // (self.per * self.phases))
        self.depth = self.lines * CHUNK
        self.sw_rows = 2 * height
        self.r_rows = self.lines * SLOT
        self.one_side = strips <= 2
        self.sent = height + 16 if self.one_side else self.rows
        self.main_at = self.sw_rows + self.r_rows
        self.halo_at = self.main_at + self.sent
        self.groups = self.sent // 8
        self.halo_rows = up(self.groups * 32, width) // width * 8
        self.total = self.halo_at + self.halo_rows

    def place(self, column):
        slot, phase = column // self.phases, column % self.phases
        return slot // self.per * CHUNK + (slot % self.per * self.phases + phase) * FINE


def iota(shape, axis):
    return lax.broadcasted_iota(jnp.int32, shape, axis)


def whole(value):
    return jnp.floor(value + 0.5)


def exponent_of(value):
    return jnp.floor(jnp.log2(value))


def join(mantissa, exponent):
    return (1.0 + mantissa * 2.0**-7) * jnp.exp2(exponent)


def part(value):
    exponent = jnp.floor(jnp.log2(value) + 0.003)
    return whole((value * jnp.exp2(-exponent) - 1.0) * 128.0), exponent


def encode_weight(weight):
    code = jnp.minimum(whole(weight * 65536.0), 32767.0)
    half = jnp.floor(code * 0.5)
    exponent = jnp.floor(half * 2.0**-7)
    value = join(half - exponent * 128.0, exponent - 63.0)
    return jnp.where(code > 2.0 * half, -value, value)


def decode_weight(value):
    mantissa, exponent = part(jnp.abs(value))
    code = (exponent + 63.0) * 256.0 + mantissa * 2.0
    return jnp.where(value < 0.0, code + 1.0, code) * 2.0**-16


def encode_science(science):
    size = jnp.abs(science)
    power = jnp.clip(exponent_of(jnp.maximum(size, 2.0**-30)), -24.0, 2.0)
    fine = power >= -12.0
    steps = jnp.where(fine, 2048.0, 128.0)
    code = jnp.clip(whole((size * jnp.exp2(-power) - 1.0) * steps), 0.0, steps - 1.0)
    high = jnp.floor(code * 0.0625)
    exponent = jnp.where(fine, power * 16.0 + (code - 16.0 * high) + 192.0, power + 264.0)
    value = join(jnp.where(fine, high, code), exponent - 125.0)
    value = jnp.where(size < 2.0**-24, 0.0, value)
    return jnp.where(science < 0.0, -value, value)


def decode_science(value):
    size = jnp.abs(value)
    mantissa, exponent = part(jnp.maximum(size, 2.0**-125))
    exponent = exponent + 125.0
    high = jnp.floor(exponent * 0.0625)
    fine = exponent < 240.0
    low = jnp.where(fine, exponent - 16.0 * high, 0.0)
    power = jnp.where(fine, high - 12.0, exponent - 264.0)
    size = jnp.where(size == 0.0, 0.0, (2048.0 + mantissa * 16.0 + low) * 2.0**-11 * jnp.exp2(power))
    return jnp.where(value < 0.0, -size, size)


def prepare(sz, n_epoch, tiles, count, nsel):
    lanes = count * SLOT
    per_owner = count // n_epoch
    width = sz.lines * CHUNK
    nbasis = 128

    def body(*refs):
        sources, refs = refs[:9], refs[9:]
        r_out, sw_out, own_out, sci_out, weight_out = refs[:5]
        var, mask, inter, offs, index, coef, basis, table, place, sems = refs[5:]
        targets = [own_out, sci_out, var, mask, inter, offs, index, coef, basis]
        copies = [
            pltpu.make_async_copy(source, target, sems.at[i])
            for i, (source, target) in enumerate(zip(sources, targets))
        ]
        for copy in reversed(copies):
            copy.start()
        me, _ = here("epoch")
        table[...] = jnp.zeros(table.shape, f32)
        col = iota((FINE, width), 0)
        base = iota((FINE, width), 1) - sz.place(col)
        base = jnp.where(col < KS, base, -1)
        for a in range(0, KS + 1, 2):
            pair = jnp.concatenate([(base == a).astype(f32), (base == a + 1).astype(f32)], axis=0)
            if a + 1 == KS:
                pair = jnp.where(iota(pair.shape, 0) < FINE, pair, 0.0)
            place[a * FINE : (a + 2) * FINE] = pair.astype(bf16)
        for copy in reversed(copies[4:]):
            copy.wait()
        for a in range(KS):
            table[a * FINE : a * FINE + KS, : basis.shape[2]] = basis[a]
        chosen = jnp.concatenate([index[e : e + 1, :] for e in range(count)], axis=1)
        onehot = (iota((nbasis, count * nsel), 0) == chosen).astype(f32)
        blocks = []
        for e in range(count):
            mine = jnp.concatenate([coef[:, e, :], jnp.zeros((SLOT - NPOLY, nsel), f32)], axis=0)
            wide = jnp.concatenate([mine] * count, axis=1)
            blocks.append(jnp.where(iota(wide.shape, 1) // nsel == e, wide, 0.0))
        combine = jnp.concatenate(blocks, axis=0)
        mixing = lax.dot_general(
            onehot, combine, (((1,), (1,)), ((), ())), precision=highest, preferred_element_type=f32
        )
        images = jnp.dot(table[...], mixing, precision=highest, preferred_element_type=f32)
        rows = lax.dot_general(
            images.astype(bf16), place[...], (((0,), (0,)), ((), ())), preferred_element_type=f32
        )
        for copy in reversed(copies[:4]):
            copy.wait()
        for e in range(count):
            weight_out[e] = mask[e].astype(f32) / var[e]
            science = jnp.where(mask[e] == 0, 0.0, sci_out[e])
            top = jnp.max(jnp.abs(science), axis=(0, 1), keepdims=True)
            scale = jnp.exp2(exponent_of(jnp.maximum(top, 2.0**-100)) - 2.0).astype(bf16).astype(f32)
            science = science / scale
            parts = [encode_science(science), encode_weight(weight_out[e])]
            sw_out[e] = jnp.concatenate(parts, axis=0).astype(bf16)
            mine = rows[e * SLOT : (e + 1) * SLOT]
            mine = jnp.concatenate(
                [mine[:, i * CHUNK : (i + 1) * CHUNK] for i in range(sz.lines)], axis=0
            )
            tile = inter[e // per_owner * count + me * per_owner + e % per_owner] - me * tiles
            tile = jnp.clip(tile, 0, tiles - 1).astype(f32)
            down, across = offs[0:1, e : e + 1].astype(f32), offs[1:2, e : e + 1].astype(f32)
            spare, spot = iota(mine.shape, 0) == NPOLY, iota(mine.shape, 1)
            for lane, value in enumerate((down, across, tile, scale)):
                mine = jnp.where(spare & (spot == lane), value, mine)
            r_out[e] = mine.astype(bf16)

    hbm, vmem = pl.BlockSpec(memory_space=pltpu.HBM), pl.BlockSpec(memory_space=pltpu.VMEM)
    shape = (count, sz.height, sz.width)

    def call(*sources):
        template, _, _, _, inter, offs, index, coef, basis = sources
        return pl.pallas_call(
            body,
            in_specs=[hbm] * 9,
            out_specs=(vmem,) * 5,
            out_shape=(
                jax.ShapeDtypeStruct((count, sz.r_rows, CHUNK), bf16),
                jax.ShapeDtypeStruct((count, sz.sw_rows, sz.width), bf16),
                jax.ShapeDtypeStruct(template.shape, bf16),
                jax.ShapeDtypeStruct(shape, f32),
                jax.ShapeDtypeStruct(shape, f32),
            ),
            scratch_shapes=[
                pltpu.VMEM(shape, f32),
                pltpu.VMEM(shape, jnp.int32),
                pltpu.SMEM(inter.shape, jnp.int32),
                pltpu.VMEM(offs.shape, jnp.int32),
                pltpu.VMEM(index.shape, jnp.int32),
                pltpu.VMEM(coef.shape, f32),
                pltpu.VMEM(basis.shape, f32),
                pltpu.VMEM(((KS + 1) * FINE, nbasis), f32),
                pltpu.VMEM(((KS + 1) * FINE, width), bf16),
                pltpu.SemaphoreType.DMA((9,)),
            ],
            compiler_params=pltpu.CompilerParams(vmem_limit_bytes=VMEM_LIMIT),
            cost_estimate=pl.CostEstimate(
                flops=1_000_000_000, bytes_accessed=6_000_000, transcendentals=0
            ),
            name="prepare",
        )(*[pltpu.with_memory_space_constraint(source, pltpu.HBM) for source in sources])

    return call


def here(axis):
    return lax.axis_index(axis), lax.axis_size(axis)


def partner(me, n, k, back):
    if n & (n - 1) == 0:
        return me ^ k
    return (me + (n - k if back else k)) % n


def pack(sz, n_epoch, tiles, count, peers):
    per_owner = count // n_epoch
    h, w = sz.height, sz.width

    def body(own, low, high, left, low_left, high_left, right, low_right, high_right, sw, r, *outs):
        slabs, sends = outs[0], outs[1:]
        me, _ = here("epoch")
        strip, strips = here("strip")
        band, bands = here("band")

        def column(middle, above, below, t, cut):
            above = jnp.where(strip > 0, above[t, h - 16 :, cut].astype(f32), 0.0)
            above = jnp.where(iota(above.shape, 0) >= 16 - REACH, above, 0.0)
            below = jnp.where(strip < strips - 1, below[t, :16, cut].astype(f32), 0.0)
            below = jnp.where(iota(below.shape, 0) < REACH, below, 0.0)
            parts = [middle[t, :, cut].astype(f32), below]
            gap = sz.rows - h - 32
            if gap:
                parts.append(jnp.zeros((gap, below.shape[1]), f32))
            return jnp.concatenate(parts + [above], axis=0)

        whole_slabs = []
        for t in range(tiles):
            parts = [column(own, low, high, t, slice(None))]
            before = column(left, low_left, high_left, t, slice(w - 128, w))
            after = column(right, low_right, high_right, t, slice(0, 128))
            lane = iota(before.shape, 1)
            before = jnp.where((lane >= 128 - REACH) & (band > 0), before, 0.0)
            after = jnp.where((lane < REACH) & (band < bands - 1), after, 0.0)
            if sz.lanes - w == 128:
                parts.append(before + after)
            else:
                gap = sz.lanes - w - 256
                parts += [after] + ([jnp.zeros((sz.rows, gap), f32)] if gap else []) + [before]
            slab = jnp.concatenate(parts, axis=1)
            slabs[t] = slab.astype(bf16)
            if sz.one_side:
                side = jnp.where(strip == 0, slab[h : h + 16], slab[sz.rows - 16 :])
                slab = jnp.concatenate([slab[:h], side], axis=0)
            whole_slabs.append(slab)
        for k, out in zip(peers, sends):
            q = partner(me, n_epoch, k, False)
            for c in range(per_owner):
                mine = q * per_owner + c
                lines = r[mine].astype(f32)
                covered = lines[NPOLY : NPOLY + 1, 2:3]
                slab = whole_slabs[0]
                for t in range(1, tiles):
                    pick = jnp.broadcast_to(covered, slab.shape) == t
                    slab = jnp.where(pick, whole_slabs[t], slab)
                halo = slab[:, sz.lanes - 128 :]
                if sz.lanes - w != 128:
                    halo = halo + slab[:, w : w + 128]
                bits = []
                for part in range(sz.halo_rows // 8 * (w // 128)):
                    piece = jnp.zeros((8, 128), f32)
                    for slot in range(4):
                        g = part * 4 + slot
                        if g < sz.groups:
                            piece = piece + pltpu.roll(halo[g * 8 : g * 8 + 8], slot * 32 + REACH, 1)
                    bits.append(piece)
                wide = w // 128
                bits = [
                    jnp.concatenate(bits[i * wide : (i + 1) * wide], axis=1)
                    for i in range(sz.halo_rows // 8)
                ]
                parts = [sw[mine].astype(f32), lines, slab[:, :w]] + bits
                out[c] = jnp.concatenate(parts, axis=0).astype(bf16)

    vmem = pl.BlockSpec(memory_space=pltpu.VMEM)
    return pl.pallas_call(
        body,
        in_specs=[vmem] * 11,
        out_shape=(jax.ShapeDtypeStruct((tiles, sz.rows, sz.lanes), bf16),)
        + tuple(jax.ShapeDtypeStruct((per_owner, sz.total, w), bf16) for _ in peers),
        compiler_params=pltpu.CompilerParams(vmem_limit_bytes=VMEM_LIMIT),
        cost_estimate=pl.CostEstimate(flops=1_000_000, bytes_accessed=1_000_000, transcendentals=0),
        name="pack",
    )


def models(sz, n_epoch, tiles, count, ks, first, last, carried):
    per_owner = count // n_epoch
    h, w = sz.height, sz.width
    total_models = (2 * len(ks) + first) * per_owner

    def body(sci, weight, r, slabs, *refs):
        refs = list(refs)
        ready = None if first else refs.pop(0)
        pays = [refs.pop(0) for _ in ks]
        before = [] if first else [refs.pop(0) for _ in range(2)]
        done = [refs.pop(0) for _ in carried]
        if last:
            resid_out, coadd_out = refs.pop(0), refs.pop(0)
        else:
            numer_out, denom_out = refs.pop(0), refs.pop(0)
            resid_outs = [refs.pop(0) for _ in range(len(ks) + first)]
            ready_out = refs.pop(0) if first else None
        rhs, lhs, *refs = refs
        me, _ = here("epoch")
        strip, strips = here("strip")
        band, bands = here("band")

        copies = []

        def send(source, target):
            copies.append(pltpu.make_async_copy(source, target, out_sems.at[len(copies)]))
            copies[-1].start()

        if last:
            fresh, sums, out_sems = refs
            for k, value in zip(carried, done):
                q = me if k == 0 else partner(me, n_epoch, k, True)
                send(value, resid_out.at[pl.ds(q * per_owner, per_owner)])

        jobs = []

        def job(kind, q, c, slab, lines):
            mine = q * per_owner + c
            own = lines if kind == "local" else r[mine].astype(f32)
            scalars = [lines[NPOLY, lane].astype(jnp.int32) for lane in range(2)]
            tile = None if kind == "sent" else own[NPOLY, 2].astype(jnp.int32)
            jobs.append((kind, mine, slab, lines, scalars, tile, own))

        if first:
            for c in range(per_owner):
                job("local", me, c, None, r[me * per_owner + c].astype(f32))
        for k, pay in zip(ks, pays):
            q = partner(me, n_epoch, k, True)
            for c in range(per_owner):
                got = pay[c].astype(f32)
                job("owned", q, c, got, got[sz.sw_rows : sz.main_at])
            for c in range(per_owner):
                job("sent", q, c, pay[c].astype(f32), r[q * per_owner + c].astype(f32))

        row = (strip * h + iota((h, 128), 0)).astype(f32)
        r_unit = (2.0 * row + 1.0) / (h * strips) - 1.0
        r_unit = jnp.concatenate([r_unit] * (sz.lanes // 128), axis=1)
        spot = iota((SLOT, CHUNK), 1)
        filled = (spot % sz.span < FINE) & (spot < sz.per * sz.span)
        c_units = []
        for i in range(sz.phases):
            col = (band * w + iota((8, sz.lanes), 1) - i).astype(f32)
            col = (2.0 * col + 1.0) / (w * bands) - 1.0
            c_units.append(jnp.concatenate([col] * (h // 8), axis=0))
        for slot in range(2):
            for line in range(sz.lines):
                at = line * CHUNK + sz.per * sz.span
                if at < (line + 1) * CHUNK:
                    rhs[slot, at : (line + 1) * CHUNK] = jnp.zeros(((line + 1) * CHUNK - at, sz.lanes), bf16)

        def windows(turn, slab, scalars):
            window = rhs.at[turn % 2]
            down, across = scalars
            slab = pltpu.roll(slab, lax.rem(sz.rows + HALF - down, sz.rows), 0)[: sz.span]
            slab = pltpu.roll(slab.astype(bf16), lax.rem(sz.lanes + HALF - across, sz.lanes), 1)
            for slot in range(sz.lines * sz.per):
                moved = pltpu.roll(slab, sz.lanes - slot * sz.phases, 1) if slot else slab
                at = slot // sz.per * CHUNK + slot % sz.per * sz.span
                window[at : at + sz.span] = moved

        def band_matrix(turn, lines):
            band_rows = lhs.at[turn % 2]
            for i in range(sz.phases * sz.lines):
                phase, line = divmod(i, sz.lines)
                part = lines[line * SLOT : (line + 1) * SLOT]
                if phase:
                    part = pltpu.roll(part, CHUNK - phase * FINE, 1)
                part = jnp.where(filled, part, 0.0)
                for p in range(NPOLY):
                    at = (phase * NPOLY + p) * h
                    band_rows[at : at + h, line * CHUNK : (line + 1) * CHUNK] = pltpu.roll(
                        jnp.broadcast_to(part[p : p + 1], (h, CHUNK)), 0, 1, stride=1, stride_axis=0
                    )

        def chunk_image(turn, i, matrix):
            at = i * NPOLY * h
            conv = jnp.dot(
                matrix[at : at + NPOLY * h].astype(bf16), rhs[turn % 2], preferred_element_type=f32
            )
            conv = [conv[p * h : (p + 1) * h] for p in range(NPOLY)]
            c_unit = c_units[i]
            return (
                conv[0]
                + r_unit * (conv[1] + r_unit * conv[3] + c_unit * conv[4])
                + c_unit * (conv[2] + c_unit * conv[5])
            )

        def sent_slab(got):
            main, halo = got[sz.main_at : sz.halo_at], got[sz.halo_at :]
            wide = w // 128
            bits = []
            for g in range(sz.groups):
                part, slot = g // 4, g % 4
                line, side = part // wide, part % wide
                piece = halo[line * 8 : line * 8 + 8, side * 128 : side * 128 + 128]
                bits.append(pltpu.roll(piece, (256 - slot * 32 - REACH) % 128, 1))
            halo = jnp.concatenate(bits, axis=0)
            lane = iota(halo.shape, 1)
            halo = jnp.where((lane < REACH) | (lane >= 128 - REACH), halo, 0.0)
            if sz.lanes - w != 128:
                gap = sz.lanes - w - 256
                pieces = [jnp.where(lane < 64, halo, 0.0)]
                if gap:
                    pieces.append(jnp.zeros((sz.sent, gap), f32))
                halo = jnp.concatenate(pieces + [jnp.where(lane < 64, 0.0, halo)], axis=1)
            slab = jnp.concatenate([main, halo], axis=1)
            if sz.one_side:
                side, none = slab[h:], jnp.zeros((sz.rows - h - 32, sz.lanes), f32)
                below, above = jnp.where(strip == 0, side, 0.0), jnp.where(strip == 0, 0.0, side)
                slab = [slab[:h], below, none, above] if none.size else [slab[:h], below, above]
                slab = jnp.concatenate(slab, axis=0)
            return slab

        numer = [before[0][t] if before else jnp.zeros((h, w), f32) for t in range(tiles)]
        denom = [before[1][t] if before else jnp.zeros((h, w), f32) for t in range(tiles)]
        kept = 0
        settled = max(turn for turn, job in enumerate(jobs) if job[0] != "sent")
        images = []
        for turn in range(0, len(jobs), 2):
            pair = list(enumerate(jobs))[turn : turn + 2]
            for at, (kind, mine, got, lines, scalars, tile, own) in pair:
                if kind != "sent":
                    band_matrix(at, lines)
            for at, (kind, mine, got, lines, scalars, tile, own) in pair:
                windows(at, sent_slab(got) if kind == "sent" else slabs[tile].astype(f32), scalars)
            parts = [None for _ in pair]
            for i in reversed(range(sz.phases)):
                for slot, (at, _) in enumerate(pair):
                    value = chunk_image(at, i, ready.at[pair[slot][1][1]] if pair[slot][1][0] == "sent" else lhs.at[at % 2])
                    value = pltpu.roll(value, sz.lanes - i, 1) if i else value
                    parts[slot] = value if parts[slot] is None else parts[slot] + value
            images += [part[:, :w] for part in parts]
        for turn, (kind, mine, got, lines, scalars, tile, own) in enumerate(jobs):
            image = images[turn]
            if kind == "owned":
                scale = jnp.broadcast_to(lines[NPOLY : NPOLY + 1, 3:4], (h, w))
                science, seen = decode_science(got[:h]) * scale, decode_weight(got[h : 2 * h])
            else:
                science, seen = sci[mine], weight[mine]
                if last:
                    fresh[kept] = science - image
                    send(fresh.at[kept], resid_out.at[mine])
                else:
                    resid_outs[kept // per_owner][kept % per_owner] = science - image
                kept += 1
            if kind != "sent":
                change = seen * (science - image)
                covered = jnp.broadcast_to(own[NPOLY : NPOLY + 1, 2:3], (h, w))
                for t in range(tiles):
                    numer[t] = numer[t] + jnp.where(covered == t, change, 0.0)
                    denom[t] = denom[t] + jnp.where(covered == t, seen, 0.0)
            if turn == settled:
                for t in range(tiles):
                    if last:
                        sums[t] = numer[t] / (denom[t] + 1.0)
                    else:
                        numer_out[t], denom_out[t] = numer[t], denom[t]
                if last:
                    send(sums, coadd_out)
        for copy in copies:
            copy.wait()
        if first:
            for e in range(count):
                band_matrix(0, r[e].astype(f32))
                ready_out[e] = lhs[0].astype(bf16)

    image = jax.ShapeDtypeStruct((per_owner, h, w), f32)
    sums = jax.ShapeDtypeStruct((tiles, h, w), f32)
    if last:
        out_shape = (jax.ShapeDtypeStruct((count, h, w), f32), sums)
    else:
        out_shape = (sums, sums) + (image,) * (len(ks) + first)
        if first:
            out_shape += (jax.ShapeDtypeStruct((count, sz.phases * NPOLY * h, sz.depth), bf16),)
    vmem, hbm = pl.BlockSpec(memory_space=pltpu.VMEM), pl.BlockSpec(memory_space=pltpu.HBM)
    scratch = [
        pltpu.VMEM((2, sz.depth, sz.lanes), bf16),
        pltpu.VMEM((2, sz.phases * NPOLY * h, sz.depth), f32),
    ]
    if last:
        new = len(ks) * per_owner
        scratch += [
            pltpu.VMEM((new, h, w), f32),
            pltpu.VMEM((tiles, h, w), f32),
            pltpu.SemaphoreType.DMA((len(carried) + new + 1,)),
        ]
    return pl.pallas_call(
        body,
        in_specs=[vmem] * (4 + len(ks) + (0 if first else 3) + len(carried)),
        out_specs=(hbm if last else vmem,) * len(out_shape),
        out_shape=out_shape,
        scratch_shapes=scratch,
        compiler_params=pltpu.CompilerParams(vmem_limit_bytes=VMEM_LIMIT),
        cost_estimate=pl.CostEstimate(
            flops=total_models * 400_000_000, bytes_accessed=1_000_000, transcendentals=0
        ),
        name="models",
    )


def surroundings(block):
    strips, bands = lax.axis_size("strip"), lax.axis_size("band")
    sent, found = {}, {}
    for down in (-1, 0, 1):
        for across in (-1, 0, 1):
            if down == 0 and across == 0:
                continue
            pairs = []
            for s in range(strips):
                for b in range(bands):
                    to_s = s ^ 1 if strips == 2 and down else s - down
                    to_b = b ^ 1 if bands == 2 and across else b - across
                    if 0 <= to_s < strips and 0 <= to_b < bands:
                        pairs.append((s * bands + b, to_s * bands + to_b))
            key = tuple(pairs)
            if key and key not in sent:
                sent[key] = lax.ppermute(block, ("strip", "band"), pairs)
            found[down, across] = key
    return {step: sent.get(key, block) for step, key in found.items()}


def local(
    template, science, variance, bad_mask, intersection, offsets, basis_index, coefficients, basis
):
    n_epoch = lax.axis_size("epoch")
    tiles = template.shape[0]
    count, height, width = science.shape
    sz = Sizes(height, width, lax.axis_size("strip"))
    around = surroundings(template)
    r, sw, own, sci, weight = prepare(sz, n_epoch, tiles, count, basis_index.shape[1])(
        template,
        science,
        variance,
        bad_mask,
        intersection,
        offsets.T,
        basis_index,
        coefficients.transpose(2, 0, 1),
        basis.transpose(1, 2, 0),
    )
    around[0, 0] = own
    peers = list(range(1, n_epoch))
    order = peers[-1:] + peers[:-1]
    slabs, *sends = pack(sz, n_epoch, tiles, count, peers)(
        *[around[down, across] for across in (0, -1, 1) for down in (0, -1, 1)], sw, r
    )
    pays = {}
    for k, send in reversed(list(zip(peers, sends))):
        pairs = [(i, partner(i, n_epoch, k, False)) for i in range(n_epoch)]
        pays[k] = lax.ppermute(send, "epoch", pairs)
    stages = [[]] + [[k] for k in order]
    sums, carried, ready = [], [], []
    for i, ks in enumerate(stages):
        first, last = i == 0, i == len(stages) - 1
        kept = [k for k, _ in carried] if last else []
        out = models(sz, n_epoch, tiles, count, ks, first, last, kept)(
            sci,
            weight,
            r,
            slabs,
            *ready,
            *[pays[k] for k in ks],
            *sums,
            *([value for _, value in carried] if last else []),
        )
        if last:
            return out
        sums = list(out[:2])
        if first:
            *out, matrices = out
            ready = [matrices]
        carried += list(zip(list(ks) + ([0] if first else []), out[2:]))


def solution(mesh):
    in_specs = (
        P(("groups", "epoch"), "strip", "band"),
        P(("groups", "epoch"), "strip", "band"),
        P(("groups", "epoch"), "strip", "band"),
        P(("groups", "epoch"), "strip", "band"),
        P("groups"),
        P(("groups", "epoch"), None),
        P(("groups", "epoch"), None),
        P(("groups", "epoch"), None, None),
        P(),
    )
    out_specs = (P(("groups", "epoch"), "strip", "band"), P(("groups", "epoch"), "strip", "band"))
    return jax.shard_map(local, mesh=mesh, in_specs=in_specs, out_specs=out_specs, check_vma=False)
```

```python
import jax
import jax.numpy as jnp
from jax import lax
from jax.experimental import pallas as pl
from jax.experimental.pallas import tpu as pltpu
from jax.sharding import PartitionSpec as P

KS = 19
HALF = 9
SHIFT = 4
NPOLY = 6
REACH = HALF + SHIFT
SLOT = 8
CHUNK = 256
FINE = 24
VMEM_LIMIT = 24 * 1024 * 1024

highest = lax.Precision.HIGHEST
f32 = jnp.float32
bf16 = jnp.bfloat16


def up(value, step):
    return -(-value // step) * step


class Sizes:
    def __init__(self, height, width, strips):
        self.height, self.width = height, width
        self.rows = up(height + 2 * REACH, 8)
        self.lanes = up(width + 2 * REACH, 128)
        self.span = up(height + KS - 1, 2 * FINE)
        self.phases = self.span // FINE
        self.per = CHUNK // self.span
        self.lines = -(-KS // (self.per * self.phases))
        self.depth = self.lines * CHUNK
        self.sw_rows = 2 * height
        self.r_rows = self.lines * SLOT
        self.one_side = strips <= 2
        self.sent = height + 16 if self.one_side else self.rows
        self.main_at = self.sw_rows + self.r_rows
        self.halo_at = self.main_at + self.sent
        self.groups = self.sent // 8
        self.halo_rows = up(self.groups * 32, width) // width * 8
        self.total = self.halo_at + self.halo_rows

    def place(self, column):
        slot, phase = column // self.phases, column % self.phases
        return slot // self.per * CHUNK + (slot % self.per * self.phases + phase) * FINE


def iota(shape, axis):
    return lax.broadcasted_iota(jnp.int32, shape, axis)


def whole(value):
    return jnp.floor(value + 0.5)


def exponent_of(value):
    return jnp.floor(jnp.log2(value))


def join(mantissa, exponent):
    return (1.0 + mantissa * 2.0**-7) * jnp.exp2(exponent)


def part(value):
    exponent = jnp.floor(jnp.log2(value) + 0.003)
    return whole((value * jnp.exp2(-exponent) - 1.0) * 128.0), exponent


def encode_weight(weight):
    code = jnp.minimum(whole(weight * 65536.0), 32767.0)
    half = jnp.floor(code * 0.5)
    exponent = jnp.floor(half * 2.0**-7)
    value = join(half - exponent * 128.0, exponent - 63.0)
    return jnp.where(code > 2.0 * half, -value, value)


def decode_weight(value):
    mantissa, exponent = part(jnp.abs(value))
    code = (exponent + 63.0) * 256.0 + mantissa * 2.0
    return jnp.where(value < 0.0, code + 1.0, code) * 2.0**-16


def encode_science(science):
    size = jnp.abs(science)
    power = jnp.clip(exponent_of(jnp.maximum(size, 2.0**-30)), -24.0, 2.0)
    fine = power >= -12.0
    steps = jnp.where(fine, 2048.0, 128.0)
    code = jnp.clip(whole((size * jnp.exp2(-power) - 1.0) * steps), 0.0, steps - 1.0)
    high = jnp.floor(code * 0.0625)
    exponent = jnp.where(fine, power * 16.0 + (code - 16.0 * high) + 192.0, power + 264.0)
    value = join(jnp.where(fine, high, code), exponent - 125.0)
    value = jnp.where(size < 2.0**-24, 0.0, value)
    return jnp.where(science < 0.0, -value, value)


def decode_science(value):
    size = jnp.abs(value)
    mantissa, exponent = part(jnp.maximum(size, 2.0**-125))
    exponent = exponent + 125.0
    high = jnp.floor(exponent * 0.0625)
    fine = exponent < 240.0
    low = jnp.where(fine, exponent - 16.0 * high, 0.0)
    power = jnp.where(fine, high - 12.0, exponent - 264.0)
    size = jnp.where(size == 0.0, 0.0, (2048.0 + mantissa * 16.0 + low) * 2.0**-11 * jnp.exp2(power))
    return jnp.where(value < 0.0, -size, size)


def prepare(sz, n_epoch, tiles, count, nsel):
    lanes = count * SLOT
    per_owner = count // n_epoch
    width = sz.lines * CHUNK
    nbasis = 128

    def body(*refs):
        sources, refs = refs[:9], refs[9:]
        r_out, sw_out, own_out, sci_out, weight_out = refs[:5]
        var, mask, inter, offs, index, coef, basis, table, place, sems = refs[5:]
        targets = [own_out, sci_out, var, mask, inter, offs, index, coef, basis]
        copies = [
            pltpu.make_async_copy(source, target, sems.at[i])
            for i, (source, target) in enumerate(zip(sources, targets))
        ]
        for copy in reversed(copies):
            copy.start()
        me, _ = here("epoch")
        table[...] = jnp.zeros(table.shape, f32)
        col = iota((FINE, width), 0)
        base = iota((FINE, width), 1) - sz.place(col)
        base = jnp.where(col < KS, base, -1)
        for a in range(0, KS + 1, 2):
            pair = jnp.concatenate([(base == a).astype(f32), (base == a + 1).astype(f32)], axis=0)
            if a + 1 == KS:
                pair = jnp.where(iota(pair.shape, 0) < FINE, pair, 0.0)
            place[a * FINE : (a + 2) * FINE] = pair.astype(bf16)
        for copy in reversed(copies[4:]):
            copy.wait()
        for a in range(KS):
            table[a * FINE : a * FINE + KS, : basis.shape[2]] = basis[a]
        chosen = jnp.concatenate([index[e : e + 1, :] for e in range(count)], axis=1)
        onehot = (iota((nbasis, count * nsel), 0) == chosen).astype(f32)
        blocks = []
        for e in range(count):
            mine = jnp.concatenate([coef[:, e, :], jnp.zeros((SLOT - NPOLY, nsel), f32)], axis=0)
            wide = jnp.concatenate([mine] * count, axis=1)
            blocks.append(jnp.where(iota(wide.shape, 1) // nsel == e, wide, 0.0))
        combine = jnp.concatenate(blocks, axis=0)
        mixing = lax.dot_general(
            onehot, combine, (((1,), (1,)), ((), ())), precision=highest, preferred_element_type=f32
        )
        images = jnp.dot(table[...], mixing, precision=highest, preferred_element_type=f32)
        rows = lax.dot_general(
            images.astype(bf16), place[...], (((0,), (0,)), ((), ())), preferred_element_type=f32
        )
        for copy in reversed(copies[:4]):
            copy.wait()
        for e in range(count):
            weight_out[e] = mask[e].astype(f32) / var[e]
            science = jnp.where(mask[e] == 0, 0.0, sci_out[e])
            top = jnp.max(jnp.abs(science), axis=(0, 1), keepdims=True)
            scale = jnp.exp2(exponent_of(jnp.maximum(top, 2.0**-100)) - 2.0).astype(bf16).astype(f32)
            science = science / scale
            parts = [encode_science(science), encode_weight(weight_out[e])]
            sw_out[e] = jnp.concatenate(parts, axis=0).astype(bf16)
            mine = rows[e * SLOT : (e + 1) * SLOT]
            mine = jnp.concatenate(
                [mine[:, i * CHUNK : (i + 1) * CHUNK] for i in range(sz.lines)], axis=0
            )
            tile = inter[e // per_owner * count + me * per_owner + e % per_owner] - me * tiles
            tile = jnp.clip(tile, 0, tiles - 1).astype(f32)
            down, across = offs[0:1, e : e + 1].astype(f32), offs[1:2, e : e + 1].astype(f32)
            spare, spot = iota(mine.shape, 0) == NPOLY, iota(mine.shape, 1)
            for lane, value in enumerate((down, across, tile, scale)):
                mine = jnp.where(spare & (spot == lane), value, mine)
            r_out[e] = mine.astype(bf16)

    hbm, vmem = pl.BlockSpec(memory_space=pltpu.HBM), pl.BlockSpec(memory_space=pltpu.VMEM)
    shape = (count, sz.height, sz.width)

    def call(*sources):
        template, _, _, _, inter, offs, index, coef, basis = sources
        return pl.pallas_call(
            body,
            in_specs=[hbm] * 9,
            out_specs=(vmem,) * 5,
            out_shape=(
                jax.ShapeDtypeStruct((count, sz.r_rows, CHUNK), bf16),
                jax.ShapeDtypeStruct((count, sz.sw_rows, sz.width), bf16),
                jax.ShapeDtypeStruct(template.shape, bf16),
                jax.ShapeDtypeStruct(shape, f32),
                jax.ShapeDtypeStruct(shape, f32),
            ),
            scratch_shapes=[
                pltpu.VMEM(shape, f32),
                pltpu.VMEM(shape, jnp.int32),
                pltpu.SMEM(inter.shape, jnp.int32),
                pltpu.VMEM(offs.shape, jnp.int32),
                pltpu.VMEM(index.shape, jnp.int32),
                pltpu.VMEM(coef.shape, f32),
                pltpu.VMEM(basis.shape, f32),
                pltpu.VMEM(((KS + 1) * FINE, nbasis), f32),
                pltpu.VMEM(((KS + 1) * FINE, width), bf16),
                pltpu.SemaphoreType.DMA((9,)),
            ],
            compiler_params=pltpu.CompilerParams(vmem_limit_bytes=VMEM_LIMIT),
            cost_estimate=pl.CostEstimate(
                flops=1_000_000_000, bytes_accessed=6_000_000, transcendentals=0
            ),
            name="prepare",
        )(*[pltpu.with_memory_space_constraint(source, pltpu.HBM) for source in sources])

    return call


def here(axis):
    return lax.axis_index(axis), lax.axis_size(axis)


def partner(me, n, k, back):
    if n & (n - 1) == 0:
        return me ^ k
    return (me + (n - k if back else k)) % n


def pack(sz, n_epoch, tiles, count, peers):
    per_owner = count // n_epoch
    h, w = sz.height, sz.width

    def body(own, low, high, left, low_left, high_left, right, low_right, high_right, sw, r, *outs):
        slabs, sends = outs[0], outs[1:]
        me, _ = here("epoch")
        strip, strips = here("strip")
        band, bands = here("band")

        def column(middle, above, below, t, cut):
            above = jnp.where(strip > 0, above[t, h - 16 :, cut].astype(f32), 0.0)
            above = jnp.where(iota(above.shape, 0) >= 16 - REACH, above, 0.0)
            below = jnp.where(strip < strips - 1, below[t, :16, cut].astype(f32), 0.0)
            below = jnp.where(iota(below.shape, 0) < REACH, below, 0.0)
            parts = [middle[t, :, cut].astype(f32), below]
            gap = sz.rows - h - 32
            if gap:
                parts.append(jnp.zeros((gap, below.shape[1]), f32))
            return jnp.concatenate(parts + [above], axis=0)

        whole_slabs = []
        for t in range(tiles):
            parts = [column(own, low, high, t, slice(None))]
            before = column(left, low_left, high_left, t, slice(w - 128, w))
            after = column(right, low_right, high_right, t, slice(0, 128))
            lane = iota(before.shape, 1)
            before = jnp.where((lane >= 128 - REACH) & (band > 0), before, 0.0)
            after = jnp.where((lane < REACH) & (band < bands - 1), after, 0.0)
            if sz.lanes - w == 128:
                parts.append(before + after)
            else:
                gap = sz.lanes - w - 256
                parts += [after] + ([jnp.zeros((sz.rows, gap), f32)] if gap else []) + [before]
            slab = jnp.concatenate(parts, axis=1)
            slabs[t] = slab.astype(bf16)
            if sz.one_side:
                side = jnp.where(strip == 0, slab[h : h + 16], slab[sz.rows - 16 :])
                slab = jnp.concatenate([slab[:h], side], axis=0)
            whole_slabs.append(slab)
        for k, out in zip(peers, sends):
            q = partner(me, n_epoch, k, False)
            for c in range(per_owner):
                mine = q * per_owner + c
                lines = r[mine].astype(f32)
                covered = lines[NPOLY : NPOLY + 1, 2:3]
                slab = whole_slabs[0]
                for t in range(1, tiles):
                    pick = jnp.broadcast_to(covered, slab.shape) == t
                    slab = jnp.where(pick, whole_slabs[t], slab)
                halo = slab[:, sz.lanes - 128 :]
                if sz.lanes - w != 128:
                    halo = halo + slab[:, w : w + 128]
                bits = []
                for part in range(sz.halo_rows // 8 * (w // 128)):
                    piece = jnp.zeros((8, 128), f32)
                    for slot in range(4):
                        g = part * 4 + slot
                        if g < sz.groups:
                            piece = piece + pltpu.roll(halo[g * 8 : g * 8 + 8], slot * 32 + REACH, 1)
                    bits.append(piece)
                wide = w // 128
                bits = [
                    jnp.concatenate(bits[i * wide : (i + 1) * wide], axis=1)
                    for i in range(sz.halo_rows // 8)
                ]
                parts = [sw[mine].astype(f32), lines, slab[:, :w]] + bits
                out[c] = jnp.concatenate(parts, axis=0).astype(bf16)

    vmem = pl.BlockSpec(memory_space=pltpu.VMEM)
    return pl.pallas_call(
        body,
        in_specs=[vmem] * 11,
        out_shape=(jax.ShapeDtypeStruct((tiles, sz.rows, sz.lanes), bf16),)
        + tuple(jax.ShapeDtypeStruct((per_owner, sz.total, w), bf16) for _ in peers),
        compiler_params=pltpu.CompilerParams(vmem_limit_bytes=VMEM_LIMIT),
        cost_estimate=pl.CostEstimate(flops=1_000_000, bytes_accessed=1_000_000, transcendentals=0),
        name="pack",
    )


def models(sz, n_epoch, tiles, count, ks, first, last, carried):
    per_owner = count // n_epoch
    h, w = sz.height, sz.width
    total_models = (2 * len(ks) + first) * per_owner

    def body(sci, weight, r, slabs, *refs):
        refs = list(refs)
        ready = None if first else refs.pop(0)
        pays = [refs.pop(0) for _ in ks]
        before = [] if first else [refs.pop(0) for _ in range(2)]
        done = [refs.pop(0) for _ in carried]
        if last:
            resid_out, coadd_out = refs.pop(0), refs.pop(0)
        else:
            numer_out, denom_out = refs.pop(0), refs.pop(0)
            resid_outs = [refs.pop(0) for _ in range(len(ks) + first)]
            ready_out = refs.pop(0) if first else None
        rhs, lhs, *refs = refs
        me, _ = here("epoch")
        strip, strips = here("strip")
        band, bands = here("band")

        copies = []

        def send(source, target):
            copies.append(pltpu.make_async_copy(source, target, out_sems.at[len(copies)]))
            copies[-1].start()

        if last:
            fresh, sums, out_sems = refs
            for k, value in zip(carried, done):
                q = me if k == 0 else partner(me, n_epoch, k, True)
                send(value, resid_out.at[pl.ds(q * per_owner, per_owner)])

        jobs = []

        def job(kind, q, c, slab, lines):
            mine = q * per_owner + c
            own = lines if kind == "local" else r[mine].astype(f32)
            scalars = [lines[NPOLY, lane].astype(jnp.int32) for lane in range(2)]
            tile = None if kind == "sent" else own[NPOLY, 2].astype(jnp.int32)
            jobs.append((kind, mine, slab, lines, scalars, tile, own))

        if first:
            for c in range(per_owner):
                job("local", me, c, None, r[me * per_owner + c].astype(f32))
        for k, pay in zip(ks, pays):
            q = partner(me, n_epoch, k, True)
            for c in range(per_owner):
                got = pay[c].astype(f32)
                job("owned", q, c, got, got[sz.sw_rows : sz.main_at])
            for c in range(per_owner):
                job("sent", q, c, pay[c].astype(f32), r[q * per_owner + c].astype(f32))

        row = (strip * h + iota((h, 128), 0)).astype(f32)
        r_unit = (2.0 * row + 1.0) / (h * strips) - 1.0
        r_units = jnp.concatenate([r_unit] * (sz.lanes // 128), axis=1)
        spot = iota((SLOT, CHUNK), 1)
        filled = (spot % sz.span < FINE) & (spot < sz.per * sz.span)
        c_units = []
        for i in range(sz.phases):
            col = (band * w + iota((8, sz.lanes), 1) - i).astype(f32)
            col = (2.0 * col + 1.0) / (w * bands) - 1.0
            c_units.append(jnp.concatenate([col] * (h // 8), axis=0))
        for slot in range(2):
            for line in range(sz.lines):
                at = line * CHUNK + sz.per * sz.span
                if at < (line + 1) * CHUNK:
                    rhs[slot, at : (line + 1) * CHUNK] = jnp.zeros(((line + 1) * CHUNK - at, sz.lanes), bf16)

        def windows(turn, slab, scalars):
            window = rhs.at[turn % 2]
            down, across = scalars
            slab = pltpu.roll(slab, lax.rem(sz.rows + HALF - down, sz.rows), 0)[: sz.span]
            slab = pltpu.roll(slab.astype(bf16), lax.rem(sz.lanes + HALF - across, sz.lanes), 1)
            for slot in range(sz.lines * sz.per):
                moved = pltpu.roll(slab, sz.lanes - slot * sz.phases, 1) if slot else slab
                at = slot // sz.per * CHUNK + slot % sz.per * sz.span
                window[at : at + sz.span] = moved

        def band_matrix(turn, lines):
            band_rows = lhs.at[turn % 2]
            for i in range(sz.phases * sz.lines):
                phase, line = divmod(i, sz.lines)
                part = lines[line * SLOT : (line + 1) * SLOT]
                if phase:
                    part = pltpu.roll(part, CHUNK - phase * FINE, 1)
                part = jnp.where(filled, part, 0.0)
                for p in range(NPOLY):
                    at = (phase * NPOLY + p) * h
                    band_rows[at : at + h, line * CHUNK : (line + 1) * CHUNK] = pltpu.roll(
                        jnp.broadcast_to(part[p : p + 1], (h, CHUNK)), 0, 1, stride=1, stride_axis=0
                    )

        def chunk_image(turn, i, matrix):
            at = i * NPOLY * h
            wide = sz.lanes if i else w
            conv = jnp.dot(
                matrix[at : at + NPOLY * h].astype(bf16),
                rhs[turn % 2, :, :wide],
                preferred_element_type=f32,
            )
            conv = [conv[p * h : (p + 1) * h] for p in range(NPOLY)]
            c_unit, r_unit = c_units[i][:, :wide], r_units[:, :wide]
            return (
                conv[0]
                + r_unit * (conv[1] + r_unit * conv[3] + c_unit * conv[4])
                + c_unit * (conv[2] + c_unit * conv[5])
            )

        def sent_slab(got):
            main, halo = got[sz.main_at : sz.halo_at], got[sz.halo_at :]
            wide = w // 128
            bits = []
            for g in range(sz.groups):
                part, slot = g // 4, g % 4
                line, side = part // wide, part % wide
                piece = halo[line * 8 : line * 8 + 8, side * 128 : side * 128 + 128]
                bits.append(pltpu.roll(piece, (256 - slot * 32 - REACH) % 128, 1))
            halo = jnp.concatenate(bits, axis=0)
            lane = iota(halo.shape, 1)
            halo = jnp.where((lane < REACH) | (lane >= 128 - REACH), halo, 0.0)
            if sz.lanes - w != 128:
                gap = sz.lanes - w - 256
                pieces = [jnp.where(lane < 64, halo, 0.0)]
                if gap:
                    pieces.append(jnp.zeros((sz.sent, gap), f32))
                halo = jnp.concatenate(pieces + [jnp.where(lane < 64, 0.0, halo)], axis=1)
            slab = jnp.concatenate([main, halo], axis=1)
            if sz.one_side:
                side, none = slab[h:], jnp.zeros((sz.rows - h - 32, sz.lanes), f32)
                below, above = jnp.where(strip == 0, side, 0.0), jnp.where(strip == 0, 0.0, side)
                slab = [slab[:h], below, none, above] if none.size else [slab[:h], below, above]
                slab = jnp.concatenate(slab, axis=0)
            return slab

        numer = [before[0][t] if before else jnp.zeros((h, w), f32) for t in range(tiles)]
        denom = [before[1][t] if before else jnp.zeros((h, w), f32) for t in range(tiles)]
        kept = 0
        settled = max(turn for turn, job in enumerate(jobs) if job[0] != "sent")
        images = []
        for turn in range(0, len(jobs), 2):
            pair = list(enumerate(jobs))[turn : turn + 2]
            for at, (kind, mine, got, lines, scalars, tile, own) in pair:
                if kind != "sent":
                    band_matrix(at, lines)
            for at, (kind, mine, got, lines, scalars, tile, own) in pair:
                windows(at, sent_slab(got) if kind == "sent" else slabs[tile].astype(f32), scalars)
            parts = [None for _ in pair]
            for i in reversed(range(sz.phases)):
                for slot, (at, _) in enumerate(pair):
                    value = chunk_image(at, i, ready.at[pair[slot][1][1]] if pair[slot][1][0] == "sent" else lhs.at[at % 2])
                    value = pltpu.roll(value, sz.lanes - i, 1)[:, :w] if i else value
                    parts[slot] = value if parts[slot] is None else parts[slot] + value
            images += parts
        for turn, (kind, mine, got, lines, scalars, tile, own) in enumerate(jobs):
            image = images[turn]
            if kind == "owned":
                scale = jnp.broadcast_to(lines[NPOLY : NPOLY + 1, 3:4], (h, w))
                science, seen = decode_science(got[:h]) * scale, decode_weight(got[h : 2 * h])
            else:
                science, seen = sci[mine], weight[mine]
                if last:
                    fresh[kept] = science - image
                    send(fresh.at[kept], resid_out.at[mine])
                else:
                    resid_outs[kept // per_owner][kept % per_owner] = science - image
                kept += 1
            if kind != "sent":
                change = seen * (science - image)
                covered = jnp.broadcast_to(own[NPOLY : NPOLY + 1, 2:3], (h, w))
                for t in range(tiles):
                    numer[t] = numer[t] + jnp.where(covered == t, change, 0.0)
                    denom[t] = denom[t] + jnp.where(covered == t, seen, 0.0)
            if turn == settled:
                for t in range(tiles):
                    if last:
                        sums[t] = numer[t] / (denom[t] + 1.0)
                        send(sums.at[t], coadd_out.at[t])
                    else:
                        numer_out[t], denom_out[t] = numer[t], denom[t]
        for copy in copies:
            copy.wait()
        if first:
            for e in range(count):
                band_matrix(0, r[e].astype(f32))
                ready_out[e] = lhs[0].astype(bf16)

    image = jax.ShapeDtypeStruct((per_owner, h, w), f32)
    sums = jax.ShapeDtypeStruct((tiles, h, w), f32)
    if last:
        out_shape = (jax.ShapeDtypeStruct((count, h, w), f32), sums)
    else:
        out_shape = (sums, sums) + (image,) * (len(ks) + first)
        if first:
            out_shape += (jax.ShapeDtypeStruct((count, sz.phases * NPOLY * h, sz.depth), bf16),)
    vmem, hbm = pl.BlockSpec(memory_space=pltpu.VMEM), pl.BlockSpec(memory_space=pltpu.HBM)
    scratch = [
        pltpu.VMEM((2, sz.depth, sz.lanes), bf16),
        pltpu.VMEM((2, sz.phases * NPOLY * h, sz.depth), f32),
    ]
    if last:
        new = len(ks) * per_owner
        scratch += [
            pltpu.VMEM((new, h, w), f32),
            pltpu.VMEM((tiles, h, w), f32),
            pltpu.SemaphoreType.DMA((len(carried) + new + tiles,)),
        ]
    return pl.pallas_call(
        body,
        in_specs=[vmem] * (4 + len(ks) + (0 if first else 3) + len(carried)),
        out_specs=(hbm if last else vmem,) * len(out_shape),
        out_shape=out_shape,
        scratch_shapes=scratch,
        compiler_params=pltpu.CompilerParams(vmem_limit_bytes=VMEM_LIMIT),
        cost_estimate=pl.CostEstimate(
            flops=total_models * 400_000_000, bytes_accessed=1_000_000, transcendentals=0
        ),
        name="models",
    )


def surroundings(block):
    strips, bands = lax.axis_size("strip"), lax.axis_size("band")
    sent, found = {}, {}
    for down in (-1, 0, 1):
        for across in (-1, 0, 1):
            if down == 0 and across == 0:
                continue
            pairs = []
            for s in range(strips):
                for b in range(bands):
                    to_s = s ^ 1 if strips == 2 and down else s - down
                    to_b = b ^ 1 if bands == 2 and across else b - across
                    if 0 <= to_s < strips and 0 <= to_b < bands:
                        pairs.append((s * bands + b, to_s * bands + to_b))
            key = tuple(pairs)
            if key and key not in sent:
                sent[key] = lax.ppermute(block, ("strip", "band"), pairs)
            found[down, across] = key
    return {step: sent.get(key, block) for step, key in found.items()}


def local(
    template, science, variance, bad_mask, intersection, offsets, basis_index, coefficients, basis
):
    n_epoch = lax.axis_size("epoch")
    tiles = template.shape[0]
    count, height, width = science.shape
    sz = Sizes(height, width, lax.axis_size("strip"))
    around = surroundings(template)
    r, sw, own, sci, weight = prepare(sz, n_epoch, tiles, count, basis_index.shape[1])(
        template,
        science,
        variance,
        bad_mask,
        intersection,
        offsets.T,
        basis_index,
        coefficients.transpose(2, 0, 1),
        basis.transpose(1, 2, 0),
    )
    around[0, 0] = own
    peers = list(range(1, n_epoch))
    order = peers[-1:] + peers[:-1]
    slabs, *sends = pack(sz, n_epoch, tiles, count, peers)(
        *[around[down, across] for across in (0, -1, 1) for down in (0, -1, 1)], sw, r
    )
    pays = {}
    for k, send in reversed(list(zip(peers, sends))):
        pairs = [(i, partner(i, n_epoch, k, False)) for i in range(n_epoch)]
        pays[k] = lax.ppermute(send, "epoch", pairs)
    stages = [[]] + [[k] for k in order]
    sums, carried, ready = [], [], []
    for i, ks in enumerate(stages):
        first, last = i == 0, i == len(stages) - 1
        kept = [k for k, _ in carried] if last else []
        out = models(sz, n_epoch, tiles, count, ks, first, last, kept)(
            sci,
            weight,
            r,
            slabs,
            *ready,
            *[pays[k] for k in ks],
            *sums,
            *([value for _, value in carried] if last else []),
        )
        if last:
            return out
        sums = list(out[:2])
        if first:
            *out, matrices = out
            ready = [matrices]
        carried += list(zip(list(ks) + ([0] if first else []), out[2:]))


def solution(mesh):
    in_specs = (
        P(("groups", "epoch"), "strip", "band"),
        P(("groups", "epoch"), "strip", "band"),
        P(("groups", "epoch"), "strip", "band"),
        P(("groups", "epoch"), "strip", "band"),
        P("groups"),
        P(("groups", "epoch"), None),
        P(("groups", "epoch"), None),
        P(("groups", "epoch"), None, None),
        P(),
    )
    out_specs = (P(("groups", "epoch"), "strip", "band"), P(("groups", "epoch"), "strip", "band"))
    return jax.shard_map(local, mesh=mesh, in_specs=in_specs, out_specs=out_specs, check_vma=False)
```

```python
import jax
import jax.numpy as jnp
from jax import lax
from jax.experimental import pallas as pl
from jax.experimental.pallas import tpu as pltpu
from jax.sharding import PartitionSpec as P

KS = 19
HALF = 9
SHIFT = 4
NPOLY = 6
REACH = HALF + SHIFT
SLOT = 8
CHUNK = 256
FINE = 24
VMEM_LIMIT = 24 * 1024 * 1024

highest = lax.Precision.HIGHEST
f32 = jnp.float32
bf16 = jnp.bfloat16


def up(value, step):
    return -(-value // step) * step


class Sizes:
    def __init__(self, height, width, strips):
        self.height, self.width = height, width
        self.rows = up(height + 2 * REACH, 8)
        self.lanes = up(width + 2 * REACH, 128)
        self.span = up(height + KS - 1, 2 * FINE)
        self.phases = self.span // FINE
        self.per = CHUNK // self.span
        self.lines = -(-KS // (self.per * self.phases))
        self.depth = self.lines * CHUNK
        self.sw_rows = 2 * height
        self.r_rows = self.lines * SLOT
        self.one_side = strips <= 2
        self.sent = height + 16 if self.one_side else self.rows
        self.main_at = self.sw_rows + self.r_rows
        self.halo_at = self.main_at + self.sent
        self.groups = self.sent // 8
        self.halo_rows = up(self.groups * 32, width) // width * 8
        self.total = self.halo_at + self.halo_rows

    def place(self, column):
        slot, phase = column // self.phases, column % self.phases
        return slot // self.per * CHUNK + (slot % self.per * self.phases + phase) * FINE


def iota(shape, axis):
    return lax.broadcasted_iota(jnp.int32, shape, axis)


def whole(value):
    return jnp.floor(value + 0.5)


def exponent_of(value):
    return jnp.floor(jnp.log2(value))


def join(mantissa, exponent):
    return (1.0 + mantissa * 2.0**-7) * jnp.exp2(exponent)


def part(value):
    exponent = jnp.floor(jnp.log2(value) + 0.003)
    return whole((value * jnp.exp2(-exponent) - 1.0) * 128.0), exponent


def encode_weight(weight):
    code = jnp.minimum(whole(weight * 65536.0), 32767.0)
    half = jnp.floor(code * 0.5)
    exponent = jnp.floor(half * 2.0**-7)
    value = join(half - exponent * 128.0, exponent - 63.0)
    return jnp.where(code > 2.0 * half, -value, value)


def decode_weight(value):
    mantissa, exponent = part(jnp.abs(value))
    code = (exponent + 63.0) * 256.0 + mantissa * 2.0
    return jnp.where(value < 0.0, code + 1.0, code) * 2.0**-16


def encode_science(science):
    size = jnp.abs(science)
    power = jnp.clip(exponent_of(jnp.maximum(size, 2.0**-30)), -24.0, 2.0)
    fine = power >= -12.0
    steps = jnp.where(fine, 2048.0, 128.0)
    code = jnp.clip(whole((size * jnp.exp2(-power) - 1.0) * steps), 0.0, steps - 1.0)
    high = jnp.floor(code * 0.0625)
    exponent = jnp.where(fine, power * 16.0 + (code - 16.0 * high) + 192.0, power + 264.0)
    value = join(jnp.where(fine, high, code), exponent - 125.0)
    value = jnp.where(size < 2.0**-24, 0.0, value)
    return jnp.where(science < 0.0, -value, value)


def decode_science(value):
    size = jnp.abs(value)
    mantissa, exponent = part(jnp.maximum(size, 2.0**-125))
    exponent = exponent + 125.0
    high = jnp.floor(exponent * 0.0625)
    fine = exponent < 240.0
    low = jnp.where(fine, exponent - 16.0 * high, 0.0)
    power = jnp.where(fine, high - 12.0, exponent - 264.0)
    size = jnp.where(size == 0.0, 0.0, (2048.0 + mantissa * 16.0 + low) * 2.0**-11 * jnp.exp2(power))
    return jnp.where(value < 0.0, -size, size)


def prepare(sz, n_epoch, tiles, count, nsel):
    lanes = count * SLOT
    per_owner = count // n_epoch
    width = sz.lines * CHUNK
    nbasis = 128

    def body(*refs):
        sources, refs = refs[:9], refs[9:]
        r_out, sw_out, own_out, sci_out, weight_out = refs[:5]
        var, mask, inter, offs, index, coef, basis, table, place, sems = refs[5:]
        targets = [own_out, sci_out, var, mask, inter, offs, index, coef, basis]
        copies = [
            pltpu.make_async_copy(source, target, sems.at[i])
            for i, (source, target) in enumerate(zip(sources, targets))
        ]
        for copy in reversed(copies):
            copy.start()
        me, _ = here("epoch")
        table[...] = jnp.zeros(table.shape, f32)
        col = iota((FINE, width), 0)
        base = iota((FINE, width), 1) - sz.place(col)
        base = jnp.where(col < KS, base, -1)
        for a in range(0, KS + 1, 2):
            pair = jnp.concatenate([(base == a).astype(f32), (base == a + 1).astype(f32)], axis=0)
            if a + 1 == KS:
                pair = jnp.where(iota(pair.shape, 0) < FINE, pair, 0.0)
            place[a * FINE : (a + 2) * FINE] = pair.astype(bf16)
        for copy in reversed(copies[4:]):
            copy.wait()
        for a in range(KS):
            table[a * FINE : a * FINE + KS, : basis.shape[2]] = basis[a]
        chosen = jnp.concatenate([index[e : e + 1, :] for e in range(count)], axis=1)
        onehot = (iota((nbasis, count * nsel), 0) == chosen).astype(f32)
        blocks = []
        for e in range(count):
            mine = jnp.concatenate([coef[:, e, :], jnp.zeros((SLOT - NPOLY, nsel), f32)], axis=0)
            wide = jnp.concatenate([mine] * count, axis=1)
            blocks.append(jnp.where(iota(wide.shape, 1) // nsel == e, wide, 0.0))
        combine = jnp.concatenate(blocks, axis=0)
        mixing = lax.dot_general(
            onehot, combine, (((1,), (1,)), ((), ())), precision=highest, preferred_element_type=f32
        )
        images = jnp.dot(table[...], mixing, precision=highest, preferred_element_type=f32)
        rows = lax.dot_general(
            images.astype(bf16), place[...], (((0,), (0,)), ((), ())), preferred_element_type=f32
        )
        for copy in reversed(copies[:4]):
            copy.wait()
        for e in range(count):
            weight_out[e] = mask[e].astype(f32) / var[e]
            science = jnp.where(mask[e] == 0, 0.0, sci_out[e])
            top = jnp.max(jnp.abs(science), axis=(0, 1), keepdims=True)
            scale = jnp.exp2(exponent_of(jnp.maximum(top, 2.0**-100)) - 2.0).astype(bf16).astype(f32)
            science = science / scale
            parts = [encode_science(science), encode_weight(weight_out[e])]
            sw_out[e] = jnp.concatenate(parts, axis=0).astype(bf16)
            mine = rows[e * SLOT : (e + 1) * SLOT]
            mine = jnp.concatenate(
                [mine[:, i * CHUNK : (i + 1) * CHUNK] for i in range(sz.lines)], axis=0
            )
            tile = inter[e // per_owner * count + me * per_owner + e % per_owner] - me * tiles
            tile = jnp.clip(tile, 0, tiles - 1).astype(f32)
            down, across = offs[0:1, e : e + 1].astype(f32), offs[1:2, e : e + 1].astype(f32)
            spare, spot = iota(mine.shape, 0) == NPOLY, iota(mine.shape, 1)
            for lane, value in enumerate((down, across, tile, scale)):
                mine = jnp.where(spare & (spot == lane), value, mine)
            r_out[e] = mine.astype(bf16)

    hbm, vmem = pl.BlockSpec(memory_space=pltpu.HBM), pl.BlockSpec(memory_space=pltpu.VMEM)
    shape = (count, sz.height, sz.width)

    def call(*sources):
        template, _, _, _, inter, offs, index, coef, basis = sources
        return pl.pallas_call(
            body,
            in_specs=[hbm] * 9,
            out_specs=(vmem,) * 5,
            out_shape=(
                jax.ShapeDtypeStruct((count, sz.r_rows, CHUNK), bf16),
                jax.ShapeDtypeStruct((count, sz.sw_rows, sz.width), bf16),
                jax.ShapeDtypeStruct(template.shape, bf16),
                jax.ShapeDtypeStruct(shape, f32),
                jax.ShapeDtypeStruct(shape, f32),
            ),
            scratch_shapes=[
                pltpu.VMEM(shape, f32),
                pltpu.VMEM(shape, jnp.int32),
                pltpu.SMEM(inter.shape, jnp.int32),
                pltpu.VMEM(offs.shape, jnp.int32),
                pltpu.VMEM(index.shape, jnp.int32),
                pltpu.VMEM(coef.shape, f32),
                pltpu.VMEM(basis.shape, f32),
                pltpu.VMEM(((KS + 1) * FINE, nbasis), f32),
                pltpu.VMEM(((KS + 1) * FINE, width), bf16),
                pltpu.SemaphoreType.DMA((9,)),
            ],
            compiler_params=pltpu.CompilerParams(vmem_limit_bytes=VMEM_LIMIT),
            cost_estimate=pl.CostEstimate(
                flops=1_000_000_000, bytes_accessed=6_000_000, transcendentals=0
            ),
            name="prepare",
        )(*[pltpu.with_memory_space_constraint(source, pltpu.HBM) for source in sources])

    return call


def here(axis):
    return lax.axis_index(axis), lax.axis_size(axis)


def partner(me, n, k, back):
    if n & (n - 1) == 0:
        return me ^ k
    return (me + (n - k if back else k)) % n


def pack(sz, n_epoch, tiles, count, peers):
    per_owner = count // n_epoch
    h, w = sz.height, sz.width

    def body(own, low, high, left, low_left, high_left, right, low_right, high_right, sw, r, *outs):
        slabs, sends = outs[0], outs[1:]
        me, _ = here("epoch")
        strip, strips = here("strip")
        band, bands = here("band")

        def column(middle, above, below, t, cut):
            above = jnp.where(strip > 0, above[t, h - 16 :, cut].astype(f32), 0.0)
            above = jnp.where(iota(above.shape, 0) >= 16 - REACH, above, 0.0)
            below = jnp.where(strip < strips - 1, below[t, :16, cut].astype(f32), 0.0)
            below = jnp.where(iota(below.shape, 0) < REACH, below, 0.0)
            parts = [middle[t, :, cut].astype(f32), below]
            gap = sz.rows - h - 32
            if gap:
                parts.append(jnp.zeros((gap, below.shape[1]), f32))
            return jnp.concatenate(parts + [above], axis=0)

        whole_slabs = []
        for t in range(tiles):
            parts = [column(own, low, high, t, slice(None))]
            before = column(left, low_left, high_left, t, slice(w - 128, w))
            after = column(right, low_right, high_right, t, slice(0, 128))
            lane = iota(before.shape, 1)
            before = jnp.where((lane >= 128 - REACH) & (band > 0), before, 0.0)
            after = jnp.where((lane < REACH) & (band < bands - 1), after, 0.0)
            if sz.lanes - w == 128:
                parts.append(before + after)
            else:
                gap = sz.lanes - w - 256
                parts += [after] + ([jnp.zeros((sz.rows, gap), f32)] if gap else []) + [before]
            slab = jnp.concatenate(parts, axis=1)
            slabs[t] = slab.astype(bf16)
            if sz.one_side:
                side = jnp.where(strip == 0, slab[h : h + 16], slab[sz.rows - 16 :])
                slab = jnp.concatenate([slab[:h], side], axis=0)
            whole_slabs.append(slab)
        for k, out in zip(peers, sends):
            q = partner(me, n_epoch, k, False)
            for c in range(per_owner):
                mine = q * per_owner + c
                lines = r[mine].astype(f32)
                covered = lines[NPOLY : NPOLY + 1, 2:3]
                slab = whole_slabs[0]
                for t in range(1, tiles):
                    pick = jnp.broadcast_to(covered, slab.shape) == t
                    slab = jnp.where(pick, whole_slabs[t], slab)
                halo = slab[:, sz.lanes - 128 :]
                if sz.lanes - w != 128:
                    halo = halo + slab[:, w : w + 128]
                bits = []
                for part in range(sz.halo_rows // 8 * (w // 128)):
                    piece = jnp.zeros((8, 128), f32)
                    for slot in range(4):
                        g = part * 4 + slot
                        if g < sz.groups:
                            piece = piece + pltpu.roll(halo[g * 8 : g * 8 + 8], slot * 32 + REACH, 1)
                    bits.append(piece)
                wide = w // 128
                bits = [
                    jnp.concatenate(bits[i * wide : (i + 1) * wide], axis=1)
                    for i in range(sz.halo_rows // 8)
                ]
                out[c, : sz.sw_rows] = sw[mine]
                out[c, sz.sw_rows : sz.main_at] = r[mine]
                out[c, sz.main_at :] = jnp.concatenate([slab[:, :w]] + bits, axis=0).astype(bf16)

    vmem = pl.BlockSpec(memory_space=pltpu.VMEM)
    return pl.pallas_call(
        body,
        in_specs=[vmem] * 11,
        out_shape=(jax.ShapeDtypeStruct((tiles, sz.rows, sz.lanes), bf16),)
        + tuple(jax.ShapeDtypeStruct((per_owner, sz.total, w), bf16) for _ in peers),
        compiler_params=pltpu.CompilerParams(vmem_limit_bytes=VMEM_LIMIT),
        cost_estimate=pl.CostEstimate(flops=1_000_000, bytes_accessed=1_000_000, transcendentals=0),
        name="pack",
    )


def models(sz, n_epoch, tiles, count, ks, first, last, carried):
    per_owner = count // n_epoch
    h, w = sz.height, sz.width
    total_models = (2 * len(ks) + first) * per_owner

    def body(sci, weight, r, slabs, *refs):
        refs = list(refs)
        ready = None if first else refs.pop(0)
        pays = [refs.pop(0) for _ in ks]
        before = [] if first else [refs.pop(0) for _ in range(2)]
        done = [refs.pop(0) for _ in carried]
        if last:
            resid_out, coadd_out = refs.pop(0), refs.pop(0)
        else:
            numer_out, denom_out = refs.pop(0), refs.pop(0)
            resid_outs = [refs.pop(0) for _ in range(len(ks) + first)]
            ready_out = refs.pop(0) if first else None
        rhs, lhs, *refs = refs
        me, _ = here("epoch")
        strip, strips = here("strip")
        band, bands = here("band")

        copies = []

        def send(source, target):
            copies.append(pltpu.make_async_copy(source, target, out_sems.at[len(copies)]))
            copies[-1].start()

        if last:
            fresh, sums, out_sems = refs
            for k, value in zip(carried, done):
                q = me if k == 0 else partner(me, n_epoch, k, True)
                send(value, resid_out.at[pl.ds(q * per_owner, per_owner)])

        jobs = []

        def job(kind, q, c, slab, lines):
            mine = q * per_owner + c
            own = lines if kind == "local" else r[mine].astype(f32)
            scalars = [lines[NPOLY, lane].astype(jnp.int32) for lane in range(2)]
            tile = None if kind == "sent" else own[NPOLY, 2].astype(jnp.int32)
            jobs.append((kind, mine, slab, lines, scalars, tile, own))

        if first:
            for c in range(per_owner):
                job("local", me, c, None, r[me * per_owner + c].astype(f32))
        for k, pay in zip(ks, pays):
            q = partner(me, n_epoch, k, True)
            for c in range(per_owner):
                got = pay[c].astype(f32)
                job("owned", q, c, got, got[sz.sw_rows : sz.main_at])
            for c in range(per_owner):
                job("sent", q, c, pay[c].astype(f32), r[q * per_owner + c].astype(f32))

        row = (strip * h + iota((h, 128), 0)).astype(f32)
        r_unit = (2.0 * row + 1.0) / (h * strips) - 1.0
        r_unit = jnp.concatenate([r_unit] * (sz.lanes // 128), axis=1)
        spot = iota((SLOT, CHUNK), 1)
        filled = (spot % sz.span < FINE) & (spot < sz.per * sz.span)
        c_units = []
        for i in range(sz.phases):
            col = (band * w + iota((8, sz.lanes), 1) - i).astype(f32)
            col = (2.0 * col + 1.0) / (w * bands) - 1.0
            c_units.append(jnp.concatenate([col] * (h // 8), axis=0))
        for slot in range(2):
            for line in range(sz.lines):
                at = line * CHUNK + sz.per * sz.span
                if at < (line + 1) * CHUNK:
                    rhs[slot, at : (line + 1) * CHUNK] = jnp.zeros(((line + 1) * CHUNK - at, sz.lanes), bf16)

        def windows(turn, slab, scalars):
            window = rhs.at[turn % 2]
            down, across = scalars
            slab = pltpu.roll(slab, lax.rem(sz.rows + HALF - down, sz.rows), 0)[: sz.span]
            slab = pltpu.roll(slab.astype(bf16), lax.rem(sz.lanes + HALF - across, sz.lanes), 1)
            for slot in range(sz.lines * sz.per):
                moved = pltpu.roll(slab, sz.lanes - slot * sz.phases, 1) if slot else slab
                at = slot // sz.per * CHUNK + slot % sz.per * sz.span
                window[at : at + sz.span] = moved

        def band_matrix(turn, lines):
            band_rows = lhs.at[turn % 2]
            for i in range(sz.phases * sz.lines):
                phase, line = divmod(i, sz.lines)
                part = lines[line * SLOT : (line + 1) * SLOT]
                if phase:
                    part = pltpu.roll(part, CHUNK - phase * FINE, 1)
                part = jnp.where(filled, part, 0.0)
                for p in range(NPOLY):
                    at = (phase * NPOLY + p) * h
                    band_rows[at : at + h, line * CHUNK : (line + 1) * CHUNK] = pltpu.roll(
                        jnp.broadcast_to(part[p : p + 1], (h, CHUNK)), 0, 1, stride=1, stride_axis=0
                    )

        def chunk_image(turn, i, matrix):
            at = i * NPOLY * h
            conv = jnp.dot(
                matrix[at : at + NPOLY * h].astype(bf16), rhs[turn % 2], preferred_element_type=f32
            )
            conv = [conv[p * h : (p + 1) * h] for p in range(NPOLY)]
            c_unit = c_units[i]
            return (
                conv[0]
                + r_unit * (conv[1] + r_unit * conv[3] + c_unit * conv[4])
                + c_unit * (conv[2] + c_unit * conv[5])
            )

        def sent_slab(got):
            main, halo = got[sz.main_at : sz.halo_at], got[sz.halo_at :]
            wide = w // 128
            bits = []
            for g in range(sz.groups):
                part, slot = g // 4, g % 4
                line, side = part // wide, part % wide
                piece = halo[line * 8 : line * 8 + 8, side * 128 : side * 128 + 128]
                bits.append(pltpu.roll(piece, (256 - slot * 32 - REACH) % 128, 1))
            halo = jnp.concatenate(bits, axis=0)
            lane = iota(halo.shape, 1)
            halo = jnp.where((lane < REACH) | (lane >= 128 - REACH), halo, 0.0)
            if sz.lanes - w != 128:
                gap = sz.lanes - w - 256
                pieces = [jnp.where(lane < 64, halo, 0.0)]
                if gap:
                    pieces.append(jnp.zeros((sz.sent, gap), f32))
                halo = jnp.concatenate(pieces + [jnp.where(lane < 64, 0.0, halo)], axis=1)
            slab = jnp.concatenate([main, halo], axis=1)
            if sz.one_side:
                side, none = slab[h:], jnp.zeros((sz.rows - h - 32, sz.lanes), f32)
                below, above = jnp.where(strip == 0, side, 0.0), jnp.where(strip == 0, 0.0, side)
                slab = [slab[:h], below, none, above] if none.size else [slab[:h], below, above]
                slab = jnp.concatenate(slab, axis=0)
            return slab

        numer = [before[0][t] if before else jnp.zeros((h, w), f32) for t in range(tiles)]
        denom = [before[1][t] if before else jnp.zeros((h, w), f32) for t in range(tiles)]
        kept = 0
        settled = max(turn for turn, job in enumerate(jobs) if job[0] != "sent")
        images = []
        for turn in range(0, len(jobs), 2):
            pair = list(enumerate(jobs))[turn : turn + 2]
            for at, (kind, mine, got, lines, scalars, tile, own) in pair:
                if kind != "sent":
                    band_matrix(at, lines)
            for at, (kind, mine, got, lines, scalars, tile, own) in pair:
                windows(at, sent_slab(got) if kind == "sent" else slabs[tile].astype(f32), scalars)
            parts = [None for _ in pair]
            for i in reversed(range(sz.phases)):
                for slot, (at, _) in enumerate(pair):
                    value = chunk_image(at, i, ready.at[pair[slot][1][1]] if pair[slot][1][0] == "sent" else lhs.at[at % 2])
                    value = pltpu.roll(value, sz.lanes - i, 1) if i else value
                    parts[slot] = value if parts[slot] is None else parts[slot] + value
            images += [part[:, :w] for part in parts]
        for turn, (kind, mine, got, lines, scalars, tile, own) in enumerate(jobs):
            image = images[turn]
            if kind == "owned":
                scale = jnp.broadcast_to(lines[NPOLY : NPOLY + 1, 3:4], (h, w))
                science, seen = decode_science(got[:h]) * scale, decode_weight(got[h : 2 * h])
            else:
                science, seen = sci[mine], weight[mine]
                if last:
                    fresh[kept] = science - image
                    send(fresh.at[kept], resid_out.at[mine])
                else:
                    resid_outs[kept // per_owner][kept % per_owner] = science - image
                kept += 1
            if kind != "sent":
                change = seen * (science - image)
                covered = jnp.broadcast_to(own[NPOLY : NPOLY + 1, 2:3], (h, w))
                for t in range(tiles):
                    numer[t] = numer[t] + jnp.where(covered == t, change, 0.0)
                    denom[t] = denom[t] + jnp.where(covered == t, seen, 0.0)
            if turn == settled:
                for t in range(tiles):
                    if last:
                        sums[t] = numer[t] / (denom[t] + 1.0)
                    else:
                        numer_out[t], denom_out[t] = numer[t], denom[t]
                if last:
                    send(sums, coadd_out)
        for copy in copies:
            copy.wait()
        if first:
            for e in range(count):
                band_matrix(0, r[e].astype(f32))
                ready_out[e] = lhs[0].astype(bf16)

    image = jax.ShapeDtypeStruct((per_owner, h, w), f32)
    sums = jax.ShapeDtypeStruct((tiles, h, w), f32)
    if last:
        out_shape = (jax.ShapeDtypeStruct((count, h, w), f32), sums)
    else:
        out_shape = (sums, sums) + (image,) * (len(ks) + first)
        if first:
            out_shape += (jax.ShapeDtypeStruct((count, sz.phases * NPOLY * h, sz.depth), bf16),)
    vmem, hbm = pl.BlockSpec(memory_space=pltpu.VMEM), pl.BlockSpec(memory_space=pltpu.HBM)
    scratch = [
        pltpu.VMEM((2, sz.depth, sz.lanes), bf16),
        pltpu.VMEM((2, sz.phases * NPOLY * h, sz.depth), f32),
    ]
    if last:
        new = len(ks) * per_owner
        scratch += [
            pltpu.VMEM((new, h, w), f32),
            pltpu.VMEM((tiles, h, w), f32),
            pltpu.SemaphoreType.DMA((len(carried) + new + 1,)),
        ]
    return pl.pallas_call(
        body,
        in_specs=[vmem] * (4 + len(ks) + (0 if first else 3) + len(carried)),
        out_specs=(hbm if last else vmem,) * len(out_shape),
        out_shape=out_shape,
        scratch_shapes=scratch,
        compiler_params=pltpu.CompilerParams(vmem_limit_bytes=VMEM_LIMIT),
        cost_estimate=pl.CostEstimate(
            flops=total_models * 400_000_000, bytes_accessed=1_000_000, transcendentals=0
        ),
        name="models",
    )


def surroundings(block):
    strips, bands = lax.axis_size("strip"), lax.axis_size("band")
    sent, found = {}, {}
    for down in (-1, 0, 1):
        for across in (-1, 0, 1):
            if down == 0 and across == 0:
                continue
            pairs = []
            for s in range(strips):
                for b in range(bands):
                    to_s = s ^ 1 if strips == 2 and down else s - down
                    to_b = b ^ 1 if bands == 2 and across else b - across
                    if 0 <= to_s < strips and 0 <= to_b < bands:
                        pairs.append((s * bands + b, to_s * bands + to_b))
            key = tuple(pairs)
            if key and key not in sent:
                sent[key] = lax.ppermute(block, ("strip", "band"), pairs)
            found[down, across] = key
    return {step: sent.get(key, block) for step, key in found.items()}


def local(
    template, science, variance, bad_mask, intersection, offsets, basis_index, coefficients, basis
):
    n_epoch = lax.axis_size("epoch")
    tiles = template.shape[0]
    count, height, width = science.shape
    sz = Sizes(height, width, lax.axis_size("strip"))
    around = surroundings(template)
    r, sw, own, sci, weight = prepare(sz, n_epoch, tiles, count, basis_index.shape[1])(
        template,
        science,
        variance,
        bad_mask,
        intersection,
        offsets.T,
        basis_index,
        coefficients.transpose(2, 0, 1),
        basis.transpose(1, 2, 0),
    )
    around[0, 0] = own
    peers = list(range(1, n_epoch))
    order = peers[-1:] + peers[:-1]
    slabs, *sends = pack(sz, n_epoch, tiles, count, peers)(
        *[around[down, across] for across in (0, -1, 1) for down in (0, -1, 1)], sw, r
    )
    pays = {}
    for k, send in reversed(list(zip(peers, sends))):
        pairs = [(i, partner(i, n_epoch, k, False)) for i in range(n_epoch)]
        pays[k] = lax.ppermute(send, "epoch", pairs)
    stages = [[]] + [[k] for k in order]
    sums, carried, ready = [], [], []
    for i, ks in enumerate(stages):
        first, last = i == 0, i == len(stages) - 1
        kept = [k for k, _ in carried] if last else []
        out = models(sz, n_epoch, tiles, count, ks, first, last, kept)(
            sci,
            weight,
            r,
            slabs,
            *ready,
            *[pays[k] for k in ks],
            *sums,
            *([value for _, value in carried] if last else []),
        )
        if last:
            return out
        sums = list(out[:2])
        if first:
            *out, matrices = out
            ready = [matrices]
        carried += list(zip(list(ks) + ([0] if first else []), out[2:]))


def solution(mesh):
    in_specs = (
        P(("groups", "epoch"), "strip", "band"),
        P(("groups", "epoch"), "strip", "band"),
        P(("groups", "epoch"), "strip", "band"),
        P(("groups", "epoch"), "strip", "band"),
        P("groups"),
        P(("groups", "epoch"), None),
        P(("groups", "epoch"), None),
        P(("groups", "epoch"), None, None),
        P(),
    )
    out_specs = (P(("groups", "epoch"), "strip", "band"), P(("groups", "epoch"), "strip", "band"))
    return jax.shard_map(local, mesh=mesh, in_specs=in_specs, out_specs=out_specs, check_vma=False)
```

```python
import jax
import jax.numpy as jnp
from jax import lax
from jax.experimental import pallas as pl
from jax.experimental.pallas import tpu as pltpu
from jax.sharding import PartitionSpec as P

KS = 19
HALF = 9
SHIFT = 4
NPOLY = 6
REACH = HALF + SHIFT
SLOT = 8
CHUNK = 256
FINE = 24
VMEM_LIMIT = 24 * 1024 * 1024

highest = lax.Precision.HIGHEST
f32 = jnp.float32
bf16 = jnp.bfloat16


def up(value, step):
    return -(-value // step) * step


class Sizes:
    def __init__(self, height, width, strips):
        self.height, self.width = height, width
        self.rows = up(height + 2 * REACH, 8)
        self.lanes = up(width + 2 * REACH, 128)
        self.span = up(height + KS - 1, 2 * FINE)
        self.phases = self.span // FINE
        self.per = CHUNK // self.span
        self.lines = -(-KS // (self.per * self.phases))
        self.depth = self.lines * CHUNK
        self.sw_rows = 2 * height
        self.r_rows = self.lines * SLOT
        self.one_side = strips <= 2
        self.sent = height + 16 if self.one_side else self.rows
        self.main_at = self.sw_rows + self.r_rows
        self.halo_at = self.main_at + self.sent
        self.groups = self.sent // 8
        self.halo_rows = up(self.groups * 32, width) // width * 8
        self.total = self.halo_at + self.halo_rows

    def place(self, column):
        slot, phase = column // self.phases, column % self.phases
        return slot // self.per * CHUNK + (slot % self.per * self.phases + phase) * FINE


def iota(shape, axis):
    return lax.broadcasted_iota(jnp.int32, shape, axis)


def whole(value):
    return jnp.floor(value + 0.5)


def exponent_of(value):
    return jnp.floor(jnp.log2(value))


def join(mantissa, exponent):
    return (1.0 + mantissa * 2.0**-7) * jnp.exp2(exponent)


def part(value):
    exponent = jnp.floor(jnp.log2(value) + 0.003)
    return whole((value * jnp.exp2(-exponent) - 1.0) * 128.0), exponent


def encode_weight(weight):
    code = jnp.minimum(whole(weight * 65536.0), 32767.0)
    half = jnp.floor(code * 0.5)
    exponent = jnp.floor(half * 2.0**-7)
    value = join(half - exponent * 128.0, exponent - 63.0)
    return jnp.where(code > 2.0 * half, -value, value)


def decode_weight(value):
    mantissa, exponent = part(jnp.abs(value))
    code = (exponent + 63.0) * 256.0 + mantissa * 2.0
    return jnp.where(value < 0.0, code + 1.0, code) * 2.0**-16


def encode_science(science):
    size = jnp.abs(science)
    power = jnp.clip(exponent_of(jnp.maximum(size, 2.0**-30)), -24.0, 2.0)
    fine = power >= -12.0
    steps = jnp.where(fine, 2048.0, 128.0)
    code = jnp.clip(whole((size * jnp.exp2(-power) - 1.0) * steps), 0.0, steps - 1.0)
    high = jnp.floor(code * 0.0625)
    exponent = jnp.where(fine, power * 16.0 + (code - 16.0 * high) + 192.0, power + 264.0)
    value = join(jnp.where(fine, high, code), exponent - 125.0)
    value = jnp.where(size < 2.0**-24, 0.0, value)
    return jnp.where(science < 0.0, -value, value)


def decode_science(value):
    size = jnp.abs(value)
    mantissa, exponent = part(jnp.maximum(size, 2.0**-125))
    exponent = exponent + 125.0
    high = jnp.floor(exponent * 0.0625)
    fine = exponent < 240.0
    low = jnp.where(fine, exponent - 16.0 * high, 0.0)
    power = jnp.where(fine, high - 12.0, exponent - 264.0)
    size = jnp.where(size == 0.0, 0.0, (2048.0 + mantissa * 16.0 + low) * 2.0**-11 * jnp.exp2(power))
    return jnp.where(value < 0.0, -size, size)


def prepare(sz, n_epoch, tiles, count, nsel):
    lanes = count * SLOT
    per_owner = count // n_epoch
    width = sz.lines * CHUNK
    nbasis = 128

    def body(*refs):
        sources, refs = refs[:9], refs[9:]
        r_out, sw_out, own_out, sci_out, weight_out = refs[:5]
        var, mask, inter, offs, index, coef, basis, table, place, sems = refs[5:]
        targets = [own_out, sci_out, var, mask, inter, offs, index, coef, basis]
        copies = [
            pltpu.make_async_copy(source, target, sems.at[i])
            for i, (source, target) in enumerate(zip(sources, targets))
        ]
        for copy in reversed(copies):
            copy.start()
        me, _ = here("epoch")
        table[...] = jnp.zeros(table.shape, f32)
        col = iota((FINE, width), 0)
        base = iota((FINE, width), 1) - sz.place(col)
        base = jnp.where(col < KS, base, -1)
        for a in range(0, KS + 1, 2):
            pair = jnp.concatenate([(base == a).astype(f32), (base == a + 1).astype(f32)], axis=0)
            if a + 1 == KS:
                pair = jnp.where(iota(pair.shape, 0) < FINE, pair, 0.0)
            place[a * FINE : (a + 2) * FINE] = pair.astype(bf16)
        for copy in reversed(copies[4:]):
            copy.wait()
        for a in range(KS):
            table[a * FINE : a * FINE + KS, : basis.shape[2]] = basis[a]
        chosen = jnp.concatenate([index[e : e + 1, :] for e in range(count)], axis=1)
        onehot = (iota((nbasis, count * nsel), 0) == chosen).astype(f32)
        blocks = []
        for e in range(count):
            mine = jnp.concatenate([coef[:, e, :], jnp.zeros((SLOT - NPOLY, nsel), f32)], axis=0)
            wide = jnp.concatenate([mine] * count, axis=1)
            blocks.append(jnp.where(iota(wide.shape, 1) // nsel == e, wide, 0.0))
        combine = jnp.concatenate(blocks, axis=0)
        mixing = lax.dot_general(
            onehot, combine, (((1,), (1,)), ((), ())), precision=highest, preferred_element_type=f32
        )
        images = jnp.dot(table[...], mixing, precision=highest, preferred_element_type=f32)
        rows = lax.dot_general(
            images.astype(bf16), place[...], (((0,), (0,)), ((), ())), preferred_element_type=f32
        )
        for copy in reversed(copies[:4]):
            copy.wait()
        for e in range(count):
            weight_out[e] = mask[e].astype(f32) / var[e]
            science = jnp.where(mask[e] == 0, 0.0, sci_out[e])
            top = jnp.max(jnp.abs(science), axis=(0, 1), keepdims=True)
            scale = jnp.exp2(exponent_of(jnp.maximum(top, 2.0**-100)) - 2.0).astype(bf16).astype(f32)
            science = science / scale
            parts = [encode_science(science), encode_weight(weight_out[e])]
            sw_out[e] = jnp.concatenate(parts, axis=0).astype(bf16)
            mine = rows[e * SLOT : (e + 1) * SLOT]
            mine = jnp.concatenate(
                [mine[:, i * CHUNK : (i + 1) * CHUNK] for i in range(sz.lines)], axis=0
            )
            tile = inter[e // per_owner * count + me * per_owner + e % per_owner] - me * tiles
            tile = jnp.clip(tile, 0, tiles - 1).astype(f32)
            down, across = offs[0:1, e : e + 1].astype(f32), offs[1:2, e : e + 1].astype(f32)
            spare, spot = iota(mine.shape, 0) == NPOLY, iota(mine.shape, 1)
            for lane, value in enumerate((down, across, tile, scale)):
                mine = jnp.where(spare & (spot == lane), value, mine)
            r_out[e] = mine.astype(bf16)

    hbm, vmem = pl.BlockSpec(memory_space=pltpu.HBM), pl.BlockSpec(memory_space=pltpu.VMEM)
    shape = (count, sz.height, sz.width)

    def call(*sources):
        template, _, _, _, inter, offs, index, coef, basis = sources
        return pl.pallas_call(
            body,
            in_specs=[hbm] * 9,
            out_specs=(vmem,) * 5,
            out_shape=(
                jax.ShapeDtypeStruct((count, sz.r_rows, CHUNK), bf16),
                jax.ShapeDtypeStruct((count, sz.sw_rows, sz.width), bf16),
                jax.ShapeDtypeStruct(template.shape, bf16),
                jax.ShapeDtypeStruct(shape, f32),
                jax.ShapeDtypeStruct(shape, f32),
            ),
            scratch_shapes=[
                pltpu.VMEM(shape, f32),
                pltpu.VMEM(shape, jnp.int32),
                pltpu.SMEM(inter.shape, jnp.int32),
                pltpu.VMEM(offs.shape, jnp.int32),
                pltpu.VMEM(index.shape, jnp.int32),
                pltpu.VMEM(coef.shape, f32),
                pltpu.VMEM(basis.shape, f32),
                pltpu.VMEM(((KS + 1) * FINE, nbasis), f32),
                pltpu.VMEM(((KS + 1) * FINE, width), bf16),
                pltpu.SemaphoreType.DMA((9,)),
            ],
            compiler_params=pltpu.CompilerParams(vmem_limit_bytes=VMEM_LIMIT),
            cost_estimate=pl.CostEstimate(
                flops=1_000_000_000, bytes_accessed=6_000_000, transcendentals=0
            ),
            name="prepare",
        )(*[pltpu.with_memory_space_constraint(source, pltpu.HBM) for source in sources])

    return call


def here(axis):
    return lax.axis_index(axis), lax.axis_size(axis)


def partner(me, n, k, back):
    if n & (n - 1) == 0:
        return me ^ k
    return (me + (n - k if back else k)) % n


def pack(sz, n_epoch, tiles, count, peers):
    per_owner = count // n_epoch
    h, w = sz.height, sz.width

    def body(own, low, high, left, low_left, high_left, right, low_right, high_right, sw, r, *outs):
        slabs, sends = outs[0], outs[1:]
        me, _ = here("epoch")
        strip, strips = here("strip")
        band, bands = here("band")

        def column(middle, above, below, t, cut):
            above = jnp.where(strip > 0, above[t, h - 16 :, cut].astype(f32), 0.0)
            above = jnp.where(iota(above.shape, 0) >= 16 - REACH, above, 0.0)
            below = jnp.where(strip < strips - 1, below[t, :16, cut].astype(f32), 0.0)
            below = jnp.where(iota(below.shape, 0) < REACH, below, 0.0)
            parts = [middle[t, :, cut].astype(f32), below]
            gap = sz.rows - h - 32
            if gap:
                parts.append(jnp.zeros((gap, below.shape[1]), f32))
            return jnp.concatenate(parts + [above], axis=0)

        whole_slabs = []
        for t in range(tiles):
            parts = [column(own, low, high, t, slice(None))]
            before = column(left, low_left, high_left, t, slice(w - 128, w))
            after = column(right, low_right, high_right, t, slice(0, 128))
            lane = iota(before.shape, 1)
            before = jnp.where((lane >= 128 - REACH) & (band > 0), before, 0.0)
            after = jnp.where((lane < REACH) & (band < bands - 1), after, 0.0)
            if sz.lanes - w == 128:
                parts.append(before + after)
            else:
                gap = sz.lanes - w - 256
                parts += [after] + ([jnp.zeros((sz.rows, gap), f32)] if gap else []) + [before]
            slab = jnp.concatenate(parts, axis=1)
            slabs[t] = slab.astype(bf16)
            if sz.one_side:
                side = jnp.where(strip == 0, slab[h : h + 16], slab[sz.rows - 16 :])
                slab = jnp.concatenate([slab[:h], side], axis=0)
            whole_slabs.append(slab)
        for k, out in zip(peers, sends):
            q = partner(me, n_epoch, k, False)
            for c in range(per_owner):
                mine = q * per_owner + c
                lines = r[mine].astype(f32)
                covered = lines[NPOLY : NPOLY + 1, 2:3]
                slab = whole_slabs[0]
                for t in range(1, tiles):
                    pick = jnp.broadcast_to(covered, slab.shape) == t
                    slab = jnp.where(pick, whole_slabs[t], slab)
                halo = slab[:, sz.lanes - 128 :]
                if sz.lanes - w != 128:
                    halo = halo + slab[:, w : w + 128]
                bits = []
                for part in range(sz.halo_rows // 8 * (w // 128)):
                    piece = jnp.zeros((8, 128), f32)
                    for slot in range(4):
                        g = part * 4 + slot
                        if g < sz.groups:
                            piece = piece + pltpu.roll(halo[g * 8 : g * 8 + 8], slot * 32 + REACH, 1)
                    bits.append(piece)
                wide = w // 128
                bits = [
                    jnp.concatenate(bits[i * wide : (i + 1) * wide], axis=1)
                    for i in range(sz.halo_rows // 8)
                ]
                out[c, : sz.sw_rows] = sw[mine]
                out[c, sz.sw_rows : sz.main_at] = r[mine]
                out[c, sz.main_at :] = jnp.concatenate([slab[:, :w]] + bits, axis=0).astype(bf16)

    vmem = pl.BlockSpec(memory_space=pltpu.VMEM)
    return pl.pallas_call(
        body,
        in_specs=[vmem] * 11,
        out_shape=(jax.ShapeDtypeStruct((tiles, sz.rows, sz.lanes), bf16),)
        + tuple(jax.ShapeDtypeStruct((per_owner, sz.total, w), bf16) for _ in peers),
        compiler_params=pltpu.CompilerParams(vmem_limit_bytes=VMEM_LIMIT),
        cost_estimate=pl.CostEstimate(flops=1_000_000, bytes_accessed=1_000_000, transcendentals=0),
        name="pack",
    )


def models(sz, n_epoch, tiles, count, ks, first, last, carried):
    per_owner = count // n_epoch
    h, w = sz.height, sz.width
    total_models = (2 * len(ks) + first) * per_owner

    def body(sci, weight, r, slabs, *refs):
        refs = list(refs)
        ready = None if first else refs.pop(0)
        pays = [refs.pop(0) for _ in ks]
        before = [] if first else [refs.pop(0) for _ in range(2)]
        done = [refs.pop(0) for _ in carried]
        if last:
            resid_out, coadd_out = refs.pop(0), refs.pop(0)
        else:
            numer_out, denom_out = refs.pop(0), refs.pop(0)
            resid_outs = [refs.pop(0) for _ in range(len(ks) + first)]
            ready_out = refs.pop(0) if first else None
        rhs, lhs, *refs = refs
        me, _ = here("epoch")
        strip, strips = here("strip")
        band, bands = here("band")

        copies = []

        def send(source, target):
            copies.append(pltpu.make_async_copy(source, target, out_sems.at[len(copies)]))
            copies[-1].start()

        if last:
            fresh, sums, out_sems = refs
            for k, value in zip(carried, done):
                q = me if k == 0 else partner(me, n_epoch, k, True)
                send(value, resid_out.at[pl.ds(q * per_owner, per_owner)])

        jobs = []

        def job(kind, q, c, slab, lines):
            mine = q * per_owner + c
            own = lines if kind == "local" else r[mine].astype(f32)
            scalars = [lines[NPOLY, lane].astype(jnp.int32) for lane in range(2)]
            tile = None if kind == "sent" else own[NPOLY, 2].astype(jnp.int32)
            jobs.append((kind, mine, slab, lines, scalars, tile, own))

        if first:
            for c in range(per_owner):
                job("local", me, c, None, r[me * per_owner + c].astype(f32))
        for k, pay in zip(ks, pays):
            q = partner(me, n_epoch, k, True)
            for c in range(per_owner):
                got = pay[c].astype(f32)
                job("owned", q, c, got, got[sz.sw_rows : sz.main_at])
            for c in range(per_owner):
                job("sent", q, c, pay[c].astype(f32), r[q * per_owner + c].astype(f32))

        row = (strip * h + iota((h, 128), 0)).astype(f32)
        r_unit = (2.0 * row + 1.0) / (h * strips) - 1.0
        r_unit = jnp.concatenate([r_unit] * (sz.lanes // 128), axis=1)
        spot = iota((SLOT, CHUNK), 1)
        filled = (spot % sz.span < FINE) & (spot < sz.per * sz.span)
        c_units = []
        for i in range(sz.phases):
            col = (band * w + iota((8, sz.lanes), 1) - i).astype(f32)
            col = (2.0 * col + 1.0) / (w * bands) - 1.0
            c_units.append(jnp.concatenate([col] * (h // 8), axis=0))
        for slot in range(2):
            for line in range(sz.lines):
                at = line * CHUNK + sz.per * sz.span
                if at < (line + 1) * CHUNK:
                    rhs[slot, at : (line + 1) * CHUNK] = jnp.zeros(((line + 1) * CHUNK - at, sz.lanes), bf16)

        def windows(turn, slab, scalars):
            window = rhs.at[turn % 2]
            down, across = scalars
            slab = pltpu.roll(slab, lax.rem(sz.rows + HALF - down, sz.rows), 0)[: sz.span]
            slab = pltpu.roll(slab.astype(bf16), lax.rem(sz.lanes + HALF - across, sz.lanes), 1)
            for slot in range(sz.lines * sz.per):
                moved = pltpu.roll(slab, sz.lanes - slot * sz.phases, 1) if slot else slab
                at = slot // sz.per * CHUNK + slot % sz.per * sz.span
                window[at : at + sz.span] = moved

        def band_matrix(turn, lines):
            band_rows = lhs.at[turn % 2]
            for i in range(sz.phases * sz.lines):
                phase, line = divmod(i, sz.lines)
                part = lines[line * SLOT : (line + 1) * SLOT]
                if phase:
                    part = pltpu.roll(part, CHUNK - phase * FINE, 1)
                part = jnp.where(filled, part, 0.0)
                for p in range(NPOLY):
                    at = (phase * NPOLY + p) * h
                    band_rows[at : at + h, line * CHUNK : (line + 1) * CHUNK] = pltpu.roll(
                        jnp.broadcast_to(part[p : p + 1], (h, CHUNK)), 0, 1, stride=1, stride_axis=0
                    )

        def chunk_image(turn, i, matrix):
            at = i * NPOLY * h
            conv = jnp.dot(
                matrix[at : at + NPOLY * h].astype(bf16), rhs[turn % 2], preferred_element_type=f32
            )
            conv = [conv[p * h : (p + 1) * h] for p in range(NPOLY)]
            c_unit = c_units[i]
            return (
                conv[0]
                + r_unit * (conv[1] + r_unit * conv[3] + c_unit * conv[4])
                + c_unit * (conv[2] + c_unit * conv[5])
            )

        def sent_slab(got):
            main, halo = got[sz.main_at : sz.halo_at], got[sz.halo_at :]
            wide = w // 128
            bits = []
            for g in range(sz.groups):
                part, slot = g // 4, g % 4
                line, side = part // wide, part % wide
                piece = halo[line * 8 : line * 8 + 8, side * 128 : side * 128 + 128]
                bits.append(pltpu.roll(piece, (256 - slot * 32 - REACH) % 128, 1))
            halo = jnp.concatenate(bits, axis=0)
            lane = iota(halo.shape, 1)
            halo = jnp.where((lane < REACH) | (lane >= 128 - REACH), halo, 0.0)
            if sz.lanes - w != 128:
                gap = sz.lanes - w - 256
                pieces = [jnp.where(lane < 64, halo, 0.0)]
                if gap:
                    pieces.append(jnp.zeros((sz.sent, gap), f32))
                halo = jnp.concatenate(pieces + [jnp.where(lane < 64, 0.0, halo)], axis=1)
            slab = jnp.concatenate([main, halo], axis=1)
            if sz.one_side:
                side, none = slab[h:], jnp.zeros((sz.rows - h - 32, sz.lanes), f32)
                below, above = jnp.where(strip == 0, side, 0.0), jnp.where(strip == 0, 0.0, side)
                slab = [slab[:h], below, none, above] if none.size else [slab[:h], below, above]
                slab = jnp.concatenate(slab, axis=0)
            return slab

        numer = [before[0][t] if before else jnp.zeros((h, w), f32) for t in range(tiles)]
        denom = [before[1][t] if before else jnp.zeros((h, w), f32) for t in range(tiles)]
        kept = 0
        settled = max(turn for turn, job in enumerate(jobs) if job[0] != "sent")
        images = []
        for turn in range(0, len(jobs), 2):
            pair = list(enumerate(jobs))[turn : turn + 2]
            for at, (kind, mine, got, lines, scalars, tile, own) in pair:
                if kind != "sent":
                    band_matrix(at, lines)
            for at, (kind, mine, got, lines, scalars, tile, own) in pair:
                windows(at, sent_slab(got) if kind == "sent" else slabs[tile].astype(f32), scalars)
            parts = [None for _ in pair]
            for i in reversed(range(sz.phases)):
                for slot, (at, _) in enumerate(pair):
                    value = chunk_image(at, i, ready.at[pair[slot][1][1]] if pair[slot][1][0] == "sent" else lhs.at[at % 2])
                    value = pltpu.roll(value, sz.lanes - i, 1) if i else value
                    parts[slot] = value if parts[slot] is None else parts[slot] + value
            images += [part[:, :w] for part in parts]
        for turn, (kind, mine, got, lines, scalars, tile, own) in enumerate(jobs):
            image = images[turn]
            if kind == "owned":
                scale = jnp.broadcast_to(lines[NPOLY : NPOLY + 1, 3:4], (h, w))
                science, seen = decode_science(got[:h]) * scale, decode_weight(got[h : 2 * h])
            else:
                science, seen = sci[mine], weight[mine]
                if last:
                    fresh[kept] = science - image
                    send(fresh.at[kept], resid_out.at[mine])
                else:
                    resid_outs[kept // per_owner][kept % per_owner] = science - image
                kept += 1
            if kind != "sent":
                change = seen * (science - image)
                covered = jnp.broadcast_to(own[NPOLY : NPOLY + 1, 2:3], (h, w))
                for t in range(tiles):
                    numer[t] = numer[t] + jnp.where(covered == t, change, 0.0)
                    denom[t] = denom[t] + jnp.where(covered == t, seen, 0.0)
            if turn == settled:
                for t in range(tiles):
                    if last:
                        sums[t] = numer[t] / (denom[t] + 1.0)
                    else:
                        numer_out[t], denom_out[t] = numer[t], denom[t]
                if last:
                    send(sums, coadd_out)
        for copy in copies:
            copy.wait()
        if first:
            for e in range(count):
                band_matrix(0, r[e].astype(f32))
                ready_out[e] = lhs[0].astype(bf16)

    image = jax.ShapeDtypeStruct((per_owner, h, w), f32)
    sums = jax.ShapeDtypeStruct((tiles, h, w), f32)
    if last:
        out_shape = (jax.ShapeDtypeStruct((count, h, w), f32), sums)
    else:
        out_shape = (sums, sums) + (image,) * (len(ks) + first)
        if first:
            out_shape += (jax.ShapeDtypeStruct((count, sz.phases * NPOLY * h, sz.depth), bf16),)
    vmem, hbm = pl.BlockSpec(memory_space=pltpu.VMEM), pl.BlockSpec(memory_space=pltpu.HBM)
    scratch = [
        pltpu.VMEM((2, sz.depth, sz.lanes), bf16),
        pltpu.VMEM((2, sz.phases * NPOLY * h, sz.depth), f32),
    ]
    if last:
        new = len(ks) * per_owner
        scratch += [
            pltpu.VMEM((new, h, w), f32),
            pltpu.VMEM((tiles, h, w), f32),
            pltpu.SemaphoreType.DMA((len(carried) + new + 1,)),
        ]
    return pl.pallas_call(
        body,
        in_specs=[vmem] * (4 + len(ks) + (0 if first else 3) + len(carried)),
        out_specs=(hbm if last else vmem,) * len(out_shape),
        out_shape=out_shape,
        scratch_shapes=scratch,
        compiler_params=pltpu.CompilerParams(vmem_limit_bytes=VMEM_LIMIT),
        cost_estimate=pl.CostEstimate(
            flops=total_models * 1_000_000, bytes_accessed=100_000, transcendentals=0
        ),
        name="models",
    )


def surroundings(block):
    strips, bands = lax.axis_size("strip"), lax.axis_size("band")
    sent, found = {}, {}
    for down in (-1, 0, 1):
        for across in (-1, 0, 1):
            if down == 0 and across == 0:
                continue
            pairs = []
            for s in range(strips):
                for b in range(bands):
                    to_s = s ^ 1 if strips == 2 and down else s - down
                    to_b = b ^ 1 if bands == 2 and across else b - across
                    if 0 <= to_s < strips and 0 <= to_b < bands:
                        pairs.append((s * bands + b, to_s * bands + to_b))
            key = tuple(pairs)
            if key and key not in sent:
                sent[key] = lax.ppermute(block, ("strip", "band"), pairs)
            found[down, across] = key
    return {step: sent.get(key, block) for step, key in found.items()}


def local(
    template, science, variance, bad_mask, intersection, offsets, basis_index, coefficients, basis
):
    n_epoch = lax.axis_size("epoch")
    tiles = template.shape[0]
    count, height, width = science.shape
    sz = Sizes(height, width, lax.axis_size("strip"))
    around = surroundings(template)
    r, sw, own, sci, weight = prepare(sz, n_epoch, tiles, count, basis_index.shape[1])(
        template,
        science,
        variance,
        bad_mask,
        intersection,
        offsets.T,
        basis_index,
        coefficients.transpose(2, 0, 1),
        basis.transpose(1, 2, 0),
    )
    around[0, 0] = own
    peers = list(range(1, n_epoch))
    order = peers[-1:] + peers[:-1]
    slabs, *sends = pack(sz, n_epoch, tiles, count, peers)(
        *[around[down, across] for across in (0, -1, 1) for down in (0, -1, 1)], sw, r
    )
    pays = {}
    for k, send in reversed(list(zip(peers, sends))):
        pairs = [(i, partner(i, n_epoch, k, False)) for i in range(n_epoch)]
        pays[k] = lax.ppermute(send, "epoch", pairs)
    stages = [[]] + [[k] for k in order]
    sums, carried, ready = [], [], []
    for i, ks in enumerate(stages):
        first, last = i == 0, i == len(stages) - 1
        kept = [k for k, _ in carried] if last else []
        out = models(sz, n_epoch, tiles, count, ks, first, last, kept)(
            sci,
            weight,
            r,
            slabs,
            *ready,
            *[pays[k] for k in ks],
            *sums,
            *([value for _, value in carried] if last else []),
        )
        if last:
            return out
        sums = list(out[:2])
        if first:
            *out, matrices = out
            ready = [matrices]
        carried += list(zip(list(ks) + ([0] if first else []), out[2:]))


def solution(mesh):
    in_specs = (
        P(("groups", "epoch"), "strip", "band"),
        P(("groups", "epoch"), "strip", "band"),
        P(("groups", "epoch"), "strip", "band"),
        P(("groups", "epoch"), "strip", "band"),
        P("groups"),
        P(("groups", "epoch"), None),
        P(("groups", "epoch"), None),
        P(("groups", "epoch"), None, None),
        P(),
    )
    out_specs = (P(("groups", "epoch"), "strip", "band"), P(("groups", "epoch"), "strip", "band"))
    return jax.shard_map(local, mesh=mesh, in_specs=in_specs, out_specs=out_specs, check_vma=False)
```
